32 devices in a mesh: dp: 16 (over z, y, core), seq: 2 (over x).
Axes of the slice: x: 2, y: 2, z: 4, core: 2. Of those that a mesh axis runs over, the one named last changes fastest.
Arguments:
- inputs: bfloat16 [16, 2048, 512], P('dp', 'seq'), may hold values from -6 to 6
- cotangent: bfloat16 [16, 2048, 512], P('dp', 'seq'), may hold values from -6 to 6
- neighbours: int32 [16, 2048, 4], P('dp', 'seq'), may hold values from 0 to 2047, as said below
- empty_rows: int32 [16, 2048], P('dp', 'seq'), may hold values 0 or 1
- first_gain: float32 [512], replicated, may hold values from 0.25 to 1.75
- query_weight: bfloat16 [512, 512], replicated, may hold values from -0.25 to 0.25
- key_weight: bfloat16 [512, 512], replicated, may hold values from -0.25 to 0.25
- value_weight: bfloat16 [512, 512], replicated, may hold values from -0.25 to 0.25
- gate_weight: bfloat16 [512, 8], replicated, may hold values from -0.25 to 0.25
- output_weight: bfloat16 [512, 512], replicated, may hold values from -1.5 to 1.5
- second_gain: float32 [512], replicated, may hold values from 0.25 to 1.75
- hidden_weight: bfloat16 [512, 2048], replicated, may hold values from -0.25 to 0.25
- return_weight: bfloat16 [2048, 512], replicated, may hold values from -0.125 to 0.125
Outputs:
- outputs: bfloat16 [16, 2048, 512], P('dp', 'seq')
- input_grad: bfloat16 [16, 2048, 512], P('dp', 'seq')
- first_gain_grad: float32 [512], replicated
- query_weight_grad: float32 [512, 512], replicated
- key_weight_grad: float32 [512, 512], replicated
- value_weight_grad: float32 [512, 512], replicated
- gate_weight_grad: float32 [512, 8], replicated
- output_weight_grad: float32 [512, 512], replicated
- second_gain_grad: float32 [512], replicated
- hidden_weight_grad: float32 [512, 2048], replicated
- return_weight_grad: float32 [2048, 512], replicated
The draws below stay inside these ranges and needn't reach their ends.
Inputs may be any that keep to these rules, and one draw needn't show every extreme that they name: `neighbours`: positions within the token's own sequence; the sequence is cut into 2 shards of 1024 consecutive positions, and among the 4096 entries of the tokens of one shard, the positions of each shard are named exactly 2048 times.
All inputs are finite; a program needn't handle non-finite values. No bound on the sum of `empty_rows` on one device may be relied on, other than what follows from the above.
Results may differ from the reference program's by a relative error of at most 0.012.
Values may be sent and summed in bfloat16 or wider, within the bound.
No kernel may reach another device: no remote copies, remote signals or barrier semaphores. Data moves between devices by JAX's collectives and lax.ppermute only.
A program may use at most 320 MiB of HBM per device.

```python
import jax
import jax.numpy as jnp
from jax import lax

D = 512
H = 8
HD = 64
FF = 2048
SPAN = 512
NEAR = 4
LENGTH = 2048
SHARD = 1024
SEQS_ALL = 16
N_SEQ = 2


def draw_neighbours(key, part):
    key = jax.random.fold_in(key, 7)
    owner_key, offset_key = jax.random.split(key)
    slots = SHARD * NEAR
    balanced = jnp.arange(slots, dtype=jnp.int32) % N_SEQ
    tiled = jnp.broadcast_to(balanced, (SEQS_ALL * N_SEQ, slots))
    owners = jax.random.permutation(owner_key, tiled, axis=1, independent=True)
    offsets = jax.random.randint(offset_key, (SEQS_ALL * N_SEQ, slots), 0, SHARD, dtype=jnp.int32)
    positions = owners * SHARD + offsets
    return positions.reshape(SEQS_ALL, LENGTH, NEAR).astype(jnp.int32)


def place_ends(drawn, rng, low, high):
    shape = drawn.shape
    place = [jax.random.randint(jax.random.fold_in(rng, axis), (), 0, shape[axis]) for axis in range(len(shape))]
    drawn = drawn.at[tuple(place)].set(low)
    longest = shape.index(max(shape))
    place[longest] = (place[longest] + 1) % shape[longest]
    return drawn.at[tuple(place)].set(high)


def block_levels(rng, shape, cuts, smallest, high):
    def one(axis_at, blocks):
        draws = jax.random.uniform(jax.random.fold_in(jax.random.fold_in(rng, 6), axis_at), (blocks,), jnp.float32, smallest / len(cuts), high / len(cuts))
        return jnp.repeat(jnp.exp(draws), shape[axis_at] // blocks).reshape((-1,) + (1,) * (len(shape) - axis_at - 1))

    loudness = one(*cuts[0])
    for cut in cuts[1:]:
        loudness = loudness * one(*cut)
    return loudness


def noise(own_key, shape, spread, reach, shards=(), kind=jnp.bfloat16):
    entries = jax.random.normal(own_key, shape, jnp.float32) * spread
    if len(shards) > 0:
        entries = block_levels(own_key, shape, shards, -0.22, 0.18) * entries
    return jnp.clip(entries, min=-reach, max=reach).astype(kind)


def setup_inputs(seed: int = 0) -> dict:
    seeds = jax.random.split(jax.random.key(seed), 14)
    return {
        "inputs": noise(seeds[0], (SEQS_ALL, LENGTH, D), 1.0, 6.0, ((0, 16), (1, 2))),
        "cotangent": noise(seeds[1], (SEQS_ALL, LENGTH, D), 1.0, 6.0, ((0, 16), (1, 2))),
        "neighbours": draw_neighbours(jax.random.fold_in(seeds[13], 71), 0),
        "empty_rows": place_ends((jax.random.randint(seeds[3], (SEQS_ALL, LENGTH), 0, 4) < 1).astype(jnp.int32), jax.random.fold_in(seeds[3], 1), 0, 1),
        "first_gain": jnp.clip(1.0 + 0.15 * jax.random.normal(seeds[4], (D,), jnp.float32), 0.25, 1.75),
        "query_weight": noise(seeds[5], (D, D), D ** -0.5, 0.25),
        "key_weight": noise(seeds[6], (D, D), D ** -0.5, 0.25),
        "value_weight": noise(seeds[7], (D, D), D ** -0.5, 0.25),
        "gate_weight": noise(seeds[8], (D, H), D ** -0.5, 0.25),
        "output_weight": noise(seeds[9], (D, D), (D // 32) ** -0.5, 1.5),
        "second_gain": jnp.clip(1.0 + 0.15 * jax.random.normal(seeds[10], (D,), jnp.float32), 0.25, 1.75),
        "hidden_weight": noise(seeds[11], (D, FF), D ** -0.5, 0.25),
        "return_weight": noise(seeds[12], (FF, D), FF ** -0.5, 0.125),
    }


@jax.custom_vjp
def low(v):
    return lax.optimization_barrier(v.astype(jnp.bfloat16)).astype(jnp.float32)

@jax.custom_vjp
def low_back(v):
    return v

def low_keep(v):
    return (low(v), None)

def low_pass(kept, grad):
    return (grad,)

def back_keep(v):
    return (v, None)

def back_low(kept, grad):
    return (low(grad),)
low.defvjp(low_keep, low_pass)
low_back.defvjp(back_keep, back_low)
NEG = -1e+30
EPS = 1e-06

def rms_gain(values, gain):
    return values * lax.rsqrt(lax.optimization_barrier(jnp.mean(values * values, axis=-1, keepdims=True)) + EPS) * gain

def matmul(left, right):
    return jnp.dot(left, right, precision=lax.Precision.HIGHEST)

def local_attention(query, keys, values):
    length = query.shape[0]
    block = 512 if length % 512 == 0 else length
    scale = HD ** (-0.5)
    keys_pad = jnp.pad(keys, ((SPAN, 0), (0, 0)))
    values_pad = jnp.pad(values, ((SPAN, 0), (0, 0)))

    def one_block(start):
        query_b = lax.dynamic_slice_in_dim(query, start, block, 0).reshape(block, H, HD)
        keys_b = lax.dynamic_slice_in_dim(keys_pad, start, block + SPAN, 0).reshape(block + SPAN, H, HD)
        values_b = lax.dynamic_slice_in_dim(values_pad, start, block + SPAN, 0).reshape(block + SPAN, H, HD)
        scores = jnp.einsum('ihd,jhd->hij', query_b, keys_b, precision=lax.Precision.HIGHEST) * scale
        scores = low_back(scores)
        query_pos = lax.broadcasted_iota(jnp.int32, (block, block + SPAN), 0)
        key_pos = lax.broadcasted_iota(jnp.int32, (block, block + SPAN), 1)
        allowed = (key_pos > query_pos) & (key_pos <= query_pos + SPAN) & (key_pos >= SPAN - start)
        scores = jnp.where(allowed[None], scores, NEG)
        probs = jax.nn.softmax(scores, axis=-1)
        result = jnp.einsum('hij,jhd->ihd', low(probs), values_b, precision=lax.Precision.HIGHEST)
        return low_back(result.reshape(block, D))
    starts = jnp.arange(length // block, dtype=jnp.int32) * block
    return lax.map(jax.checkpoint(one_block), starts).reshape(length, D)

def layer(inputs, first_gain, query_weight, key_weight, value_weight, gate_weight, output_weight, second_gain, hidden_weight, return_weight, neighbours, open_rows):
    length = inputs.shape[0]
    scale = HD ** (-0.5)
    normed = low(rms_gain(inputs, first_gain))
    query = low_back(low(matmul(normed, query_weight)))
    keys = low_back(low(matmul(normed, key_weight)))
    values = low_back(low(matmul(normed, value_weight)))
    gate_logit = low_back(matmul(normed, gate_weight))
    local_out = local_attention(query, keys, values).reshape(length, H, HD)
    near_keys = keys[neighbours].reshape(length, NEAR, H, HD)
    near_values = values[neighbours].reshape(length, NEAR, H, HD)
    query_heads = query.reshape(length, H, HD)
    match = lax.optimization_barrier(jnp.sum(query_heads[:, None] * near_keys, axis=-1)) * scale
    match_w = jax.nn.softmax(match, axis=1)
    recalled = lax.optimization_barrier(jnp.sum(match_w[..., None] * near_values, axis=1))
    gate = jax.nn.sigmoid(gate_logit)
    mix = (1.0 - gate) * open_rows[:, None]
    blended = local_out + mix[..., None] * (recalled - local_out)
    attended = low_back(matmul(low(blended.reshape(length, D)), output_weight))
    resid = inputs + attended
    normed2 = low(rms_gain(resid, second_gain))
    hidden_pre = low_back(matmul(normed2, hidden_weight))
    active = low(jax.nn.gelu(hidden_pre))
    return resid + matmul(active, return_weight)

def reference(inputs, cotangent, neighbours, empty_rows, first_gain, query_weight, key_weight, value_weight, gate_weight, output_weight, second_gain, hidden_weight, return_weight):
    params = (first_gain.astype(jnp.float32), query_weight.astype(jnp.float32), key_weight.astype(jnp.float32), value_weight.astype(jnp.float32), gate_weight.astype(jnp.float32), output_weight.astype(jnp.float32), second_gain.astype(jnp.float32), hidden_weight.astype(jnp.float32), return_weight.astype(jnp.float32))

    def one_sequence(totals, item):
        seq_in, seq_cot, seq_near, seq_empty = item
        open_rows = 1.0 - seq_empty.astype(jnp.float32)

        def forward(values, *weights):
            return layer(values, *weights, seq_near, open_rows)
        result, pull = jax.vjp(forward, seq_in.astype(jnp.float32), *params)
        grads = pull(seq_cot.astype(jnp.float32))
        totals = tuple((total + grad for total, grad in zip(totals, grads[1:])))
        return (totals, (result.astype(jnp.bfloat16), grads[0].astype(jnp.bfloat16)))
    zeros = tuple((jnp.zeros_like(param) for param in params))
    totals, (outputs, input_grad) = lax.scan(one_sequence, zeros, (inputs, cotangent, neighbours, empty_rows))
    return (outputs, input_grad, totals[0], totals[1], totals[2], totals[3], totals[4], totals[5], totals[6], totals[7], totals[8])
```

```python
import functools

import jax
import jax.numpy as jnp
from jax import lax
from jax.experimental import pallas as pl
from jax.experimental.pallas import tpu as pltpu
from jax.sharding import PartitionSpec as P

H = 8
HD = 64
LANES = 2 * HD
WIDE = H * LANES
SPAN = 512
NEAR = 4
SCALE = HD ** (-0.5)
NEG = -1e30
EPS = 1e-06
VMEM_LIMIT = 56 * 1024 * 1024

F32 = jnp.float32
BF16 = jnp.bfloat16


def rms_gain(values, gain):
    return values * lax.rsqrt(jnp.mean(values * values, axis=-1, keepdims=True) + EPS) * gain


def dot(left, right):
    return jnp.dot(left, right, preferred_element_type=F32)


def dot_back(left, right):
    return lax.dot_general(left, right, (((1,), (1,)), ((), ())), preferred_element_type=F32)


def rows_dot(left, right):
    return lax.dot_general(left, right, (((0,), (0,)), ((), ())), preferred_element_type=F32)


def block_rows(rows):
    return 256 if rows % 256 == 0 else rows


def allowed_keys(block, first, base):
    query_pos = lax.broadcasted_iota(jnp.int32, (block, block + SPAN), 0)
    key_pos = lax.broadcasted_iota(jnp.int32, (block, block + SPAN), 1)
    inside = (key_pos > query_pos) & (key_pos <= query_pos + SPAN)
    return inside & (key_pos >= SPAN - base - first)


def local_kernel(base_ref, query_ref, memory_ref, out_ref, total_ref):
    rows = query_ref.shape[0]
    block = block_rows(rows)
    base = base_ref[0]
    for first in range(0, rows, block):
        here = slice(first, first + block)
        query = query_ref[here, :]
        window = memory_ref[first : first + block + SPAN, :]
        scores = jnp.where(allowed_keys(block, first, base), dot_back(query, window), NEG)
        top = jnp.max(scores, axis=1, keepdims=True)
        expo = jnp.exp(scores - top)
        total = jnp.sum(expo, axis=1, keepdims=True)
        out_ref[here, :] = dot(expo.astype(BF16), window) / total
        total_ref[here, :] = jnp.broadcast_to(top + jnp.log(total), (block, LANES))


def local_attention(base, query, window):
    rows = query.shape[0]
    head = lambda n: pl.BlockSpec((n, LANES), lambda h: (0, h))
    return pl.pallas_call(
        local_kernel,
        grid=(H,),
        in_specs=[pl.BlockSpec(memory_space=pltpu.SMEM), head(rows), head(SPAN + rows)],
        out_specs=[head(rows), head(rows)],
        out_shape=[jax.ShapeDtypeStruct((rows, WIDE), F32)] * 2,
        compiler_params=pltpu.CompilerParams(vmem_limit_bytes=VMEM_LIMIT),
        name="local_attention",
    )(base, query, window)


def local_back_kernel(
    base_ref, query_ref, memory_ref, grad_ref, total_ref, inner_ref, partial_ref, far_ref, query_grad_ref, memory_grad_ref, sums_ref
):
    rows = query_ref.shape[0]
    length = far_ref.shape[0]
    block = block_rows(rows)
    base = base_ref[0]
    start = length - rows - SPAN
    left = lax.broadcasted_iota(jnp.int32, (block, LANES), 1) < HD
    sums_ref[...] = far_ref[...].astype(F32)
    for first in range(0, rows, block):
        here = slice(first, first + block)
        query = query_ref[here, :]
        grad = grad_ref[here, :]
        window = memory_ref[first : first + block + SPAN, :]
        scores = jnp.where(allowed_keys(block, first, base), dot_back(query, window), NEG)
        probs = jnp.exp(scores - total_ref[here, 0:1])
        prob_grad = dot_back(grad, window)
        score_grad = (probs * (prob_grad - inner_ref[here, HD : HD + 1])).astype(BF16)
        query_grad = dot(score_grad, window) * SCALE
        query_grad_ref[here, :] = (partial_ref[here, :] + jnp.where(left, query_grad, 0.0)).astype(BF16)
        there = slice(start + first, start + first + block + SPAN)
        sums_ref[there, :] += rows_dot(score_grad, query) + rows_dot(probs.astype(BF16), grad)
    memory_grad_ref[...] = sums_ref[...].astype(BF16)


def local_attention_back(base, query, window, grad, total, inner, partial, far):
    rows = query.shape[0]
    length = far.shape[0]
    head = lambda n: pl.BlockSpec((n, LANES), lambda h: (0, h))
    return pl.pallas_call(
        local_back_kernel,
        grid=(H,),
        in_specs=[
            pl.BlockSpec(memory_space=pltpu.SMEM),
            head(rows),
            head(SPAN + rows),
            head(rows),
            head(rows),
            head(rows),
            head(rows),
            head(length),
        ],
        out_specs=[head(rows), head(length)],
        out_shape=[
            jax.ShapeDtypeStruct((rows, WIDE), BF16),
            jax.ShapeDtypeStruct((length, WIDE), BF16),
        ],
        scratch_shapes=[pltpu.VMEM((length, LANES), F32)],
        compiler_params=pltpu.CompilerParams(vmem_limit_bytes=VMEM_LIMIT),
        name="local_attention_back",
    )(base, query, window, grad, total, inner, partial, far)


def to_token_rows(tile_ref, wide, count):
    for h in range(H):
        tile_ref[pl.ds(h, count, stride=H), :] = wide[:, h * LANES : (h + 1) * LANES].astype(F32)


def head_of(tile_ref, h, count):
    return tile_ref[pl.ds(h, count, stride=H), :]


def lane_sums(products):
    ones = jnp.ones((LANES, LANES), BF16)
    return dot(products.astype(BF16), ones)


def retrieve_kernel(
    index_ref, memory_ref, query_ref, gate_ref, local_ref, open_ref, near_ref, weight_ref, recalled_ref, blended_ref, table, query_rows, near_rows, out_rows
):
    step = pl.program_id(0)
    count = query_ref.shape[0]
    length = memory_ref.shape[0]

    @pl.when(step == 0)
    def build():
        for at in range(0, length, 256):
            for h in range(H):
                table[pl.ds(at * H + h, 256, stride=H), :] = memory_ref[
                    at : at + 256, h * LANES : (h + 1) * LANES
                ].astype(F32)

    to_token_rows(query_rows, query_ref[...], count)
    unroll = 8

    def gather(group, carry):
        for k in range(unroll):
            t = group * unroll + k
            for j in range(NEAR):
                row = index_ref[(step * count + t) * NEAR + j]
                near_rows[j, pl.ds(pl.multiple_of(t * H, H), H), :] = table[pl.ds(pl.multiple_of(row * H, H), H), :]
        return carry

    lax.fori_loop(0, count // unroll, gather, 0)
    query = query_rows[...]
    match = [lane_sums(near_rows[j] * query) for j in range(NEAR)]
    top = functools.reduce(jnp.maximum, match)
    expo = [jnp.exp(m - top) for m in match]
    scale = 1.0 / sum(expo[1:], expo[0])
    recalled = None
    for j in range(NEAR):
        weight = expo[j] * scale
        near = near_rows[j]
        weight_ref[j] = weight.astype(BF16)
        near_ref[j] = near.astype(BF16)
        recalled = weight * near if recalled is None else recalled + weight * near
    out_rows[...] = recalled
    open_rows = open_ref[...]
    right = lax.broadcasted_iota(jnp.int32, (count, LANES), 1) >= HD
    for h in range(H):
        lanes = slice(h * LANES, (h + 1) * LANES)
        recalled_h = head_of(out_rows, h, count)
        local = local_ref[:, lanes]
        mix = (1.0 - jax.nn.sigmoid(gate_ref[:, lanes])) * open_rows
        recalled_ref[:, lanes] = recalled_h
        blended = local + mix * (recalled_h - local)
        blended_ref[:, lanes] = jnp.where(right, blended, 0.0).astype(BF16)


def retrieve(index, memory, query, gate, local, open_rows):
    rows = query.shape[0]
    length = memory.shape[0]
    count = min(128, rows)
    wide = pl.BlockSpec((count, WIDE), lambda c: (c, 0))
    near = pl.BlockSpec((NEAR, count * H, LANES), lambda c: (0, c, 0))
    return pl.pallas_call(
        retrieve_kernel,
        grid=(rows // count,),
        in_specs=[
            pl.BlockSpec(memory_space=pltpu.SMEM),
            pl.BlockSpec((length, WIDE), lambda c: (0, 0)),
            wide,
            wide,
            wide,
            pl.BlockSpec((count, 1), lambda c: (c, 0)),
        ],
        out_specs=[near, near, wide, wide],
        out_shape=[
            jax.ShapeDtypeStruct((NEAR, rows * H, LANES), BF16),
            jax.ShapeDtypeStruct((NEAR, rows * H, LANES), BF16),
            jax.ShapeDtypeStruct((rows, WIDE), F32),
            jax.ShapeDtypeStruct((rows, WIDE), BF16),
        ],
        scratch_shapes=[
            pltpu.VMEM((length * H, LANES), F32),
            pltpu.VMEM((count * H, LANES), F32),
            pltpu.VMEM((NEAR, count * H, LANES), F32),
            pltpu.VMEM((count * H, LANES), F32),
        ],
        compiler_params=pltpu.CompilerParams(vmem_limit_bytes=VMEM_LIMIT),
        name="retrieve",
    )(index, memory, query, gate, local, open_rows)


def retrieve_back_kernel(
    index_ref, grad_ref, query_ref, gate_ref, local_ref, recalled_ref, open_ref, near_ref, weight_ref,
    local_grad_ref, inner_ref, partial_ref, far_ref,
    sums_even, sums_odd, query_rows, grad_rows, out_rows, terms,
):
    step = pl.program_id(0)
    count = query_ref.shape[0]
    length = far_ref.shape[0]

    @pl.when(step == 0)
    def clear():
        sums_even[...] = jnp.zeros_like(sums_even)
        sums_odd[...] = jnp.zeros_like(sums_odd)

    to_token_rows(query_rows, query_ref[...], count)
    open_rows = open_ref[...]
    gates = []
    for h in range(H):
        lanes = slice(h * LANES, (h + 1) * LANES)
        grad = grad_ref[:, lanes]
        local = local_ref[:, lanes]
        gate = jax.nn.sigmoid(gate_ref[:, lanes])
        mix = (1.0 - gate) * open_rows
        mix_grad = lane_sums(grad * (recalled_ref[:, lanes] - local))
        inner = lane_sums(grad * local)
        local_grad_ref[:, lanes] = ((1.0 - mix) * grad).astype(BF16)
        inner_ref[:, lanes] = (1.0 - mix) * inner
        gates.append(-mix_grad * open_rows * gate * (1.0 - gate))
        grad_rows[pl.ds(h, count, stride=H), :] = mix * grad
    grad = grad_rows[...]
    left_rows = lax.broadcasted_iota(jnp.int32, (count * H, LANES), 1) < HD
    grad = jnp.where(left_rows, 0.0, grad)
    source = query_rows[...] + grad
    weight_grad = [lane_sums(near_ref[j].astype(F32) * grad) for j in range(NEAR)]
    inner = None
    for j in range(NEAR):
        term = weight_ref[j].astype(F32) * weight_grad[j]
        inner = term if inner is None else inner + term
    query_grad = None
    for j in range(NEAR):
        weight = weight_ref[j].astype(F32)
        match_grad = weight * (weight_grad[j] - inner)
        term = match_grad * near_ref[j].astype(F32)
        query_grad = term if query_grad is None else query_grad + term
        terms[j] = jnp.where(left_rows, match_grad, weight) * source
    out_rows[...] = query_grad * SCALE
    left = lax.broadcasted_iota(jnp.int32, (count, LANES), 1) < HD
    for h in range(H):
        lanes = slice(h * LANES, (h + 1) * LANES)
        partial_ref[:, lanes] = jnp.where(left, head_of(out_rows, h, count), gates[h])
    unroll = 8

    def scatter(group, carry):
        for k in range(unroll):
            t = group * unroll + k
            for j in range(NEAR):
                row = index_ref[(step * count + t) * NEAR + j]
                sums = (sums_even, sums_odd)[j % 2]
                there = pl.ds(pl.multiple_of(row * H, H), H)
                sums[there, :] = sums[there, :] + terms[j, pl.ds(pl.multiple_of(t * H, H), H), :]
        return carry

    lax.fori_loop(0, count // unroll, scatter, 0)

    @pl.when(step == pl.num_programs(0) - 1)
    def finish():
        for at in range(0, length, 256):
            for h in range(H):
                there = pl.ds(at * H + h, 256, stride=H)
                far_ref[at : at + 256, h * LANES : (h + 1) * LANES] = (
                    sums_even[there, :] + sums_odd[there, :]
                ).astype(BF16)


def retrieve_back(index, grad, query, gate, local, recalled, open_rows, near, weight, length):
    rows = query.shape[0]
    count = min(128, rows)
    wide = pl.BlockSpec((count, WIDE), lambda c: (c, 0))
    tall = pl.BlockSpec((NEAR, count * H, LANES), lambda c: (0, c, 0))
    return pl.pallas_call(
        retrieve_back_kernel,
        grid=(rows // count,),
        in_specs=[
            pl.BlockSpec(memory_space=pltpu.SMEM),
            wide,
            wide,
            wide,
            wide,
            wide,
            pl.BlockSpec((count, 1), lambda c: (c, 0)),
            tall,
            tall,
        ],
        out_specs=[wide, wide, wide, pl.BlockSpec((length, WIDE), lambda c: (0, 0))],
        out_shape=[
            jax.ShapeDtypeStruct((rows, WIDE), BF16),
            jax.ShapeDtypeStruct((rows, WIDE), F32),
            jax.ShapeDtypeStruct((rows, WIDE), F32),
            jax.ShapeDtypeStruct((length, WIDE), BF16),
        ],
        scratch_shapes=[
            pltpu.VMEM((length * H, LANES), F32),
            pltpu.VMEM((length * H, LANES), F32),
            pltpu.VMEM((count * H, LANES), F32),
            pltpu.VMEM((count * H, LANES), F32),
            pltpu.VMEM((count * H, LANES), F32),
            pltpu.VMEM((NEAR, count * H, LANES), F32),
        ],
        compiler_params=pltpu.CompilerParams(vmem_limit_bytes=VMEM_LIMIT),
        name="retrieve_back",
    )(index, grad, query, gate, local, recalled, open_rows, near, weight)


def turned(block, shift):
    size = lax.axis_size("seq")
    return lax.ppermute(block, "seq", [((i + shift) % size, i) for i in range(size)])


def level_groups():
    dp = [("dp", b) for b in range(lax.axis_size("dp").bit_length() - 1)]
    seq = [("seq", b) for b in range(lax.axis_size("seq").bit_length() - 1)]
    rest = dp[2:] + seq[1:]
    return [dp[:1], seq[:1] + dp[1:2]] + [rest[i : i + 2] for i in range(0, len(rest), 2)]


def own_place(group):
    place = 0
    for k, (axis, bit) in enumerate(group):
        place = place + (((lax.axis_index(axis) >> bit) & 1) << k)
    return place


def swapped(block, group, distance):
    flips = {"dp": 0, "seq": 0}
    for k, (axis, bit) in enumerate(group):
        if (distance >> k) & 1:
            flips[axis] |= 1 << bit
    n_seq = lax.axis_size("seq")
    both = range(lax.axis_size("dp") * n_seq)
    if not flips["seq"]:
        return lax.ppermute(block, "dp", [(i, i ^ flips["dp"]) for i in range(lax.axis_size("dp"))])
    if not flips["dp"]:
        return lax.ppermute(block, "seq", [(i, i ^ flips["seq"]) for i in range(n_seq)])
    route = [(i, (i // n_seq ^ flips["dp"]) * n_seq + (i % n_seq ^ flips["seq"])) for i in both]
    return lax.ppermute(block, ("dp", "seq"), route)


def summed_everywhere(block):
    groups = level_groups()
    for group in groups:
        members = 2 ** len(group)
        place = own_place(group)
        count = block.shape[0] // members
        part = lambda d: lax.dynamic_slice_in_dim(block, (place ^ d) * count, count, 0)
        arrived = [swapped(part(d), group, d) for d in range(1, members)]
        total = part(0).astype(F32)
        for piece in arrived:
            total = total + piece.astype(F32)
        block = total.astype(BF16)
    for group in groups[::-1]:
        members = 2 ** len(group)
        place = own_place(group)
        pieces = jnp.stack([block] + [swapped(block, group, d) for d in range(1, members)])
        for k in range(len(group)):
            halves = pieces.reshape((-1, 2, 2**k) + block.shape)
            pieces = jnp.where((place >> k) & 1, halves[:, ::-1], halves).reshape(pieces.shape)
        block = pieces.reshape((-1,) + block.shape[1:])
    return block


def body(
    inputs,
    cotangent,
    neighbours,
    empty_rows,
    first_gain,
    query_weight,
    key_weight,
    value_weight,
    gate_weight,
    output_weight,
    second_gain,
    hidden_weight,
    return_weight,
):
    rows, width = inputs.shape[1:]
    hidden = hidden_weight.shape[1]
    n_seq = lax.axis_size("seq")
    length = rows * n_seq
    base = lax.axis_index("seq") * rows
    base_ref = jnp.reshape(base, (1,)).astype(jnp.int32)
    inputs = inputs.reshape(rows, width)
    cotangent = cotangent.reshape(rows, width)
    others = [turned(inputs, shift) for shift in range(1, n_seq)]

    heads = lambda w: w.reshape(width, H, HD)
    gate_column = gate_weight.reshape(width, H, 1)
    ask_weight = jnp.concatenate(
        [heads(query_weight), jnp.broadcast_to(gate_column, (width, H, HD))], axis=2
    ).reshape(width, WIDE)
    ask_weight_back = jnp.concatenate(
        [heads(query_weight), jnp.pad(gate_column, ((0, 0), (0, 0), (0, HD - 1)))], axis=2
    ).reshape(width, WIDE)
    memory_weight = jnp.concatenate([heads(key_weight), heads(value_weight)], axis=2).reshape(width, WIDE)
    blend_weight = jnp.pad(output_weight.reshape(H, HD, width), ((0, 0), (HD, 0), (0, 0))).reshape(WIDE, width)

    inputs_f = inputs.astype(F32)
    normed = rms_gain(inputs_f, first_gain).astype(BF16)
    ask = dot(normed, ask_weight)
    left = (lax.broadcasted_iota(jnp.int32, (1, WIDE), 1) % LANES) < HD
    query = jnp.where(left, ask * SCALE, 0.0).astype(BF16)
    others_normed = rms_gain(jnp.concatenate(others, axis=0).astype(F32), first_gain).astype(BF16)
    all_normed = jnp.concatenate([others_normed, normed], axis=0)
    memory = dot(all_normed, memory_weight).astype(BF16)
    window = memory[length - rows - SPAN :]

    local_out, log_total = local_attention(base_ref, query, window)
    index = (neighbours.reshape(rows * NEAR) + (length - rows - base)) % length
    open_rows = (1 - empty_rows.reshape(rows, 1)).astype(F32)
    near, weight, recalled, blended = retrieve(index, memory, query, ask, local_out, open_rows)

    resid = inputs_f + dot(blended, blend_weight)
    normed2 = rms_gain(resid, second_gain).astype(BF16)
    hidden_pre = dot(normed2, hidden_weight)
    active = jax.nn.gelu(hidden_pre).astype(BF16)
    outputs = (resid + dot(active, return_weight)).astype(BF16)
    return_weight_grad = rows_dot(active, cotangent)
    active_grad = dot_back(cotangent, return_weight)
    hidden_grad = jax.vjp(jax.nn.gelu, hidden_pre)[1](active_grad)[0].astype(BF16)
    hidden_weight_grad = rows_dot(normed2, hidden_grad)
    normed2_grad = dot_back(hidden_grad, hidden_weight)
    resid_part, second_gain_grad = jax.vjp(rms_gain, resid, second_gain)[1](normed2_grad)
    resid_grad = cotangent.astype(F32) + resid_part
    resid_grad_b = resid_grad.astype(BF16)
    blend_weight_grad = rows_dot(blended, resid_grad_b)
    output_weight_grad = blend_weight_grad.reshape(H, 2, HD, width)[:, 1].reshape(width, width)
    blended_grad = dot_back(resid_grad_b, blend_weight)

    columns = hidden // width
    early = [return_weight_grad]
    early += [hidden_weight_grad[:, c * width : (c + 1) * width] for c in range(columns)]
    early += [output_weight_grad]
    early_sum = summed_everywhere(jnp.concatenate([g.astype(BF16) for g in early], axis=0))

    local_grad, inner, partial, far = retrieve_back(
        index, blended_grad, query, ask, local_out, recalled, open_rows, near, weight, length
    )
    ask_grad, memory_grad = local_attention_back(
        base_ref, query, window, local_grad, log_total, inner, partial, far
    )

    others_grad = dot_back(memory_grad[: length - rows], memory_weight).astype(BF16)
    normed_grad = dot_back(ask_grad, ask_weight_back) + dot_back(memory_grad[length - rows :], memory_weight)
    for shift in range(1, n_seq):
        piece = others_grad[(shift - 1) * rows : shift * rows]
        normed_grad = normed_grad + turned(piece, n_seq - shift).astype(F32)
    input_part, first_gain_grad = jax.vjp(rms_gain, inputs_f, first_gain)[1](normed_grad)
    input_grad = (resid_grad + input_part).astype(BF16)

    ask_weight_grad = rows_dot(normed, ask_grad).reshape(width, H, 2, HD)
    memory_weight_grad = rows_dot(all_normed, memory_grad).reshape(width, H, 2, HD)
    gains = jnp.zeros((32, width), F32)
    gate_weight_grad = ask_weight_grad[:, :, 1, 0].reshape(H, width)
    gains = jnp.concatenate([first_gain_grad[None], second_gain_grad[None], jnp.zeros((6, width), F32), gate_weight_grad], axis=0)
    gains = jnp.pad(gains, ((0, 240), (0, 0)))
    flat = lambda g: g.reshape(width, width)
    late = [flat(ask_weight_grad[:, :, 0]), flat(memory_weight_grad[:, :, 0]), flat(memory_weight_grad[:, :, 1]), gains]
    late_sum = summed_everywhere(jnp.concatenate([g.astype(BF16) for g in late], axis=0))

    early_sum = early_sum.astype(F32)
    late_sum = late_sum.astype(F32)
    at = hidden
    hidden_sum = jnp.concatenate([early_sum[at + c * width : at + (c + 1) * width] for c in range(columns)], axis=1)
    at = 3 * width
    return (
        outputs.reshape(1, rows, width),
        input_grad.reshape(1, rows, width),
        late_sum[at],
        late_sum[:width],
        late_sum[width : 2 * width],
        late_sum[2 * width : 3 * width],
        late_sum[at + 8 : at + 8 + H].reshape(width, H),
        early_sum[2 * hidden :],
        late_sum[at + 1],
        hidden_sum,
        early_sum[:hidden],
    )


def solution(mesh):
    split = P("dp", "seq", None)
    in_specs = (split, split, split, P("dp", "seq")) + (P(),) * 9
    out_specs = (split, split) + (P(),) * 9
    return jax.shard_map(body, mesh=mesh, in_specs=in_specs, out_specs=out_specs, check_vma=False)
```

```python
import functools

import jax
import jax.numpy as jnp
from jax import lax
from jax.experimental import pallas as pl
from jax.experimental.pallas import tpu as pltpu
from jax.sharding import PartitionSpec as P

H = 8
HD = 64
LANES = 2 * HD
WIDE = H * LANES
SPAN = 512
NEAR = 4
SCALE = HD ** (-0.5)
NEG = -1e30
EPS = 1e-06
VMEM_LIMIT = 56 * 1024 * 1024

F32 = jnp.float32
BF16 = jnp.bfloat16


def dot(left, right):
    return jnp.dot(left, right, preferred_element_type=F32)


def dot_back(left, right):
    return lax.dot_general(left, right, (((1,), (1,)), ((), ())), preferred_element_type=F32)


def rows_dot(left, right):
    return lax.dot_general(left, right, (((0,), (0,)), ((), ())), preferred_element_type=F32)


def cost_of(microseconds):
    return pl.CostEstimate(flops=int(microseconds * 1e9), bytes_accessed=int(microseconds * 3e6), transcendentals=0)


def block_rows(rows):
    return 256 if rows % 256 == 0 else rows


def head_lanes(h):
    return slice(h * LANES, (h + 1) * LANES)


TILE = 256
REACH = SPAN + TILE
HEADS = 2
CHUNKS = 32
EARLY_ROWS = 144
LATE_ROWS = 64


def window_parts(first):
    before = max(SPAN - first, 0)
    parts = [(True, SPAN - before, before)] if before else []
    return parts + [(False, max(first - SPAN, 0), REACH - before)]


def window_keys(halo_ref, own_ref, first, lanes):
    return [(halo_ref if halo else own_ref)[at : at + n, lanes] for halo, at, n in window_parts(first)]


def window_bias(query_axis):
    shape = (TILE, REACH) if query_axis == 0 else (REACH, TILE)
    query = lax.broadcasted_iota(jnp.int32, shape, query_axis)
    key = lax.broadcasted_iota(jnp.int32, shape, 1 - query_axis)
    return jnp.where((key > query) & (key <= query + SPAN), 0.0, NEG)


def masked(scores, bias, first, base, key_axis):
    cut = lambda v, i, j: v[i:j] if key_axis == 0 else v[:, i:j]
    out = []
    for at in range(0, REACH, TILE):
        part = cut(scores, at, at + TILE)
        if at == 0 or at == SPAN:
            part = part + cut(bias, at, at + TILE)
        if first + at < SPAN:
            part = part + jnp.where(base + first + at >= SPAN, 0.0, NEG)
        out.append(part)
    return jnp.concatenate(out, axis=key_axis)


def pipelined(work, before, middle, after):
    ready = before(*work[0])
    held = None
    for k, item in enumerate(work):
        following = before(*work[k + 1]) if k + 1 < len(work) else None
        done = middle(item, ready)
        if held is not None:
            after(*held)
        held, ready = (item, done), following
    after(*held)


def local_kernel(start, base_ref, ask_ref, halo_ref, own_ref, out_ref, total_ref, bias_ref, totals):
    step = pl.program_id(0)
    base = base_ref[0]

    @pl.when(step == 0)
    def fill():
        bias_ref[...] = window_bias(0)

    lane = lax.broadcasted_iota(jnp.int32, (TILE, LANES), 1)

    def scores(at, g):
        query = jnp.where(lane < HD, ask_ref[at : at + TILE, head_lanes(g)], 0.0).astype(BF16)
        return jnp.concatenate([dot_back(query, k) for k in window_keys(halo_ref, own_ref, start + at, head_lanes(g))], axis=1)

    def softmax(item, raw):
        raw = masked(raw, bias_ref, start + item[0], base, 1)
        top = jnp.max(raw, axis=1, keepdims=True)
        expo = jnp.exp(raw - top)
        return expo.astype(BF16), jnp.sum(expo, axis=1, keepdims=True), top

    def finish(item, done):
        at, g = item
        expo, total, top = done
        out, column = None, 0
        for keys in window_keys(halo_ref, own_ref, start + at, head_lanes(g)):
            term = dot(expo[:, column : column + keys.shape[0]], keys)
            column += keys.shape[0]
            out = term if out is None else out + term
        here = slice(at, at + TILE)
        out_ref[here, head_lanes(g)] = (out * (1.0 / total)).astype(BF16)
        totals[here, :] = jnp.where(lane == step * HEADS + g, top + jnp.log(total), totals[here, :])

    pipelined([(at, g) for g in range(HEADS) for at in range(0, ask_ref.shape[0], TILE)], scores, softmax, finish)

    @pl.when(step == H // HEADS - 1)
    def turn():
        for at in range(0, ask_ref.shape[0], LANES):
            total_ref[:, at : at + LANES] = totals[at : at + LANES, :].T[:H, :]


def local_attention(base, ask, halo, own, start, stop, earlier=(), after=()):
    rows = ask.shape[0]
    count = stop - start
    wide = HEADS * LANES
    part = lambda h: (start // count, h)
    held = [pl.BlockSpec(memory_space=pl.ANY)] * (len(earlier) + len(after))
    return pl.pallas_call(
        lambda *refs: local_kernel(start, *refs[:4], *refs[4 + len(held) :]),
        grid=(H // HEADS,),
        in_specs=[
            pl.BlockSpec(memory_space=pltpu.SMEM),
            pl.BlockSpec((count, wide), part),
            pl.BlockSpec((SPAN, wide), lambda h: (0, h)),
            pl.BlockSpec((rows, wide), lambda h: (0, h)),
        ]
        + held,
        out_specs=[pl.BlockSpec((count, wide), part), pl.BlockSpec((H, count), lambda h: (0, start // count))],
        out_shape=[jax.ShapeDtypeStruct((rows, WIDE), BF16), jax.ShapeDtypeStruct((H, rows), F32)],
        scratch_shapes=[pltpu.VMEM((TILE, REACH), F32), pltpu.VMEM((count, LANES), F32)],
        input_output_aliases={4 + k: k for k in range(len(earlier))},
        compiler_params=pltpu.CompilerParams(vmem_limit_bytes=VMEM_LIMIT),
        cost_estimate=cost_of(count / 80),
        name="local_attention",
    )(base, ask, halo, own, *earlier, *after)


def local_back_kernel(
    first_step, base_ref, ask_ref, halo_ref, own_ref, grad_ref, total_ref, inner_ref, partial_ref, far_grad_ref,
    ask_grad_ref, memory_grad_ref, sums_ref, bias_ref,
):
    step = pl.program_id(0) + first_step
    rows = ask_ref.shape[0]
    base = base_ref[0]
    start = far_grad_ref.shape[0] - rows - SPAN

    @pl.when(step == first_step)
    def fill():
        bias_ref[...] = window_bias(1)

    left = left_lanes(TILE)
    sums_ref[...] = far_grad_ref[...].astype(F32)

    def query_of(first, g):
        return jnp.where(left, ask_ref[first : first + TILE, head_lanes(g)], 0.0).astype(BF16)

    def products(first, g):
        keys = window_keys(halo_ref, own_ref, first, head_lanes(g))
        query, grad = query_of(first, g), grad_ref[first : first + TILE, head_lanes(g)]
        join = lambda rows: jnp.concatenate([dot_back(k, rows) for k in keys], axis=0)
        return join(query), join(grad)

    def score_grads(item, done):
        first, g = item
        scores, prob_grad = done
        here = slice(first, first + TILE)
        total = total_ref[pl.ds(step * HEADS + g, 1), here]
        inner = inner_ref[pl.ds(step * HEADS + g, 1), here]
        probs = jnp.exp(masked(scores, bias_ref, first, base, 0) - total)
        return (probs * (prob_grad - inner)).astype(BF16), probs.astype(BF16)

    def finish(item, done):
        first, g = item
        score_grad, probs = done
        here, lanes = slice(first, first + TILE), head_lanes(g)
        query_grad, row = None, 0
        for keys in window_keys(halo_ref, own_ref, first, lanes):
            term = rows_dot(score_grad[row : row + keys.shape[0]], keys)
            row += keys.shape[0]
            query_grad = term if query_grad is None else query_grad + term
        sums_ref[start + first : start + first + REACH, lanes] += dot(score_grad, query_of(first, g)) + dot(
            probs, grad_ref[here, lanes]
        )
        partial = partial_ref[here, lanes].astype(F32)
        ask_grad_ref[here, lanes] = (partial + jnp.where(left, query_grad * SCALE, 0.0)).astype(BF16)

    pipelined([(first, g) for g in range(HEADS) for first in range(0, rows, TILE)], products, score_grads, finish)
    memory_grad_ref[...] = sums_ref[...].astype(BF16)


def local_attention_back(base, ask, halo, own, grad, total, inner, partial, far_grad, steps, earlier=(), after=()):
    rows = ask.shape[0]
    length = far_grad.shape[0]
    first = steps[0]
    head = lambda n: pl.BlockSpec((n, HEADS * LANES), lambda h: (0, h + first))
    flat = pl.BlockSpec((H, rows), lambda h: (0, 0))
    held = [pl.BlockSpec(memory_space=pl.ANY)] * (len(earlier) + len(after))
    return pl.pallas_call(
        lambda *refs: local_back_kernel(first, *refs[:9], *refs[9 + len(held) :]),
        grid=(len(steps),),
        in_specs=[
            pl.BlockSpec(memory_space=pltpu.SMEM),
            head(rows),
            head(SPAN),
            head(rows),
            head(rows),
            flat,
            flat,
            head(rows),
            head(length),
        ]
        + held,
        out_specs=[head(rows), head(length)],
        out_shape=[
            jax.ShapeDtypeStruct((rows, WIDE), BF16),
            jax.ShapeDtypeStruct((length, WIDE), BF16),
        ],
        scratch_shapes=[pltpu.VMEM((length, HEADS * LANES), F32), pltpu.VMEM((REACH, TILE), F32)],
        input_output_aliases={9 + k: k for k in range(len(earlier))},
        compiler_params=pltpu.CompilerParams(vmem_limit_bytes=VMEM_LIMIT),
        cost_estimate=cost_of(5 * len(steps)),
        name="local_attention_back",
    )(base, ask, halo, own, grad, total, inner, partial, far_grad, *earlier, *after)


def token_tile(ref, token):
    return ref[pl.ds(pl.multiple_of(token * H, H), H), :]


def put_heads(ref, h, values):
    ref[pl.ds(h, values.shape[0], stride=H), :] = values


def take_heads(ref, h, count):
    return ref[pl.ds(h, count, stride=H), :]


def left_lanes(count):
    return lax.broadcasted_iota(jnp.int32, (count, LANES), 1) < HD


def build_table(table, others_ref, own_ref):
    base = 0
    for ref in (others_ref, own_ref):
        for at in range(0, ref.shape[0], 256):
            for h in range(H):
                table[pl.ds((base + at) * H + h, 256, stride=H), :] = ref[at : at + 256, head_lanes(h)].astype(F32)
        base += ref.shape[0]


def row_sums(values):
    return jnp.sum(values, axis=1, keepdims=True)


def softmax_over(match):
    top = functools.reduce(jnp.maximum, match)
    expo = [jnp.exp(m - top) for m in match]
    scale = 1.0 / functools.reduce(jnp.add, expo)
    return [e * scale for e in expo]


TOKENS = 128
GROUP = 16


def lane_sums(values):
    return dot(values.astype(BF16), jnp.ones((LANES, LANES), BF16))


def gather_group(index_ref, table, near_rows, first, group):
    for k in range(GROUP):
        t = group * GROUP + k
        for j in range(NEAR):
            near_rows[j, t * H : (t + 1) * H, :] = token_tile(table, index_ref[(first + t) * NEAR + j])


def scatter_group(index_ref, sums, terms, first, group):
    for k in range(GROUP):
        t = group * GROUP + k
        for j in range(NEAR):
            there = pl.ds(pl.multiple_of(index_ref[(first + t) * NEAR + j] * H, H), H)
            held = sums[j % len(sums)]
            held[there, :] = held[there, :] + terms[j, t * H : (t + 1) * H, :]


def retrieve_kernel(
    index_ref, others_ref, own_ref, ask_ref, local_ref, open_ref, near_ref, weight_ref, blended_ref,
    table, ask_rows, out_rows, near_rows,
):
    step = pl.program_id(0)
    count = ask_ref.shape[0]
    first = step * count

    @pl.when(step == 0)
    def build():
        build_table(table, others_ref, own_ref)

    for h in range(H):
        put_heads(ask_rows, h, ask_ref[:, head_lanes(h)].astype(F32))
    left = left_lanes(GROUP * H)
    groups = count // GROUP
    gather_group(index_ref, table, near_rows, first, 0)
    for group in range(groups):
        if group + 1 < groups:
            gather_group(index_ref, table, near_rows, first, group + 1)
        here = slice(group * GROUP * H, (group + 1) * GROUP * H)
        query = jnp.where(left, ask_rows[here, :], 0.0)
        weight = softmax_over([lane_sums(near_rows[j, here, :] * query) for j in range(NEAR)])
        out_rows[here, :] = functools.reduce(jnp.add, [weight[j] * near_rows[j, here, :] for j in range(NEAR)])
        for j in range(NEAR):
            weight_ref[j, here, :] = weight[j].astype(BF16)
            near_ref[j, here, :] = near_rows[j, here, :].astype(BF16)
    open_rows = open_ref[...]
    left = left_lanes(count)
    for h in range(H):
        lanes = head_lanes(h)
        local = local_ref[:, lanes].astype(F32)
        mix = (1.0 - jax.nn.sigmoid(ask_ref[:, lanes].astype(F32))) * open_rows
        blended = local + mix * (take_heads(out_rows, h, count) - local)
        blended_ref[:, lanes] = jnp.where(left, 0.0, blended).astype(BF16)


def retrieve(index, others, own, ask, local, open_rows):
    rows = ask.shape[0]
    length = others.shape[0] + rows
    count = min(TOKENS, rows)
    wide = pl.BlockSpec((count, WIDE), lambda c: (c, 0))
    tall = pl.BlockSpec((NEAR, count * H, LANES), lambda c: (0, c, 0))
    return pl.pallas_call(
        retrieve_kernel,
        grid=(rows // count,),
        in_specs=[
            pl.BlockSpec(memory_space=pltpu.SMEM),
            pl.BlockSpec((length - rows, WIDE), lambda c: (0, 0)),
            pl.BlockSpec((rows, WIDE), lambda c: (0, 0)),
            wide,
            wide,
            pl.BlockSpec((count, 1), lambda c: (c, 0)),
        ],
        out_specs=[tall, tall, wide],
        out_shape=[
            jax.ShapeDtypeStruct((NEAR, rows * H, LANES), BF16),
            jax.ShapeDtypeStruct((NEAR, rows * H, LANES), BF16),
            jax.ShapeDtypeStruct((rows, WIDE), BF16),
        ],
        scratch_shapes=[
            pltpu.VMEM((length * H, LANES), F32),
            pltpu.VMEM((count * H, LANES), F32),
            pltpu.VMEM((count * H, LANES), F32),
            pltpu.VMEM((NEAR, count * H, LANES), F32),
        ],
        compiler_params=pltpu.CompilerParams(vmem_limit_bytes=VMEM_LIMIT),
        cost_estimate=cost_of(12),
        name="retrieve",
    )(index, others, own, ask, local, open_rows)


def retrieve_back_kernel(
    index_ref, grad_ref, ask_ref, local_ref, open_ref, near_ref, weight_ref,
    local_grad_ref, inner_ref, partial_ref, far_ref,
    sums_even, sums_odd, ask_rows, grad_rows, out_rows, mixed, terms,
):
    step = pl.program_id(0)
    count = ask_ref.shape[0]
    first = step * count
    length = far_ref.shape[0]

    @pl.when(step == 0)
    def clear():
        sums_even[...] = jnp.zeros_like(sums_even)
        sums_odd[...] = jnp.zeros_like(sums_odd)

    open_rows = open_ref[...]
    left = left_lanes(count)
    lane = lax.broadcasted_iota(jnp.int32, (count, LANES), 1)
    inner_all = jnp.zeros((count, LANES), F32)
    for h in range(H):
        lanes = head_lanes(h)
        grad = grad_ref[:, lanes].astype(F32)
        ask = ask_ref[:, lanes].astype(F32)
        mix = (1.0 - jax.nn.sigmoid(ask)) * open_rows
        inner = row_sums(grad * local_ref[:, lanes].astype(F32))
        inner_all = jnp.where(lane == HD + h, inner - mix * inner, inner_all)
        mixed[:, lanes] = mix * inner
        local_grad_ref[:, lanes] = (grad - mix * grad).astype(BF16)
        put_heads(ask_rows, h, jnp.where(left, ask, mix))
        put_heads(grad_rows, h, grad)
    inner_ref[...] = inner_all.T[HD : HD + H, :]
    groups = count // GROUP
    left_tile = left_lanes(GROUP * H)
    sums = (sums_even, sums_odd)
    for group in range(groups):
        here = slice(group * GROUP * H, (group + 1) * GROUP * H)
        ask = ask_rows[here, :]
        grad = ask * grad_rows[here, :]
        source = jnp.where(left_tile, ask, grad)
        near = [near_ref[j, here, :].astype(F32) for j in range(NEAR)]
        weight_grad = [lane_sums(n * grad) for n in near]
        weight = [weight_ref[j, here, :].astype(F32) for j in range(NEAR)]
        inner = functools.reduce(jnp.add, [w * g for w, g in zip(weight, weight_grad)])
        match_grad = [w * (g - inner) for w, g in zip(weight, weight_grad)]
        query_grad = functools.reduce(jnp.add, [g * n for g, n in zip(match_grad, near)])
        out_rows[here, :] = jnp.where(left_tile, query_grad * SCALE, inner)
        for j in range(NEAR):
            terms[j, here, :] = jnp.where(left_tile, match_grad[j], weight[j]) * source
        if group:
            scatter_group(index_ref, sums, terms, first, group - 1)
    scatter_group(index_ref, sums, terms, first, groups - 1)
    for h in range(H):
        lanes = head_lanes(h)
        tile = take_heads(out_rows, h, count)
        gate = jax.nn.sigmoid(ask_ref[:, lanes].astype(F32))
        partial_ref[:, lanes] = jnp.where(left, tile, gate * (mixed[:, lanes] - tile)).astype(BF16)

    @pl.when(step == pl.num_programs(0) - 1)
    def finish():
        for at in range(0, length, 256):
            for h in range(H):
                there = pl.ds(at * H + h, 256, stride=H)
                far_ref[at : at + 256, head_lanes(h)] = (sums_even[there, :] + sums_odd[there, :]).astype(BF16)


def retrieve_back(index, grad, ask, local, open_rows, near, weight, length, after=()):
    rows = ask.shape[0]
    count = min(TOKENS, rows)
    wide = pl.BlockSpec((count, WIDE), lambda c: (c, 0))
    tall = pl.BlockSpec((NEAR, count * H, LANES), lambda c: (0, c, 0))
    return pl.pallas_call(
        lambda *refs: retrieve_back_kernel(*refs[:7], *refs[7 + len(after) :]),
        grid=(rows // count,),
        in_specs=[
            pl.BlockSpec(memory_space=pltpu.SMEM),
            wide,
            wide,
            wide,
            pl.BlockSpec((count, 1), lambda c: (c, 0)),
            tall,
            tall,
        ]
        + [pl.BlockSpec(memory_space=pl.ANY)] * len(after),
        out_specs=[
            wide,
            pl.BlockSpec((H, count), lambda c: (0, c)),
            wide,
            pl.BlockSpec((length, WIDE), lambda c: (0, 0)),
        ],
        out_shape=[
            jax.ShapeDtypeStruct((rows, WIDE), BF16),
            jax.ShapeDtypeStruct((H, rows), F32),
            jax.ShapeDtypeStruct((rows, WIDE), BF16),
            jax.ShapeDtypeStruct((length, WIDE), BF16),
        ],
        scratch_shapes=[
            pltpu.VMEM((length * H, LANES), F32),
            pltpu.VMEM((length * H, LANES), F32),
            pltpu.VMEM((count * H, LANES), F32),
            pltpu.VMEM((count * H, LANES), F32),
            pltpu.VMEM((count * H, LANES), F32),
            pltpu.VMEM((count, WIDE), F32),
            pltpu.VMEM((NEAR, count * H, LANES), F32),
        ],
        compiler_params=pltpu.CompilerParams(vmem_limit_bytes=VMEM_LIMIT),
        cost_estimate=cost_of(24),
        name="retrieve_back",
    )(index, grad, ask, local, open_rows, near, weight, *after)


def turned(block, shift):
    size = lax.axis_size("seq")
    return lax.ppermute(block, "seq", [((i + shift) % size, i) for i in range(size)])


def index_bits(axis):
    return [(axis, b) for b in range(lax.axis_size(axis).bit_length() - 1)]


def level_groups():
    dp, seq = index_bits("dp"), index_bits("seq")
    return [dp[:1], dp[1:3], seq[:1] + dp[3:4]], dp[4:] + seq[1:]


def own_place(group):
    place = 0
    for k, (axis, bit) in enumerate(group):
        place = place + (((lax.axis_index(axis) >> bit) & 1) << k)
    return place


def own_chunk():
    chunk = 0
    for group in level_groups()[0]:
        chunk = (chunk << len(group)) + own_place(group)
    return jnp.reshape(chunk, (1,)).astype(jnp.int32)


def swapped(block, group, distance):
    flips = {"dp": 0, "seq": 0}
    for k, (axis, bit) in enumerate(group):
        if (distance >> k) & 1:
            flips[axis] |= 1 << bit
    n_dp, n_seq = lax.axis_size("dp"), lax.axis_size("seq")
    if not flips["seq"]:
        return lax.ppermute(block, "dp", [(i, i ^ flips["dp"]) for i in range(n_dp)])
    if not flips["dp"]:
        return lax.ppermute(block, "seq", [(i, i ^ flips["seq"]) for i in range(n_seq)])
    route = [(i, (i // n_seq ^ flips["dp"]) * n_seq + (i % n_seq ^ flips["seq"])) for i in range(n_dp * n_seq)]
    return lax.ppermute(block, ("dp", "seq"), route)


def whole_call(kernel, name, *operands, outs, scratch=(), after=(), cost=0.3):
    place = lambda v: pltpu.SMEM if v.dtype == jnp.int32 else pltpu.VMEM
    count = len(operands)

    def without_after(*refs):
        kernel(*refs[:count], *refs[count + len(after) :])

    return pl.pallas_call(
        without_after,
        in_specs=[pl.BlockSpec(memory_space=place(v)) for v in operands] + [pl.BlockSpec(memory_space=pl.ANY)] * len(after),
        out_specs=[pl.BlockSpec(memory_space=pltpu.VMEM)] * len(outs),
        out_shape=[jax.ShapeDtypeStruct(shape, dtype) for shape, dtype in outs],
        scratch_shapes=list(scratch),
        compiler_params=pltpu.CompilerParams(vmem_limit_bytes=VMEM_LIMIT),
        cost_estimate=cost_of(cost),
        name=name,
    )(*operands, *after)


def add_pieces(own, arrived, pieces, after=()):
    rows, width = own.shape
    count = rows // pieces

    def kernel(*refs):
        terms, outs = refs[: 1 + len(arrived)], refs[1 + len(arrived) :]
        for k, out in enumerate(outs):
            here = slice(k * count, (k + 1) * count)
            total = terms[0][here, :].astype(F32)
            for term in terms[1:]:
                total = total + term[here, :].astype(F32)
            out[...] = total.astype(BF16)

    return whole_call(kernel, "add_pieces", own, *arrived, outs=[((count, width), BF16)] * pieces, after=after)


def join_pieces(pieces, after=()):
    count, width = pieces[0].shape

    def kernel(*refs):
        for k, ref in enumerate(refs[:-1]):
            refs[-1][k * count : (k + 1) * count, :] = ref[...]

    return whole_call(kernel, "join_pieces", *pieces, outs=[((count * len(pieces), width), BF16)], after=after)[0]


def scatter_start(own, send):
    return own, [swapped(send, level_groups()[0][0], 1)]


def scatter_level(held, level, after=()):
    own, arrived = held
    group = level_groups()[0][level]
    pieces = add_pieces(own, arrived, 2 ** len(group), after)
    return pieces[0], [swapped(piece, group, d) for d, piece in enumerate(pieces) if d]


def scatter_finish(held, after=()):
    total = add_pieces(*held, 1, after)[0]
    for bit in level_groups()[1]:
        total = add_pieces(total, [swapped(total, [bit], 1)], 1)[0]
    return total


def gather_level(total, level):
    group = level_groups()[0][level]
    return [total] + [swapped(total, group, d) for d in range(1, 2 ** len(group))]


def rms_unit(values):
    scale = lax.rsqrt(jnp.mean(values * values, axis=-1, keepdims=True) + EPS)
    return values * scale, scale


def rms_back(unit, scale, grad):
    return scale * (grad - unit * jnp.mean(grad * unit, axis=-1, keepdims=True))


def project_kernel(inputs_ref, gain_ref, ask_weight_ref, memory_weight_ref, normed_ref, ask_ref, memory_ref):
    left = (lax.broadcasted_iota(jnp.int32, (1, WIDE), 1) % LANES) < HD
    rows = inputs_ref.shape[0]
    block = block_rows(rows)
    for at in range(0, rows, block):
        here = slice(at, at + block)
        normed = (rms_unit(inputs_ref[here, :].astype(F32))[0] * gain_ref[0:1, :]).astype(BF16)
        normed_ref[here, :] = normed
        memory_ref[here, :] = dot(normed, memory_weight_ref[...]).astype(BF16)
        if ask_ref is not None:
            ask = dot(normed, ask_weight_ref[...])
            ask_ref[here, :] = jnp.where(left, ask * SCALE, ask).astype(BF16)


def project(inputs, gain, ask_weight, memory_weight, after=()):
    rows, width = inputs.shape
    outs = [((rows, width), BF16), ((rows, WIDE), BF16), ((rows, WIDE), BF16)]
    return whole_call(
        project_kernel, "project", inputs, gain, ask_weight, memory_weight, outs=outs, after=after, cost=3
    )


def project_memory(inputs, gain, memory_weight, after=()):
    rows, width = inputs.shape

    def kernel(inputs_ref, gain_ref, weight_ref, normed_ref, memory_ref):
        project_kernel(inputs_ref, gain_ref, None, weight_ref, normed_ref, None, memory_ref)

    outs = [((rows, width), BF16), ((rows, WIDE), BF16)]
    return whole_call(kernel, "project_memory", inputs, gain, memory_weight, outs=outs, after=after, cost=2)


ROOT = 0.7978845608028654
CUBE = 0.044715


def gelu_and_slope(x):
    square = x * x
    tanh = jnp.tanh(ROOT * (x * (1.0 + CUBE * square)))
    half = 0.5 * (1.0 + tanh)
    slope = half + (0.5 * ROOT) * x * (1.0 - tanh * tanh) * (1.0 + (3.0 * CUBE) * square)
    return x * half, slope


def feed_forward_kernel(
    chunk_ref, inputs_ref, cotangent_ref, blended_ref, blend_weight_ref, gain_ref, hidden_weight_ref, return_weight_ref,
    outputs_ref, resid_grad_ref, blended_grad_ref, gain_grad_ref, own_ref, send_ref,
    resid, normed, active, hidden_grad, resid_grad_b, return_sums, hidden_sums, blend_sums,
):
    rows, width = inputs_ref.shape
    hidden = hidden_weight_ref.shape[1]
    block = block_rows(rows)
    blocks = [slice(at, at + block) for at in range(0, rows, block)]
    gain = gain_ref[0:1, :]
    for here in blocks:
        values = inputs_ref[here, :].astype(F32) + dot(blended_ref[here, :], blend_weight_ref[...])
        resid[here, :] = values
        normed[here, :] = (rms_unit(values)[0] * gain).astype(BF16)

    def products(here, lanes):
        return dot(normed[here, :], hidden_weight_ref[:, lanes]), dot_back(cotangent_ref[here, :], return_weight_ref[lanes, :])

    def activate(item, done):
        value, slope = gelu_and_slope(done[0])
        return value.astype(BF16), (done[1] * slope).astype(BF16)

    def keep(item, done):
        active[item[0], item[1]] = done[0]
        hidden_grad[item[0], item[1]] = done[1]

    step = min(width, hidden)
    columns = [slice(at, at + step) for at in range(0, hidden, step)]
    pipelined([(here, lanes) for here in blocks for lanes in columns], products, activate, keep)
    gain_grad = jnp.zeros((1, width), F32)
    for here in blocks:
        outputs_ref[here, :] = (resid[here, :] + dot(active[here, :], return_weight_ref[...])).astype(BF16)
        grad = dot_back(hidden_grad[here, :], hidden_weight_ref[...])
        unit, scale = rms_unit(resid[here, :])
        gain_grad = gain_grad + jnp.sum(grad * unit, axis=0, keepdims=True)
        total = cotangent_ref[here, :].astype(F32) + rms_back(unit, scale, grad * gain)
        resid_grad_ref[here, :] = total
        resid_grad_b[here, :] = total.astype(BF16)
        blended_grad_ref[here, :] = dot_back(total.astype(BF16), blend_weight_ref[...]).astype(BF16)
    gain_grad_ref[...] = jnp.broadcast_to(gain_grad, gain_grad_ref.shape)
    for lanes in columns:
        return_sums[lanes, :] = rows_dot(active[:, lanes], cotangent_ref[...]).astype(BF16)
        hidden_sums[:, lanes] = rows_dot(normed[...], hidden_grad[:, lanes]).astype(BF16)
    blend_sums[...] = rows_dot(blended_ref[...], resid_grad_b[...]).astype(BF16)
    tall, flat = hidden // CHUNKS, width // CHUNKS
    per_head = HD // flat
    for r in range(CHUNKS):
        chunk = chunk_ref[0] ^ r
        out = own_ref if r < CHUNKS // 2 else send_ref
        at = (r % (CHUNKS // 2)) * EARLY_ROWS
        out[at : at + tall, :] = return_sums[pl.ds(pl.multiple_of(chunk * tall, tall), tall), :]
        at += tall
        for c in range(hidden // width):
            out[at : at + flat, :] = hidden_sums[
                pl.ds(pl.multiple_of(chunk * flat, flat), flat), c * width : (c + 1) * width
            ]
            at += flat
        row = (chunk // per_head) * LANES + HD + (chunk % per_head) * flat
        out[at : at + flat, :] = blend_sums[pl.ds(pl.multiple_of(row, flat), flat), :]


def feed_forward(chunk, inputs, cotangent, blended, blend_weight, gain, hidden_weight, return_weight):
    rows, width = inputs.shape
    hidden = hidden_weight.shape[1]
    half = ((CHUNKS // 2 * EARLY_ROWS, width), BF16)
    return whole_call(
        feed_forward_kernel,
        "feed_forward",
        chunk,
        inputs,
        cotangent,
        blended,
        blend_weight,
        gain,
        hidden_weight,
        return_weight,
        outs=[((rows, width), BF16), ((rows, width), F32), ((rows, WIDE), BF16), ((8, width), F32), half, half],
        scratch=[
            pltpu.VMEM((rows, width), F32),
            pltpu.VMEM((rows, width), BF16),
            pltpu.VMEM((rows, hidden), BF16),
            pltpu.VMEM((rows, hidden), BF16),
            pltpu.VMEM((rows, width), BF16),
            pltpu.VMEM((hidden, width), BF16),
            pltpu.VMEM((width, hidden), BF16),
            pltpu.VMEM((WIDE, width), BF16),
        ],
        cost=20,
    )


def unpack_early_kernel(chunk_ref, own_ref, other_ref, return_ref, hidden_ref, output_ref):
    width = return_ref.shape[1]
    tall, flat = return_ref.shape[0] // CHUNKS, hidden_ref.shape[0] // CHUNKS
    for r in range(CHUNKS):
        chunk = chunk_ref[0] ^ r
        source = own_ref if r < CHUNKS // 2 else other_ref
        at = (r % (CHUNKS // 2)) * EARLY_ROWS
        return_ref[pl.ds(pl.multiple_of(chunk * tall, tall), tall), :] = source[at : at + tall, :].astype(F32)
        at += tall
        there = pl.ds(pl.multiple_of(chunk * flat, flat), flat)
        for c in range(hidden_ref.shape[1] // width):
            hidden_ref[there, c * width : (c + 1) * width] = source[at : at + flat, :].astype(F32)
            at += flat
        output_ref[there, :] = source[at : at + flat, :].astype(F32)


def unpack_early(chunk, own, other, return_shape, hidden_shape, after=()):
    width = return_shape[1]
    outs = [(return_shape, F32), (hidden_shape, F32), ((width, width), F32)]
    return whole_call(unpack_early_kernel, "unpack_early", chunk, own, other, outs=outs, after=after)


def late_kernel(
    chunk_ref, others_ref, normed_ref, ask_ref, memory_ref, first_ref, second_ref, own_ref, send_ref, ask_sums, memory_sums, small_sums
):
    width = normed_ref.shape[1]
    far = others_ref.shape[0]
    flat = width // CHUNKS
    ask_sums[...] = rows_dot(normed_ref[...], ask_ref[...]).astype(BF16)
    memory_sums[...] = (
        rows_dot(others_ref[...], memory_ref[:far, :]) + rows_dot(normed_ref[...], memory_ref[far:, :])
    ).astype(BF16)
    row = lax.broadcasted_iota(jnp.int32, (width, width), 0)
    column = lax.broadcasted_iota(jnp.int32, (width, width), 1)
    turn = lambda ref: jnp.sum(jnp.where(row == column, ref[0:1, :], 0.0), axis=1, keepdims=True)
    lane = lax.broadcasted_iota(jnp.int32, (width, LANES), 1)
    small = jnp.where(lane == H, turn(first_ref), jnp.where(lane == H + 1, turn(second_ref), 0.0))
    for h in range(H):
        at = h * LANES + HD
        small = jnp.where(lane == h, ask_sums[:, at : at + 1].astype(F32), small)
    small_sums[...] = small.astype(BF16)
    for r in range(CHUNKS):
        chunk = chunk_ref[0] ^ r
        out = own_ref if r < CHUNKS // 2 else send_ref
        at = (r % (CHUNKS // 2)) * LATE_ROWS
        here = pl.ds(pl.multiple_of(chunk * flat, flat), flat)
        for pair in range(H // 2):
            lanes = slice(pair * LANES, (pair + 1) * LANES)
            even = slice(2 * pair * LANES, 2 * pair * LANES + HD)
            odd = slice((2 * pair + 1) * LANES, (2 * pair + 1) * LANES + HD)
            out[at : at + flat, lanes] = jnp.concatenate([ask_sums[here, even], ask_sums[here, odd]], axis=1)
        out[at + flat : at + 2 * flat, :] = memory_sums[here, :width]
        out[at + 2 * flat : at + 3 * flat, :] = memory_sums[here, width:]
        out[at + 3 * flat : at + 4 * flat, :LANES] = small_sums[here, :]
        out[at + 3 * flat : at + 4 * flat, LANES:] = jnp.zeros((flat, width - LANES), BF16)


def unpack_late_kernel(
    chunk_ref, own_ref, other_ref, query_ref, key_ref, value_ref, gate_ref, first_ref, second_ref, small_ref
):
    width = query_ref.shape[1]
    flat = width // CHUNKS
    for r in range(CHUNKS):
        chunk = chunk_ref[0] ^ r
        source = own_ref if r < CHUNKS // 2 else other_ref
        at = (r % (CHUNKS // 2)) * LATE_ROWS
        there = pl.ds(pl.multiple_of(chunk * flat, flat), flat)
        query_ref[there, :] = source[at : at + flat, :].astype(F32)
        for half in range(2):
            at += flat
            for pair in range(H // 4):
                lanes = slice((half * H // 4 + pair) * LANES, (half * H // 4 + pair + 1) * LANES)
                even = source[at : at + flat, 2 * pair * LANES : (2 * pair + 1) * LANES]
                odd = source[at : at + flat, (2 * pair + 1) * LANES : (2 * pair + 2) * LANES]
                key_ref[there, lanes] = jnp.concatenate([even[:, :HD], odd[:, :HD]], axis=1).astype(F32)
                value_ref[there, lanes] = jnp.concatenate([even[:, HD:], odd[:, HD:]], axis=1).astype(F32)
        at += flat
        small_ref[there, :] = source[at : at + flat, :LANES].astype(F32)
    gate_ref[...] = small_ref[:, :H]
    turned_small = small_ref[...].T
    first_ref[...] = turned_small[H : H + 1, :]
    second_ref[...] = turned_small[H + 1 : H + 2, :]


def pack_late(chunk, others, normed, ask_grad, memory_grad, first_grad, second_grad, after=()):
    width = normed.shape[1]
    half = ((CHUNKS // 2 * LATE_ROWS, width), BF16)
    return whole_call(
        late_kernel,
        "late_weight_grads",
        chunk,
        others,
        normed,
        ask_grad,
        memory_grad,
        first_grad,
        second_grad,
        outs=[half, half],
        scratch=[pltpu.VMEM((width, WIDE), BF16), pltpu.VMEM((width, WIDE), BF16), pltpu.VMEM((width, LANES), BF16)],
        after=after,
    )


def unpack_late(chunk, own, other):
    width = own.shape[1]
    square, row = ((width, width), F32), ((1, width), F32)
    return whole_call(
        unpack_late_kernel,
        "unpack_late",
        chunk,
        own,
        other,
        outs=[square, square, square, ((width, H), F32), row, row],
        scratch=[pltpu.VMEM((width, LANES), F32)],
    )


def normed_back_kernel(
    inputs_ref, others_ref, ask_ref, memory_ref, ask_weight_ref, memory_weight_ref, own_grad_ref, others_grad_ref, gain_ref
):
    rows, width = inputs_ref.shape
    length = memory_ref.shape[0]
    block = block_rows(rows)

    def unit(ref, here):
        values = ref[here, :].astype(F32)
        return values * lax.rsqrt(jnp.mean(values * values, axis=-1, keepdims=True) + EPS)

    gain = jnp.zeros((1, width), F32)
    for at in range(0, length - rows, block):
        here = slice(at, at + block)
        grad = dot_back(memory_ref[here, :], memory_weight_ref[...])
        others_grad_ref[here, :] = grad.astype(BF16)
        gain = gain + jnp.sum(grad * unit(others_ref, here), axis=0, keepdims=True)
    for at in range(0, rows, block):
        here = slice(at, at + block)
        there = slice(length - rows + at, length - rows + at + block)
        grad = dot_back(ask_ref[here, :], ask_weight_ref[...]) + dot_back(memory_ref[there, :], memory_weight_ref[...])
        own_grad_ref[here, :] = grad
        gain = gain + jnp.sum(grad * unit(inputs_ref, here), axis=0, keepdims=True)
    gain_ref[...] = jnp.broadcast_to(gain, gain_ref.shape)


def normed_back(inputs, others, ask_grad, memory_grad, ask_weight, memory_weight, after=()):
    rows, width = inputs.shape
    return whole_call(
        normed_back_kernel,
        "normed_back",
        inputs,
        others,
        ask_grad,
        memory_grad,
        ask_weight,
        memory_weight,
        outs=[((rows, width), F32), (others.shape, BF16), ((8, width), F32)],
        after=after,
    )


def input_back_kernel(inputs_ref, gain_ref, resid_grad_ref, own_ref, *refs):
    arrived, out_ref = refs[:-1], refs[-1]
    values = inputs_ref[...].astype(F32)
    grad = own_ref[...]
    for ref in arrived:
        grad = grad + ref[...].astype(F32)
    grad = grad * gain_ref[0:1, :]
    scale = lax.rsqrt(jnp.mean(values * values, axis=-1, keepdims=True) + EPS)
    unit = values * scale
    part = scale * (grad - unit * jnp.mean(grad * unit, axis=-1, keepdims=True))
    out_ref[...] = (resid_grad_ref[...] + part).astype(BF16)


def body(
    inputs,
    cotangent,
    neighbours,
    empty_rows,
    first_gain,
    query_weight,
    key_weight,
    value_weight,
    gate_weight,
    output_weight,
    second_gain,
    hidden_weight,
    return_weight,
):
    rows, width = inputs.shape[1:]
    n_seq = lax.axis_size("seq")
    length = rows * n_seq
    base = lax.axis_index("seq") * rows
    base_ref = jnp.reshape(base, (1,)).astype(jnp.int32)
    inputs = inputs.reshape(rows, width)
    cotangent = cotangent.reshape(rows, width)
    others = [turned(inputs, shift) for shift in range(1, n_seq)]
    others = jnp.concatenate(others, axis=0) if n_seq > 2 else others[0]

    gain_rows = lambda gain: jnp.broadcast_to(gain, (8, width))
    heads = lambda w: w.reshape(width, H, HD)
    gate_column = gate_weight.reshape(width, H, 1)
    ask_weight = jnp.concatenate(
        [heads(query_weight), jnp.broadcast_to(gate_column, (width, H, HD))], axis=2
    ).reshape(width, WIDE)
    ask_weight_back = jnp.concatenate(
        [heads(query_weight), jnp.pad(gate_column, ((0, 0), (0, 0), (0, HD - 1)))], axis=2
    ).reshape(width, WIDE)
    memory_weight = jnp.concatenate([heads(key_weight), heads(value_weight)], axis=2).reshape(width, WIDE)
    blend_weight = jnp.pad(output_weight.reshape(H, HD, width), ((0, 0), (HD, 0), (0, 0))).reshape(WIDE, width)
    chunk = own_chunk()
    index = (neighbours.reshape(rows * NEAR) + (length - rows - base)) % length
    open_rows = (1 - empty_rows.reshape(rows, 1)).astype(F32)

    normed, ask, own = project(inputs, gain_rows(first_gain), ask_weight, memory_weight)
    split = SPAN if rows == 2 * SPAN else rows
    attended = ()
    if split < rows:
        attended = local_attention(base_ref, ask, own[:SPAN], own, split, rows)
    others_normed, others_memory = project_memory(others, gain_rows(first_gain), memory_weight, after=attended[:1])
    halo = others_memory[length - rows - SPAN :]
    local_out, log_total = local_attention(base_ref, ask, halo, own, 0, split, attended)
    near, weight, blended = retrieve(index, others_memory, own, ask, local_out, open_rows)

    outputs, resid_grad, blended_grad, second_gain_grad, early_own, early_send = feed_forward(
        chunk, inputs, cotangent, blended, blend_weight, gain_rows(second_gain), hidden_weight, return_weight
    )
    early = scatter_start(early_own, early_send)
    early = scatter_level(early, 1)
    local_grad, inner, partial, far = retrieve_back(
        index, blended_grad, ask, local_out, open_rows, near, weight, length, after=[early[0]]
    )
    early = scatter_level(early, 2, after=[inner])
    steps = list(range(H // HEADS))
    back = functools.partial(
        local_attention_back, base_ref, ask, halo, own, local_grad, log_total, inner, partial, far
    )
    grads = back(steps[: len(steps) // 2], after=[early[0]])
    early_total = scatter_finish(early, after=[grads[0]])
    early = gather_level(early_total, 2)
    ask_grad, memory_grad = back(steps[len(steps) // 2 :], grads, after=[early_total])
    early_total = join_pieces(early, after=[ask_grad])
    early = gather_level(early_total, 1)
    own_grad, others_grad, first_gain_grad = normed_back(
        inputs, others, ask_grad, memory_grad, ask_weight_back, memory_weight, after=[early_total]
    )
    arrived = [turned(others_grad[(k - 1) * rows : k * rows], n_seq - k) for k in range(1, n_seq)]
    own_late, send_late = pack_late(
        chunk, others_normed, normed, ask_grad, memory_grad, first_gain_grad, second_gain_grad, after=[others_grad]
    )
    late = scatter_start(own_late, send_late)
    early_own = join_pieces(early, after=[own_late])
    early_other = swapped(early_own, level_groups()[0][0], 1)
    late = scatter_level(late, 1, after=[early_own])
    input_grad = whole_call(
        input_back_kernel, "input_back", inputs, gain_rows(first_gain), resid_grad, own_grad, *arrived,
        outs=[((rows, width), BF16)], after=[late[0]],
    )[0]
    late = scatter_level(late, 2, after=[input_grad])
    late_total = scatter_finish(late)
    late = gather_level(late_total, 2)
    return_sum, hidden_sum, output_sum = unpack_early(
        chunk, early_own, early_other, return_weight.shape, hidden_weight.shape, after=[late_total]
    )
    late_total = join_pieces(late, after=[return_sum])
    late = gather_level(late_total, 1)
    late_own = join_pieces(late)
    late_other = swapped(late_own, level_groups()[0][0], 1)
    query_sum, key_sum, value_sum, gate_sum, first_sum, second_sum = unpack_late(chunk, late_own, late_other)
    return (
        outputs.reshape(1, rows, width),
        input_grad.reshape(1, rows, width),
        first_sum.reshape(width),
        query_sum,
        key_sum,
        value_sum,
        gate_sum,
        output_sum,
        second_sum.reshape(width),
        hidden_sum,
        return_sum,
    )


def solution(mesh):
    split = P("dp", "seq", None)
    in_specs = (split, split, split, P("dp", "seq")) + (P(),) * 9
    out_specs = (split, split) + (P(),) * 9
    return jax.shard_map(body, mesh=mesh, in_specs=in_specs, out_specs=out_specs, check_vma=False)
```

```python
import functools
import math

import jax
import jax.numpy as jnp
from jax import lax
from jax.experimental import pallas as pl
from jax.experimental.pallas import tpu as pltpu
from jax.sharding import PartitionSpec as P

H = 8
HD = 64
LANES = 2 * HD
WIDE = H * LANES
SPAN = 512
NEAR = 4
SCALE = HD ** (-0.5)
NEG = -1e30
EPS = 1e-06
MIB = 1024 * 1024

F32 = jnp.float32
BF16 = jnp.bfloat16
TOKEN = ((8, LANES), F32)


def dot(left, right):
    return jnp.dot(left, right, preferred_element_type=F32)


def dot_back(left, right):
    return lax.dot_general(left, right, (((1,), (1,)), ((), ())), preferred_element_type=F32)


def rows_dot(left, right):
    return lax.dot_general(left, right, (((0,), (0,)), ((), ())), preferred_element_type=F32)


def cost_of(microseconds):
    return pl.CostEstimate(flops=int(microseconds * 1e9), bytes_accessed=int(microseconds * 3e6), transcendentals=0)


def block_rows(rows):
    return 256 if rows % 256 == 0 else rows


def head_lanes(h):
    return slice(h * LANES, (h + 1) * LANES)


TILE = 256
REACH = SPAN + TILE
HEADS = 2
CHUNKS = 32
EARLY_ROWS = 128
LATE_ROWS = 64
EXTRA_ROWS = 16


def window_parts(first):
    before = max(SPAN - first, 0)
    parts = [(True, SPAN - before, before)] if before else []
    return parts + [(False, max(first - SPAN, 0), REACH - before)]


def window_keys(halo_ref, own_ref, first, lanes):
    return [(halo_ref if halo else own_ref)[at : at + n, lanes] for halo, at, n in window_parts(first)]


def window_bias(query_axis):
    shape = (TILE, REACH) if query_axis == 0 else (REACH, TILE)
    query = lax.broadcasted_iota(jnp.int32, shape, query_axis)
    key = lax.broadcasted_iota(jnp.int32, shape, 1 - query_axis)
    return jnp.where((key > query) & (key <= query + SPAN), 0.0, NEG)


def masked(scores, bias, first, base, key_axis):
    cut = lambda v, i, j: v[i:j] if key_axis == 0 else v[:, i:j]
    out = []
    for at in range(0, REACH, TILE):
        part = cut(scores, at, at + TILE)
        if at == 0 or at == SPAN:
            part = part + cut(bias, at, at + TILE)
        if first + at < SPAN:
            part = part + jnp.where(base + first + at >= SPAN, 0.0, NEG)
        out.append(part)
    return jnp.concatenate(out, axis=key_axis)


def pipelined(work, before, middle, after):
    ready = before(*work[0])
    held = None
    for k, item in enumerate(work):
        following = before(*work[k + 1]) if k + 1 < len(work) else None
        done = middle(item, ready)
        if held is not None:
            after(*held)
        held, ready = (item, done), following
    after(*held)


def local_kernel(start, base_ref, ask_ref, halo_ref, own_ref, out_ref, total_ref, bias_ref, totals):
    step = pl.program_id(0)
    base = base_ref[0]

    @pl.when(step == 0)
    def fill():
        bias_ref[...] = window_bias(0)

    lane = lax.broadcasted_iota(jnp.int32, (TILE, LANES), 1)

    def scores(at, g):
        query = jnp.where(lane < HD, ask_ref[at : at + TILE, head_lanes(g)], 0.0).astype(BF16)
        return jnp.concatenate([dot_back(query, k) for k in window_keys(halo_ref, own_ref, start + at, head_lanes(g))], axis=1)

    def softmax(item, raw):
        raw = masked(raw, bias_ref, start + item[0], base, 1)
        top = jnp.max(raw, axis=1, keepdims=True)
        expo = jnp.exp(raw - top)
        return expo.astype(BF16), jnp.sum(expo, axis=1, keepdims=True), top

    def finish(item, done):
        at, g = item
        expo, total, top = done
        out, column = None, 0
        for keys in window_keys(halo_ref, own_ref, start + at, head_lanes(g)):
            term = dot(expo[:, column : column + keys.shape[0]], keys)
            column += keys.shape[0]
            out = term if out is None else out + term
        here = slice(at, at + TILE)
        out_ref[here, head_lanes(g)] = (out * (1.0 / total)).astype(BF16)
        totals[here, :] = jnp.where(lane == step * HEADS + g, top + jnp.log(total), totals[here, :])

    pipelined([(at, g) for g in range(HEADS) for at in range(0, ask_ref.shape[0], TILE)], scores, softmax, finish)

    @pl.when(step == H // HEADS - 1)
    def turn():
        for at in range(0, ask_ref.shape[0], LANES):
            total_ref[:, at : at + LANES] = totals[at : at + LANES, :].T[:H, :]


def halo_of(others_memory):
    far = others_memory.shape[0]
    if far % SPAN:
        return others_memory[far - SPAN :], 0
    return others_memory, far // SPAN - 1


def local_attention(base, ask, halo, own, start, stop, earlier=(), after=()):
    rows = ask.shape[0]
    count = stop - start
    wide = HEADS * LANES
    part = lambda h: (start // count, h)
    held = [pl.BlockSpec(memory_space=pl.ANY)] * (len(earlier) + len(after))
    return pl.pallas_call(
        lambda *refs: local_kernel(start, *refs[:4], *refs[4 + len(held) :]),
        grid=(H // HEADS,),
        in_specs=[
            pl.BlockSpec(memory_space=pltpu.SMEM),
            pl.BlockSpec((count, wide), part),
            pl.BlockSpec((SPAN, wide), lambda h: (halo[1], h)),
            pl.BlockSpec((rows, wide), lambda h: (0, h)),
        ]
        + held,
        out_specs=[pl.BlockSpec((count, wide), part), pl.BlockSpec((H, count), lambda h: (0, start // count))],
        out_shape=[pltpu.HBM((rows, WIDE), BF16), pltpu.HBM((H, rows), F32)],
        scratch_shapes=[pltpu.VMEM((TILE, REACH), F32), pltpu.VMEM((count, LANES), F32)],
        input_output_aliases={4 + k: k for k in range(len(earlier))},
        compiler_params=pltpu.CompilerParams(vmem_limit_bytes=12 * MIB),
        cost_estimate=cost_of(count / 80),
        name="local_attention",
    )(base, *in_hbm(ask, halo[0], own, *earlier), *after)


def local_back_kernel(
    first_step, base_ref, ask_ref, halo_ref, own_ref, grad_ref, total_ref, inner_ref, partial_ref, far_grad_ref,
    ask_grad_ref, memory_grad_ref, sums_ref, bias_ref,
):
    step = pl.program_id(0) + first_step
    rows = ask_ref.shape[0]
    base = base_ref[0]
    start = far_grad_ref.shape[0] - rows - SPAN

    @pl.when(step == first_step)
    def fill():
        bias_ref[...] = window_bias(1)

    left = left_lanes(TILE)
    sums_ref[...] = far_grad_ref[...].astype(F32)

    def query_of(first, g):
        return jnp.where(left, ask_ref[first : first + TILE, head_lanes(g)], 0.0).astype(BF16)

    def products(first, g):
        keys = window_keys(halo_ref, own_ref, first, head_lanes(g))
        query, grad = query_of(first, g), grad_ref[first : first + TILE, head_lanes(g)]
        join = lambda rows: jnp.concatenate([dot_back(k, rows) for k in keys], axis=0)
        return join(query), join(grad)

    def score_grads(item, done):
        first, g = item
        scores, prob_grad = done
        here = slice(first, first + TILE)
        total = total_ref[pl.ds(step * HEADS + g, 1), here]
        inner = inner_ref[pl.ds(step * HEADS + g, 1), here]
        probs = jnp.exp(masked(scores, bias_ref, first, base, 0) - total)
        return (probs * (prob_grad - inner)).astype(BF16), probs.astype(BF16)

    def finish(item, done):
        first, g = item
        score_grad, probs = done
        here, lanes = slice(first, first + TILE), head_lanes(g)
        query_grad, row = None, 0
        for keys in window_keys(halo_ref, own_ref, first, lanes):
            term = rows_dot(score_grad[row : row + keys.shape[0]], keys)
            row += keys.shape[0]
            query_grad = term if query_grad is None else query_grad + term
        sums_ref[start + first : start + first + REACH, lanes] += dot(score_grad, query_of(first, g)) + dot(
            probs, grad_ref[here, lanes]
        )
        partial = partial_ref[here, lanes].astype(F32)
        ask_grad_ref[here, lanes] = (partial + jnp.where(left, query_grad * SCALE, 0.0)).astype(BF16)

    pipelined([(first, g) for g in range(HEADS) for first in range(0, rows, TILE)], products, score_grads, finish)
    memory_grad_ref[...] = sums_ref[...].astype(BF16)


def local_attention_back(base, ask, halo, own, grad, total, inner, partial, far_grad, steps, earlier=(), after=()):
    rows = ask.shape[0]
    length = far_grad.shape[0]
    first = steps[0]
    head = lambda n: pl.BlockSpec((n, HEADS * LANES), lambda h: (0, h + first))
    flat = pl.BlockSpec((H, rows), lambda h: (0, 0))
    held = [pl.BlockSpec(memory_space=pl.ANY)] * (len(earlier) + len(after))
    return pl.pallas_call(
        lambda *refs: local_back_kernel(first, *refs[:9], *refs[9 + len(held) :]),
        grid=(len(steps),),
        in_specs=[
            pl.BlockSpec(memory_space=pltpu.SMEM),
            head(rows),
            pl.BlockSpec((SPAN, HEADS * LANES), lambda h: (halo[1], h + first)),
            head(rows),
            head(rows),
            flat,
            flat,
            head(rows),
            head(length),
        ]
        + held,
        out_specs=[head(rows), head(length)],
        out_shape=[
            pltpu.HBM((rows, WIDE), BF16),
            pltpu.HBM((length, WIDE), BF16),
        ],
        scratch_shapes=[pltpu.VMEM((length, HEADS * LANES), F32), pltpu.VMEM((REACH, TILE), F32)],
        input_output_aliases={9 + k: k for k in range(len(earlier))},
        compiler_params=pltpu.CompilerParams(vmem_limit_bytes=20 * MIB),
        cost_estimate=cost_of(0.3),
        name="local_attention_back",
    )(base, *in_hbm(ask, halo[0], own, grad, total, inner, partial, far_grad, *earlier), *after)


def token_tile(ref, token):
    return ref[pl.ds(pl.multiple_of(token * H, H), H), :]


def put_heads(ref, h, values):
    ref[pl.ds(h, values.shape[0], stride=H), :] = values


def take_heads(ref, h, count):
    return ref[pl.ds(h, count, stride=H), :]


def left_lanes(count):
    return lax.broadcasted_iota(jnp.int32, (count, LANES), 1) < HD


def build_table(table, others_ref, own_ref):
    base = 0
    for ref in (others_ref, own_ref):
        for at in range(0, ref.shape[0], 256):
            for h in range(H):
                table[pl.ds((base + at) * H + h, 256, stride=H), :] = ref[at : at + 256, head_lanes(h)].astype(F32)
        base += ref.shape[0]


def row_sums(values):
    return jnp.sum(values, axis=1, keepdims=True)


def softmax_over(match):
    top = functools.reduce(jnp.maximum, match)
    expo = [jnp.exp(m - top) for m in match]
    scale = 1.0 / functools.reduce(jnp.add, expo)
    return [e * scale for e in expo]


TOKENS = 128
GROUP = 16


def lane_sums(values):
    return dot(values.astype(BF16), jnp.ones((LANES, LANES), BF16))


def gather_group(index_ref, table, near_rows, first, group):
    for k in range(GROUP):
        t = group * GROUP + k
        for j in range(NEAR):
            near_rows[j, t * H : (t + 1) * H, :] = token_tile(table, index_ref[(first + t) * NEAR + j])


def scatter_group(index_ref, sums, terms, first, group):
    for k in range(GROUP):
        t = group * GROUP + k
        for j in range(NEAR):
            there = pl.ds(pl.multiple_of(index_ref[(first + t) * NEAR + j] * H, H), H)
            held = sums[j % len(sums)]
            held[there, :] = held[there, :] + terms[j, t * H : (t + 1) * H, :]


def retrieve_kernel(
    index_ref, others_ref, own_ref, ask_ref, local_ref, open_ref, near_ref, weight_ref, blended_ref,
    table, ask_rows, out_rows, near_rows,
):
    step = pl.program_id(0)
    count = ask_ref.shape[0]
    first = step * count

    @pl.when(step == 0)
    def build():
        build_table(table, others_ref, own_ref)

    for h in range(H):
        put_heads(ask_rows, h, ask_ref[:, head_lanes(h)].astype(F32))
    left = left_lanes(GROUP * H)
    groups = count // GROUP
    gather_group(index_ref, table, near_rows, first, 0)
    for group in range(groups):
        if group + 1 < groups:
            gather_group(index_ref, table, near_rows, first, group + 1)
        here = slice(group * GROUP * H, (group + 1) * GROUP * H)
        query = jnp.where(left, ask_rows[here, :], 0.0)
        weight = softmax_over([lane_sums(near_rows[j, here, :] * query) for j in range(NEAR)])
        out_rows[here, :] = functools.reduce(jnp.add, [weight[j] * near_rows[j, here, :] for j in range(NEAR)])
        for j in range(NEAR):
            weight_ref[j, here, :] = weight[j].astype(BF16)
            near_ref[j, here, :] = near_rows[j, here, :].astype(BF16)
    open_rows = open_ref[...]
    left = left_lanes(count)
    for h in range(H):
        lanes = head_lanes(h)
        local = local_ref[:, lanes].astype(F32)
        mix = (1.0 - jax.nn.sigmoid(ask_ref[:, lanes].astype(F32))) * open_rows
        blended = local + mix * (take_heads(out_rows, h, count) - local)
        blended_ref[:, lanes] = jnp.where(left, 0.0, blended).astype(BF16)


def retrieve(index, others, own, ask, local, open_rows):
    rows = ask.shape[0]
    length = others.shape[0] + rows
    count = min(TOKENS, rows)
    wide = pl.BlockSpec((count, WIDE), lambda c: (c, 0))
    tall = pl.BlockSpec((NEAR, count * H, LANES), lambda c: (0, c, 0))
    return pl.pallas_call(
        retrieve_kernel,
        grid=(rows // count,),
        in_specs=[
            pl.BlockSpec(memory_space=pltpu.SMEM),
            pl.BlockSpec((length - rows, WIDE), lambda c: (0, 0)),
            pl.BlockSpec((rows, WIDE), lambda c: (0, 0)),
            wide,
            wide,
            pl.BlockSpec((count, 1), lambda c: (c, 0)),
        ],
        out_specs=[tall, tall, wide],
        out_shape=[
            pltpu.HBM((NEAR, rows * H, LANES), BF16),
            pltpu.HBM((NEAR, rows * H, LANES), BF16),
            jax.ShapeDtypeStruct((rows, WIDE), BF16),
        ],
        scratch_shapes=[
            pltpu.VMEM((length * H, LANES), F32),
            pltpu.VMEM((count * H, LANES), F32),
            pltpu.VMEM((count * H, LANES), F32),
            pltpu.VMEM((NEAR, count * H, LANES), F32),
        ],
        compiler_params=pltpu.CompilerParams(vmem_limit_bytes=28 * MIB),
        cost_estimate=cost_of(12),
        name="retrieve",
    )(index, *in_hbm(others, own, ask, local), open_rows)


def retrieve_back_kernel(
    index_ref, grad_ref, ask_ref, local_ref, open_ref, near_ref, weight_ref,
    local_grad_ref, inner_ref, partial_ref, far_ref,
    sums_even, sums_odd, ask_rows, grad_rows, out_rows, mixed, terms,
):
    step = pl.program_id(0)
    count = ask_ref.shape[0]
    first = step * count
    length = far_ref.shape[0]

    @pl.when(step == 0)
    def clear():
        sums_even[...] = jnp.zeros_like(sums_even)
        sums_odd[...] = jnp.zeros_like(sums_odd)

    open_rows = open_ref[...]
    left = left_lanes(count)
    lane = lax.broadcasted_iota(jnp.int32, (count, LANES), 1)
    inner_all = jnp.zeros((count, LANES), F32)
    for h in range(H):
        lanes = head_lanes(h)
        grad = grad_ref[:, lanes].astype(F32)
        ask = ask_ref[:, lanes].astype(F32)
        mix = (1.0 - jax.nn.sigmoid(ask)) * open_rows
        inner = row_sums(grad * local_ref[:, lanes].astype(F32))
        inner_all = jnp.where(lane == HD + h, inner - mix * inner, inner_all)
        mixed[:, lanes] = mix * inner
        local_grad_ref[:, lanes] = (grad - mix * grad).astype(BF16)
        put_heads(ask_rows, h, jnp.where(left, ask, mix))
        put_heads(grad_rows, h, grad)
    inner_ref[...] = inner_all.T[HD : HD + H, :]
    groups = count // GROUP
    left_tile = left_lanes(GROUP * H)
    sums = (sums_even, sums_odd)
    for group in range(groups):
        here = slice(group * GROUP * H, (group + 1) * GROUP * H)
        ask = ask_rows[here, :]
        grad = ask * grad_rows[here, :]
        source = jnp.where(left_tile, ask, grad)
        near = [near_ref[j, here, :].astype(F32) for j in range(NEAR)]
        weight_grad = [lane_sums(n * grad) for n in near]
        weight = [weight_ref[j, here, :].astype(F32) for j in range(NEAR)]
        inner = functools.reduce(jnp.add, [w * g for w, g in zip(weight, weight_grad)])
        match_grad = [w * (g - inner) for w, g in zip(weight, weight_grad)]
        query_grad = functools.reduce(jnp.add, [g * n for g, n in zip(match_grad, near)])
        out_rows[here, :] = jnp.where(left_tile, query_grad * SCALE, inner)
        for j in range(NEAR):
            terms[j, here, :] = jnp.where(left_tile, match_grad[j], weight[j]) * source
        if group:
            scatter_group(index_ref, sums, terms, first, group - 1)
    scatter_group(index_ref, sums, terms, first, groups - 1)
    for h in range(H):
        lanes = head_lanes(h)
        tile = take_heads(out_rows, h, count)
        gate = jax.nn.sigmoid(ask_ref[:, lanes].astype(F32))
        partial_ref[:, lanes] = jnp.where(left, tile, (gate / HD) * (mixed[:, lanes] - tile)).astype(BF16)

    @pl.when(step == pl.num_programs(0) - 1)
    def finish():
        for at in range(0, length, 256):
            for h in range(H):
                there = pl.ds(at * H + h, 256, stride=H)
                far_ref[at : at + 256, head_lanes(h)] = (sums_even[there, :] + sums_odd[there, :]).astype(BF16)


def retrieve_back(index, grad, ask, local, open_rows, near, weight, length, after=()):
    rows = ask.shape[0]
    count = min(TOKENS, rows)
    wide = pl.BlockSpec((count, WIDE), lambda c: (c, 0))
    tall = pl.BlockSpec((NEAR, count * H, LANES), lambda c: (0, c, 0))
    return pl.pallas_call(
        lambda *refs: retrieve_back_kernel(*refs[:7], *refs[7 + len(after) :]),
        grid=(rows // count,),
        in_specs=[
            pl.BlockSpec(memory_space=pltpu.SMEM),
            wide,
            wide,
            wide,
            pl.BlockSpec((count, 1), lambda c: (c, 0)),
            tall,
            tall,
        ]
        + [pl.BlockSpec(memory_space=pl.ANY)] * len(after),
        out_specs=[
            wide,
            pl.BlockSpec((H, count), lambda c: (0, c)),
            wide,
            pl.BlockSpec((length, WIDE), lambda c: (0, 0)),
        ],
        out_shape=[
            pltpu.HBM((rows, WIDE), BF16),
            pltpu.HBM((H, rows), F32),
            pltpu.HBM((rows, WIDE), BF16),
            pltpu.HBM((length, WIDE), BF16),
        ],
        scratch_shapes=[
            pltpu.VMEM((length * H, LANES), F32),
            pltpu.VMEM((length * H, LANES), F32),
            pltpu.VMEM((count * H, LANES), F32),
            pltpu.VMEM((count * H, LANES), F32),
            pltpu.VMEM((count * H, LANES), F32),
            pltpu.VMEM((count, WIDE), F32),
            pltpu.VMEM((NEAR, count * H, LANES), F32),
        ],
        compiler_params=pltpu.CompilerParams(vmem_limit_bytes=40 * MIB),
        cost_estimate=cost_of(24),
        name="retrieve_back",
    )(index, *in_vmem(grad), *in_hbm(ask, local), open_rows, *in_hbm(near, weight), *after)


def turned(block, shift):
    size = lax.axis_size("seq")
    return lax.ppermute(block, "seq", [((i + shift) % size, i) for i in range(size)])


def index_bits(axis):
    return [(axis, b) for b in range(lax.axis_size(axis).bit_length() - 1)]


def level_groups():
    dp, seq = index_bits("dp"), index_bits("seq")
    return [dp[:1], dp[1:3], seq[:1] + dp[3:4]], dp[4:] + seq[1:]


def own_place(group):
    place = 0
    for k, (axis, bit) in enumerate(group):
        place = place + (((lax.axis_index(axis) >> bit) & 1) << k)
    return place


def own_chunk():
    chunk = 0
    for group in level_groups()[0]:
        chunk = (chunk << len(group)) + own_place(group)
    return jnp.reshape(chunk, (1,)).astype(jnp.int32)


def swapped(block, group, distance):
    flips = {"dp": 0, "seq": 0}
    for k, (axis, bit) in enumerate(group):
        if (distance >> k) & 1:
            flips[axis] |= 1 << bit
    n_dp, n_seq = lax.axis_size("dp"), lax.axis_size("seq")
    if not flips["seq"]:
        return lax.ppermute(block, "dp", [(i, i ^ flips["dp"]) for i in range(n_dp)])
    if not flips["dp"]:
        return lax.ppermute(block, "seq", [(i, i ^ flips["seq"]) for i in range(n_seq)])
    route = [(i, (i // n_seq ^ flips["dp"]) * n_seq + (i % n_seq ^ flips["seq"])) for i in range(n_dp * n_seq)]
    return lax.ppermute(block, ("dp", "seq"), route)


def in_hbm(*arrays):
    return [pltpu.with_memory_space_constraint(v, pltpu.HBM) for v in arrays]


def in_vmem(*arrays):
    return [pltpu.with_memory_space_constraint(v, pltpu.VMEM) for v in arrays]


def whole_call(kernel, name, *operands, outs, scratch=(), after=(), cost=0.3, spare=4, resident=(), streamed=(), inside=(), after_far=()):
    count, late = len(operands), len(streamed)
    operands = [in_hbm(v)[0] if k in streamed else v for k, v in enumerate(operands)]
    operands = [in_vmem(v)[0] if k in inside else v for k, v in enumerate(operands)]

    def place(k, v):
        if v.dtype == jnp.int32:
            return pltpu.SMEM
        return pltpu.HBM if k in streamed else pltpu.VMEM

    held = [pltpu.VMEM(operands[k].shape, operands[k].dtype) for k in streamed]
    shapes = [(v.shape, v.dtype) for k, v in enumerate(operands) if k not in inside]
    shapes += [(v.shape, v.dtype) for v in scratch]
    shapes += [out for k, out in enumerate(outs) if k not in resident]
    size = sum(math.prod(shape) * jnp.dtype(dtype).itemsize for shape, dtype in shapes)

    def wrapped(*refs):
        ins, rest = list(refs[:count]), refs[count + len(after) + len(after_far) :]
        if not late:
            return kernel(*ins, *rest)
        rest, copies = rest[: -2 * late], {}
        for n, k in enumerate(streamed):
            held_ref, sem = refs[-2 * late + n], refs[-late + n]
            copies[k] = pltpu.make_async_copy(ins[k], held_ref, sem)
            copies[k].start()
            ins[k] = held_ref
        return kernel(lambda k: copies[k].wait(), *ins, *rest)

    return pl.pallas_call(
        wrapped,
        in_specs=[pl.BlockSpec(memory_space=place(k, v)) for k, v in enumerate(operands)]
        + [pl.BlockSpec(memory_space=pl.ANY)] * len(after)
        + [pl.BlockSpec(memory_space=pltpu.HBM)] * len(after_far),
        out_specs=[pl.BlockSpec(memory_space=pltpu.VMEM)] * len(outs),
        out_shape=[
            pltpu.VMEM(shape, dtype) if k in resident else jax.ShapeDtypeStruct(shape, dtype)
            for k, (shape, dtype) in enumerate(outs)
        ],
        scratch_shapes=list(scratch) + held + [pltpu.SemaphoreType.DMA(())] * late,
        compiler_params=pltpu.CompilerParams(vmem_limit_bytes=size + spare * MIB),
        cost_estimate=cost_of(cost),
        name=name,
    )(*operands, *after, *in_hbm(*after_far))


def add_pieces(own, arrived, pieces, extra=0, **order):
    rows, width = own.shape
    count = (rows - extra) // pieces

    def kernel(*refs):
        terms, outs = refs[: 1 + len(arrived)], refs[1 + len(arrived) :]

        def total(here):
            values = terms[0][here, :].astype(F32)
            for term in terms[1:]:
                values = values + term[here, :].astype(F32)
            return values.astype(BF16)

        for k, out in enumerate(outs):
            out[:count, :] = total(slice(k * count, (k + 1) * count))
        if extra:
            last = total(slice(rows - extra, rows))
            for out in outs:
                out[count:, :] = last

    outs = [((count + extra, width), BF16)] * pieces
    return whole_call(kernel, "add_pieces", own, *arrived, outs=outs, **order)


def join_pieces(pieces, **order):
    count, width = pieces[0].shape

    def kernel(*refs):
        for k, ref in enumerate(refs[:-1]):
            refs[-1][k * count : (k + 1) * count, :] = ref[...]

    return whole_call(kernel, "join_pieces", *pieces, outs=[((count * len(pieces), width), BF16)], **order)[0]


def scatter_start(own, send):
    return own, [swapped(send, level_groups()[0][0], 1)]


def scatter_level(held, level, extra=0, **order):
    own, arrived = held
    group = level_groups()[0][level]
    pieces = add_pieces(own, arrived, 2 ** len(group), extra, **order)
    return pieces[0], [swapped(piece, group, d) for d, piece in enumerate(pieces) if d]


def scatter_finish(held, **order):
    total = add_pieces(*held, 1, **order)[0]
    for bit in level_groups()[1]:
        total = add_pieces(total, [swapped(total, [bit], 1)], 1)[0]
    return total


def gather_level(total, level):
    group = level_groups()[0][level]
    return [total] + [swapped(total, group, d) for d in range(1, 2 ** len(group))]


def rms_unit(values):
    scale = lax.rsqrt(jnp.mean(values * values, axis=-1, keepdims=True) + EPS)
    return values * scale, scale


def rms_back(unit, scale, grad):
    return scale * (grad - unit * jnp.mean(grad * unit, axis=-1, keepdims=True))


def lay_weights_kernel(wait, query_ref, key_ref, value_ref, gate_ref, output_ref, ask_ref, memory_ref, blend_ref):
    width = query_ref.shape[0]
    gate = gate_ref[...].astype(F32)
    for k in (0, 1, 2, 4):
        wait(k)
    for h in range(H):
        here = slice(h * HD, (h + 1) * HD)
        column = jnp.broadcast_to(gate[:, h : h + 1], (width, HD)).astype(BF16)
        ask_ref[:, head_lanes(h)] = jnp.concatenate([query_ref[:, here], column], axis=1)
        memory_ref[:, head_lanes(h)] = jnp.concatenate([key_ref[:, here], value_ref[:, here]], axis=1)
        blend_ref[h * LANES : h * LANES + HD, :] = jnp.zeros((HD, width), BF16)
        blend_ref[h * LANES + HD : (h + 1) * LANES, :] = output_ref[here, :]


def lay_weights(query_weight, key_weight, value_weight, gate_weight, output_weight):
    width = query_weight.shape[0]
    wide = ((width, WIDE), BF16)
    return whole_call(
        lay_weights_kernel,
        "lay_weights",
        query_weight,
        key_weight,
        value_weight,
        gate_weight,
        output_weight,
        outs=[wide, wide, ((WIDE, width), BF16)],
        streamed=(0, 1, 2, 4),
    )


def project_kernel(inputs_ref, gain_ref, ask_weight_ref, memory_weight_ref, normed_ref, ask_ref, memory_ref):
    normed = (rms_unit(inputs_ref[...].astype(F32))[0] * gain_ref[0:1, :]).astype(BF16)
    normed_ref[...] = normed
    memory_ref[...] = dot(normed, memory_weight_ref[...]).astype(BF16)
    if ask_ref is not None:
        left = (lax.broadcasted_iota(jnp.int32, (1, WIDE), 1) % LANES) < HD
        ask = dot(normed, ask_weight_ref[...])
        ask_ref[...] = jnp.where(left, ask * SCALE, ask).astype(BF16)


def row_blocks_call(kernel, name, *operands, outs, cost):
    rows = operands[0].shape[0]
    block = block_rows(rows)
    rows_spec = lambda width: pl.BlockSpec((block, width), lambda k: (k, 0))
    whole = lambda v: pl.BlockSpec(v.shape, lambda k: (0, 0))
    return pl.pallas_call(
        kernel,
        grid=(rows // block,),
        in_specs=[rows_spec(operands[0].shape[1])] + [whole(v) for v in operands[1:]],
        out_specs=[rows_spec(width) for width in outs],
        out_shape=[pltpu.HBM((rows, width), BF16) for width in outs],
        compiler_params=pltpu.CompilerParams(vmem_limit_bytes=14 * MIB),
        cost_estimate=cost_of(cost),
        name=name,
    )(*operands)


def project(inputs, gain, ask_weight, memory_weight):
    width = inputs.shape[1]
    return row_blocks_call(
        project_kernel, "project", inputs, gain, ask_weight, memory_weight, outs=[width, WIDE, WIDE], cost=3
    )


def project_memory(inputs, gain, memory_weight):
    def kernel(inputs_ref, gain_ref, weight_ref, normed_ref, memory_ref):
        project_kernel(inputs_ref, gain_ref, None, weight_ref, normed_ref, None, memory_ref)

    return row_blocks_call(
        kernel, "project_memory", inputs, gain, memory_weight, outs=[inputs.shape[1], WIDE], cost=2
    )


ROOT = 0.7978845608028654
CUBE = 0.044715


def gelu_and_slope(x):
    square = x * x
    tanh = jnp.tanh(ROOT * (x * (1.0 + CUBE * square)))
    half = 0.5 * (1.0 + tanh)
    slope = half + (0.5 * ROOT) * x * (1.0 - tanh * tanh) * (1.0 + (3.0 * CUBE) * square)
    return x * half, slope


def hidden_kernel(
    wait, chunk_ref, inputs_ref, cotangent_ref, blended_ref, blend_weight_ref, gain_ref, hidden_weight_ref, return_weight_ref,
    resid_ref, active, hidden_grad, own_ref, send_ref,
    normed, return_sums, hidden_sums,
):
    rows, width = inputs_ref.shape
    hidden = hidden_weight_ref.shape[1]
    block = block_rows(rows)
    gain = gain_ref[0:1, :]
    columns = [slice(at, at + width) for at in range(0, hidden, width)]
    wait(1)

    def row_block(k, carry):
        here = pl.ds(pl.multiple_of(k * block, block), block)
        resid = inputs_ref[here, :].astype(F32) + dot(blended_ref[here, :], blend_weight_ref[...])
        resid_ref[here, :] = resid
        normed_here = (rms_unit(resid)[0] * gain).astype(BF16)
        normed[here, :] = normed_here

        @pl.when(k == 0)
        def weights():
            for n in (2, 6, 7):
                wait(n)

        cotangent = cotangent_ref[here, :]

        def products(lanes):
            return dot(normed_here, hidden_weight_ref[:, lanes]), dot_back(cotangent, return_weight_ref[lanes, :])

        def activate(item, done):
            value, slope = gelu_and_slope(done[0])
            return value.astype(BF16), (done[1] * slope).astype(BF16)

        def keep(item, done):
            active[here, item[0]] = done[0]
            hidden_grad[here, item[0]] = done[1]

        pipelined([(lanes,) for lanes in columns], products, activate, keep)
        return carry

    lax.fori_loop(0, rows // block, row_block, 0)

    def column_block(k, carry):
        lanes = pl.ds(pl.multiple_of(k * width, width), width)
        return_sums[lanes, :] = rows_dot(active[:, lanes], cotangent_ref[...]).astype(BF16)
        hidden_sums[:, lanes] = rows_dot(normed[...], hidden_grad[:, lanes]).astype(BF16)
        return carry

    lax.fori_loop(0, hidden // width, column_block, 0)
    tall, flat = hidden // CHUNKS, width // CHUNKS

    def pack(r, carry):
        for half, out in enumerate((own_ref, send_ref)):
            chunk = chunk_ref[0] ^ (r + half * (CHUNKS // 2))
            rows_at = lambda offset, count: pl.ds(pl.multiple_of(r * EARLY_ROWS + offset, flat), count)
            out[rows_at(0, tall), :] = return_sums[pl.ds(pl.multiple_of(chunk * tall, tall), tall), :]
            for c in range(hidden // width):
                out[rows_at(tall + c * flat, flat), :] = hidden_sums[
                    pl.ds(pl.multiple_of(chunk * flat, flat), flat), c * width : (c + 1) * width
                ]
        return carry

    lax.fori_loop(0, CHUNKS // 2, pack, 0)


def hidden_layer(chunk, inputs, cotangent, blended, blend_weight, gain, hidden_weight, return_weight):
    rows, width = inputs.shape
    hidden = hidden_weight.shape[1]
    half = ((CHUNKS // 2 * EARLY_ROWS, width), BF16)
    return whole_call(
        hidden_kernel,
        "hidden_layer",
        chunk,
        inputs,
        cotangent,
        blended,
        blend_weight,
        gain,
        hidden_weight,
        return_weight,
        outs=[((rows, width), F32), ((rows, hidden), BF16), ((rows, hidden), BF16), half, half],
        scratch=[
            pltpu.VMEM((rows, width), BF16),
            pltpu.VMEM((hidden, width), BF16),
            pltpu.VMEM((width, hidden), BF16),
        ],
        cost=20,
        spare=12,
        resident=(0, 1, 2),
        streamed=(1, 6, 2, 7),
    )


def resid_kernel(
    wait, resid_ref, cotangent_ref, blended_ref, active, hidden_grad, blend_weight_ref, gain_ref, hidden_weight_ref, return_weight_ref,
    outputs_ref, resid_grad_ref, blended_grad_ref, gain_grad_ref, blend_sums_ref,
    resid_grad_b,
):
    rows, width = resid_ref.shape
    block = block_rows(rows)
    gain = gain_ref[0:1, :]
    wait(7)

    def row_block(k, gain_grad):
        here = pl.ds(pl.multiple_of(k * block, block), block)
        resid = resid_ref[here, :]
        unit, scale = rms_unit(resid)
        grad = dot_back(hidden_grad[here, :], hidden_weight_ref[...])

        @pl.when(k == 0)
        def weights():
            wait(8)
            wait(1)

        outputs_ref[here, :] = (resid + dot(active[here, :], return_weight_ref[...])).astype(BF16)
        total = cotangent_ref[here, :].astype(F32) + rms_back(unit, scale, grad * gain)
        resid_grad_ref[here, :] = total
        resid_grad_b[here, :] = total.astype(BF16)
        blended_grad_ref[here, :] = dot_back(total.astype(BF16), blend_weight_ref[...]).astype(BF16)
        return gain_grad + jnp.sum(grad * unit, axis=0, keepdims=True)

    gain_grad = lax.fori_loop(0, rows // block, row_block, jnp.zeros((1, width), F32))
    gain_grad_ref[...] = jnp.broadcast_to(gain_grad, gain_grad_ref.shape)
    blend_sums_ref[...] = rows_dot(blended_ref[...], resid_grad_b[...]).astype(BF16)


def resid_layer(resid, cotangent, blended, active, hidden_grad, blend_weight, gain, hidden_weight, return_weight, after=()):
    rows, width = resid.shape
    return whole_call(
        resid_kernel,
        "resid_layer",
        resid,
        cotangent,
        blended,
        active,
        hidden_grad,
        blend_weight,
        gain,
        hidden_weight,
        return_weight,
        outs=[
            ((rows, width), BF16),
            ((rows, width), F32),
            ((rows, WIDE), BF16),
            ((8, width), F32),
            ((WIDE, width), BF16),
        ],
        scratch=[pltpu.VMEM((rows, width), BF16)],
        after=after,
        cost=8,
        spare=6,
        streamed=(7, 8, 1),
        inside=(0, 3, 4),
        resident=(2,),
    )


def unpack_early_kernel(chunk_ref, own_ref, other_ref, return_ref, hidden_ref, token_ref):
    token_ref[...] = jnp.zeros_like(token_ref)
    width = return_ref.shape[1]
    tall, flat = return_ref.shape[0] // CHUNKS, hidden_ref.shape[0] // CHUNKS
    for r in range(CHUNKS):
        chunk = chunk_ref[0] ^ r
        source = own_ref if r < CHUNKS // 2 else other_ref
        at = (r % (CHUNKS // 2)) * EARLY_ROWS
        return_ref[pl.ds(pl.multiple_of(chunk * tall, tall), tall), :] = source[at : at + tall, :].astype(F32)
        at += tall
        there = pl.ds(pl.multiple_of(chunk * flat, flat), flat)
        for c in range(hidden_ref.shape[1] // width):
            hidden_ref[there, c * width : (c + 1) * width] = source[at : at + flat, :].astype(F32)
            at += flat


def unpack_early(chunk, own, other, return_shape, hidden_shape, after=()):
    outs = [(return_shape, F32), (hidden_shape, F32), TOKEN]
    return whole_call(unpack_early_kernel, "unpack_early", chunk, own, other, outs=outs, after=after)


def late_kernel(
    chunk_ref, others_ref, normed_ref, ask_ref, memory_ref, first_ref, second_ref, blend_ref, own_ref, send_ref, ask_sums, memory_sums
):
    width = normed_ref.shape[1]
    far = others_ref.shape[0]
    flat = width // CHUNKS
    ask_sums[...] = rows_dot(normed_ref[...], ask_ref[...]).astype(BF16)
    memory_sums[...] = (
        rows_dot(others_ref[...], memory_ref[:far, :]) + rows_dot(normed_ref[...], memory_ref[far:, :])
    ).astype(BF16)
    lane = lax.broadcasted_iota(jnp.int32, (width, LANES), 1)
    small = jnp.zeros((width, LANES), F32)
    for h in range(H):
        at = h * LANES + HD
        small = jnp.where(lane == h, HD * ask_sums[:, at : at + 1].astype(F32), small)
    zeros = jnp.zeros((EXTRA_ROWS - H - 2, width), F32)
    extra = jnp.concatenate([small.T[:H, :], first_ref[0:1, :], second_ref[0:1, :], zeros], axis=0).astype(BF16)
    for out in (own_ref, send_ref):
        out[CHUNKS // 2 * LATE_ROWS :, :] = extra
    for r in range(CHUNKS):
        chunk = chunk_ref[0] ^ r
        out = own_ref if r < CHUNKS // 2 else send_ref
        at = (r % (CHUNKS // 2)) * LATE_ROWS
        here = pl.ds(pl.multiple_of(chunk * flat, flat), flat)
        for pair in range(H // 2):
            lanes = slice(pair * LANES, (pair + 1) * LANES)
            even = slice(2 * pair * LANES, 2 * pair * LANES + HD)
            odd = slice((2 * pair + 1) * LANES, (2 * pair + 1) * LANES + HD)
            out[at : at + flat, lanes] = jnp.concatenate([ask_sums[here, even], ask_sums[here, odd]], axis=1)
        out[at + flat : at + 2 * flat, :] = memory_sums[here, :width]
        out[at + 2 * flat : at + 3 * flat, :] = memory_sums[here, width:]
        row = (chunk // (HD // flat)) * LANES + HD + (chunk % (HD // flat)) * flat
        out[at + 3 * flat : at + 4 * flat, :] = blend_ref[pl.ds(pl.multiple_of(row, flat), flat), :]


def unpack_late_kernel(
    chunk_ref, own_ref, other_ref, extra_ref, query_ref, key_ref, value_ref, output_ref, gate_ref, first_ref, second_ref
):
    width = query_ref.shape[1]
    flat = width // CHUNKS
    for r in range(CHUNKS):
        chunk = chunk_ref[0] ^ r
        source = own_ref if r < CHUNKS // 2 else other_ref
        at = (r % (CHUNKS // 2)) * LATE_ROWS
        there = pl.ds(pl.multiple_of(chunk * flat, flat), flat)
        query_ref[there, :] = source[at : at + flat, :].astype(F32)
        for half in range(2):
            at += flat
            for pair in range(H // 4):
                lanes = slice((half * H // 4 + pair) * LANES, (half * H // 4 + pair + 1) * LANES)
                even = source[at : at + flat, 2 * pair * LANES : (2 * pair + 1) * LANES]
                odd = source[at : at + flat, (2 * pair + 1) * LANES : (2 * pair + 2) * LANES]
                key_ref[there, lanes] = jnp.concatenate([even[:, :HD], odd[:, :HD]], axis=1).astype(F32)
                value_ref[there, lanes] = jnp.concatenate([even[:, HD:], odd[:, HD:]], axis=1).astype(F32)
        at += flat
        output_ref[there, :] = source[at : at + flat, :].astype(F32)
    extra = extra_ref[...].astype(F32)
    gate_ref[...] = extra[:H, :]
    first_ref[...] = extra[H : H + 1, :]
    second_ref[...] = extra[H + 1 : H + 2, :]


def pack_late(chunk, others, normed, ask_grad, memory_grad, first_grad, second_grad, blend_grad, after=()):
    width = normed.shape[1]
    half = ((CHUNKS // 2 * LATE_ROWS + EXTRA_ROWS, width), BF16)
    return whole_call(
        late_kernel,
        "late_weight_grads",
        chunk,
        others,
        normed,
        ask_grad,
        memory_grad,
        first_grad,
        second_grad,
        blend_grad,
        outs=[half, half],
        scratch=[pltpu.VMEM((width, WIDE), BF16), pltpu.VMEM((width, WIDE), BF16)],
        after=after,
    )


def unpack_late(chunk, own, other, extra):
    width = own.shape[1]
    square, row = ((width, width), F32), ((1, width), F32)
    return whole_call(
        unpack_late_kernel,
        "unpack_late",
        chunk,
        own,
        other,
        extra,
        outs=[square] * 4 + [((H, width), F32), row, row],
    )


def normed_back_kernel(
    inputs_ref, others_ref, ask_ref, memory_ref, ask_weight_ref, memory_weight_ref, own_grad_ref, others_grad_ref, gain_ref
):
    rows, width = inputs_ref.shape
    length = memory_ref.shape[0]
    block = block_rows(rows)

    def unit(ref, here):
        values = ref[here, :].astype(F32)
        return values * lax.rsqrt(jnp.mean(values * values, axis=-1, keepdims=True) + EPS)

    gain = jnp.zeros((1, width), F32)
    for at in range(0, length - rows, block):
        here = slice(at, at + block)
        grad = dot_back(memory_ref[here, :], memory_weight_ref[...])
        others_grad_ref[here, :] = grad.astype(BF16)
        gain = gain + jnp.sum(grad * unit(others_ref, here), axis=0, keepdims=True)
    for at in range(0, rows, block):
        here = slice(at, at + block)
        there = slice(length - rows + at, length - rows + at + block)
        grad = dot_back(ask_ref[here, :], ask_weight_ref[...]) + dot_back(memory_ref[there, :], memory_weight_ref[...])
        own_grad_ref[here, :] = grad
        gain = gain + jnp.sum(grad * unit(inputs_ref, here), axis=0, keepdims=True)
    gain_ref[...] = jnp.broadcast_to(gain, gain_ref.shape)


def normed_back(inputs, others, ask_grad, memory_grad, ask_weight, memory_weight, after=()):
    rows, width = inputs.shape
    return whole_call(
        normed_back_kernel,
        "normed_back",
        inputs,
        others,
        ask_grad,
        memory_grad,
        ask_weight,
        memory_weight,
        outs=[((rows, width), F32), (others.shape, BF16), ((8, width), F32)],
        after=after,
    )


def input_back_kernel(inputs_ref, gain_ref, resid_grad_ref, own_ref, *refs):
    arrived, out_ref, token_ref = refs[:-2], refs[-2], refs[-1]
    token_ref[...] = jnp.zeros_like(token_ref)
    values = inputs_ref[...].astype(F32)
    grad = own_ref[...]
    for ref in arrived:
        grad = grad + ref[...].astype(F32)
    grad = grad * gain_ref[0:1, :]
    scale = lax.rsqrt(jnp.mean(values * values, axis=-1, keepdims=True) + EPS)
    unit = values * scale
    part = scale * (grad - unit * jnp.mean(grad * unit, axis=-1, keepdims=True))
    out_ref[...] = (resid_grad_ref[...] + part).astype(BF16)


def body(
    inputs,
    cotangent,
    neighbours,
    empty_rows,
    first_gain,
    query_weight,
    key_weight,
    value_weight,
    gate_weight,
    output_weight,
    second_gain,
    hidden_weight,
    return_weight,
):
    rows, width = inputs.shape[1:]
    n_seq = lax.axis_size("seq")
    length = rows * n_seq
    base = lax.axis_index("seq") * rows
    base_ref = jnp.reshape(base, (1,)).astype(jnp.int32)
    inputs = inputs.reshape(rows, width)
    cotangent = cotangent.reshape(rows, width)
    others = [turned(inputs, shift) for shift in range(1, n_seq)]
    others = jnp.concatenate(others, axis=0) if n_seq > 2 else others[0]

    gain_rows = lambda gain: jnp.broadcast_to(gain, (8, width))
    ask_weight, memory_weight, blend_weight = lay_weights(
        query_weight, key_weight, value_weight, gate_weight, output_weight
    )
    chunk = own_chunk()
    index = (neighbours.reshape(rows * NEAR) + (length - rows - base)) % length
    open_rows = (1 - empty_rows.reshape(rows, 1)).astype(F32)

    normed, ask, own = project(inputs, gain_rows(first_gain), ask_weight, memory_weight)
    split = SPAN if rows == 2 * SPAN else rows
    attended = ()
    if split < rows:
        attended = local_attention(base_ref, ask, (own, 0), own, split, rows)
    others_normed, others_memory = project_memory(others, gain_rows(first_gain), memory_weight)
    halo = halo_of(others_memory)
    local_out, log_total = local_attention(base_ref, ask, halo, own, 0, split, attended)
    near, weight, blended = retrieve(index, others_memory, own, ask, local_out, open_rows)

    resid, active, hidden_grad, early_own, early_send = hidden_layer(
        chunk, inputs, cotangent, blended, blend_weight, gain_rows(second_gain), hidden_weight, return_weight
    )
    early = scatter_start(early_own, early_send)
    outputs, resid_grad, blended_grad, second_gain_grad, blend_grad = resid_layer(
        resid, cotangent, blended, active, hidden_grad, blend_weight, gain_rows(second_gain), hidden_weight, return_weight
    )
    early = scatter_level(early, 1, after=[second_gain_grad])
    local_grad, inner, partial, far = retrieve_back(
        index, blended_grad, ask, local_out, open_rows, near, weight, length, after=[early[0]]
    )
    early = scatter_level(early, 2, after_far=[inner])
    steps = list(range(H // HEADS))
    back = functools.partial(
        local_attention_back, base_ref, ask, halo, own, local_grad, log_total, inner, partial, far
    )
    grads = back(steps[:1], after=[early[0]])
    early_total = scatter_finish(early, after_far=[grads[0]])
    early = gather_level(early_total, 2)
    grads = back(steps[1:2], grads, after=[early_total])
    early_total = join_pieces(early, after_far=[grads[0]])
    early = gather_level(early_total, 1)
    ask_grad, memory_grad = back(steps[2:], grads, after=[early_total])
    own_grad, others_grad, first_gain_grad = normed_back(
        inputs, others, ask_grad, memory_grad, ask_weight, memory_weight
    )
    arrived = [turned(others_grad[(k - 1) * rows : k * rows], n_seq - k) for k in range(1, n_seq)]
    own_late, send_late = pack_late(
        chunk, others_normed, normed, ask_grad, memory_grad, first_gain_grad, second_gain_grad, blend_grad,
        after=[],
    )
    late = scatter_start(own_late, send_late)
    early_own = join_pieces(early, after=[own_late])
    early_other = swapped(early_own, level_groups()[0][0], 1)
    late = scatter_level(late, 1, EXTRA_ROWS, after=[early_own])
    late = scatter_level(late, 2, EXTRA_ROWS)
    input_grad, token = whole_call(
        input_back_kernel, "input_back", inputs, gain_rows(first_gain), resid_grad, own_grad, *arrived,
        outs=[((rows, width), BF16), TOKEN], after=[late[0]],
    )
    late_total = scatter_finish(late, after=[token])
    extra = late_total[LATE_ROWS:]
    late_total = late_total[:LATE_ROWS]
    late = gather_level(late_total, 2)
    return_sum, hidden_sum, token = unpack_early(
        chunk, early_own, early_other, return_weight.shape, hidden_weight.shape, after=[late_total]
    )
    late_total = join_pieces(late, after=[token])
    late = gather_level(late_total, 1)
    late_own = join_pieces(late)
    late_other = swapped(late_own, level_groups()[0][0], 1)
    query_sum, key_sum, value_sum, output_sum, gate_sum, first_sum, second_sum = unpack_late(chunk, late_own, late_other, extra)
    return (
        outputs.reshape(1, rows, width),
        input_grad.reshape(1, rows, width),
        first_sum.reshape(width),
        query_sum,
        key_sum,
        value_sum,
        gate_sum.T,
        output_sum,
        second_sum.reshape(width),
        hidden_sum,
        return_sum,
    )


def solution(mesh):
    split = P("dp", "seq", None)
    in_specs = (split, split, split, P("dp", "seq")) + (P(),) * 9
    out_specs = (split, split) + (P(),) * 9
    return jax.shard_map(body, mesh=mesh, in_specs=in_specs, out_specs=out_specs, check_vma=False)
```

```python
import functools
import math

import jax
import jax.numpy as jnp
from jax import lax
from jax.experimental import pallas as pl
from jax.experimental.pallas import tpu as pltpu
from jax.sharding import PartitionSpec as P

H = 8
HD = 64
LANES = 2 * HD
WIDE = H * LANES
SPAN = 512
NEAR = 4
SCALE = HD ** (-0.5)
NEG = -1e30
SHUT = 100.0
EPS = 1e-06
MIB = 1024 * 1024

F32 = jnp.float32
BF16 = jnp.bfloat16
TOKEN = ((8, LANES), F32)


def dot(left, right):
    return jnp.dot(left, right, preferred_element_type=F32)


def dot_back(left, right):
    return lax.dot_general(left, right, (((1,), (1,)), ((), ())), preferred_element_type=F32)


def rows_dot(left, right):
    return lax.dot_general(left, right, (((0,), (0,)), ((), ())), preferred_element_type=F32)


def cost_of(microseconds):
    return pl.CostEstimate(flops=int(microseconds * 1e9), bytes_accessed=int(microseconds * 3e6), transcendentals=0)


def block_rows(rows):
    return 256 if rows % 256 == 0 else rows


def head_lanes(h):
    return slice(h * LANES, (h + 1) * LANES)


TILE = 256
REACH = SPAN + TILE
HEADS = 2
BACK_HEADS = 1
CHUNKS = 32
EARLY_ROWS = 128
LATE_ROWS = 64
EXTRA_ROWS = 16


def window_parts(first):
    before = max(SPAN - first, 0)
    parts = [(True, SPAN - before, before)] if before else []
    return parts + [(False, max(first - SPAN, 0), REACH - before)]


def window_keys(halo_ref, own_ref, first, lanes):
    return [(halo_ref if halo else own_ref)[at : at + n, lanes] for halo, at, n in window_parts(first)]


def window_bias(query_axis):
    shape = (TILE, REACH) if query_axis == 0 else (REACH, TILE)
    query = lax.broadcasted_iota(jnp.int32, shape, query_axis)
    key = lax.broadcasted_iota(jnp.int32, shape, 1 - query_axis)
    return jnp.where((key > query) & (key <= query + SPAN), 0.0, NEG)


def masked(scores, bias, first, base, key_axis):
    cut = lambda v, i, j: v[i:j] if key_axis == 0 else v[:, i:j]
    out = []
    for at in range(0, REACH, TILE):
        part = cut(scores, at, at + TILE)
        if at == 0 or at == SPAN:
            part = part + cut(bias, at, at + TILE)
        if first + at < SPAN:
            part = part + jnp.where(base + first + at >= SPAN, 0.0, NEG)
        out.append(part)
    return jnp.concatenate(out, axis=key_axis)


def pipelined(work, before, middle, after):
    ready = before(*work[0])
    held = None
    for k, item in enumerate(work):
        following = before(*work[k + 1]) if k + 1 < len(work) else None
        done = middle(item, ready)
        if held is not None:
            after(*held)
        held, ready = (item, done), following
    after(*held)


def local_kernel(start, base_ref, ask_ref, halo_ref, own_ref, out_ref, total_ref, bias_ref, totals):
    step = pl.program_id(0)
    base = base_ref[0]

    @pl.when(step == 0)
    def fill():
        bias_ref[...] = window_bias(0)

    lane = lax.broadcasted_iota(jnp.int32, (TILE, LANES), 1)

    def scores(at, g):
        query = jnp.where(lane < HD, ask_ref[at : at + TILE, head_lanes(g)], 0.0).astype(BF16)
        return jnp.concatenate([dot_back(query, k) for k in window_keys(halo_ref, own_ref, start + at, head_lanes(g))], axis=1)

    def softmax(item, raw):
        raw = masked(raw, bias_ref, start + item[0], base, 1)
        top = jnp.max(raw, axis=1, keepdims=True)
        expo = jnp.exp(raw - top)
        return expo.astype(BF16), jnp.sum(expo, axis=1, keepdims=True), top

    def finish(item, done):
        at, g = item
        expo, total, top = done
        out, column = None, 0
        for keys in window_keys(halo_ref, own_ref, start + at, head_lanes(g)):
            term = dot(expo[:, column : column + keys.shape[0]], keys)
            column += keys.shape[0]
            out = term if out is None else out + term
        here = slice(at, at + TILE)
        out_ref[here, head_lanes(g)] = (out * (1.0 / total)).astype(BF16)
        totals[here, :] = jnp.where(lane == step * HEADS + g, top + jnp.log(total), totals[here, :])

    pipelined([(at, g) for g in range(HEADS) for at in range(0, ask_ref.shape[0], TILE)], scores, softmax, finish)

    @pl.when(step == H // HEADS - 1)
    def turn():
        for at in range(0, ask_ref.shape[0], LANES):
            total_ref[:, at : at + LANES] = totals[at : at + LANES, :].T[:H, :]


def local_attention(base, ask, halo, own, start, stop, earlier=(), after=()):
    rows = ask.shape[0]
    count = stop - start
    wide = HEADS * LANES
    part = lambda h: (start // count, h)
    held = [pl.BlockSpec(memory_space=pl.ANY)] * (len(earlier) + len(after))
    return pl.pallas_call(
        lambda *refs: local_kernel(start, *refs[:4], *refs[4 + len(held) :]),
        grid=(H // HEADS,),
        in_specs=[
            pl.BlockSpec(memory_space=pltpu.SMEM),
            pl.BlockSpec((count, wide), part),
            pl.BlockSpec((SPAN, wide), lambda h: (0, h)),
            pl.BlockSpec((rows, wide), lambda h: (0, h)),
        ]
        + held,
        out_specs=[pl.BlockSpec((count, wide), part), pl.BlockSpec((H, count), lambda h: (0, start // count))],
        out_shape=[pltpu.HBM((rows, WIDE), BF16), pltpu.HBM((H, rows), F32)],
        scratch_shapes=[pltpu.VMEM((TILE, REACH), F32), pltpu.VMEM((count, LANES), F32)],
        input_output_aliases={4 + k: k for k in range(len(earlier))},
        compiler_params=pltpu.CompilerParams(vmem_limit_bytes=12 * MIB),
        cost_estimate=cost_of(count / 80),
        name="local_attention",
    )(base, *in_hbm(ask, halo, own, *earlier), *after)


def local_back_kernel(
    first_step, base_ref, ask_ref, halo_ref, own_ref, grad_ref, total_ref, inner_ref, partial_ref, far_grad_ref,
    ask_grad_ref, memory_grad_ref, sums_ref, bias_ref,
):
    step = pl.program_id(0) + first_step
    rows = ask_ref.shape[0]
    base = base_ref[0]
    start = far_grad_ref.shape[0] - rows - SPAN

    @pl.when(step == first_step)
    def fill():
        bias_ref[...] = window_bias(1)

    left = left_lanes(TILE)
    sums_ref[...] = far_grad_ref[...].astype(F32)

    def query_of(first, g):
        return jnp.where(left, ask_ref[first : first + TILE, head_lanes(g)], 0.0).astype(BF16)

    def products(first, g):
        keys = window_keys(halo_ref, own_ref, first, head_lanes(g))
        query, grad = query_of(first, g), grad_ref[first : first + TILE, head_lanes(g)]
        join = lambda rows: jnp.concatenate([dot_back(k, rows) for k in keys], axis=0)
        return join(query), join(grad)

    def score_grads(item, done):
        first, g = item
        scores, prob_grad = done
        here = slice(first, first + TILE)
        total = total_ref[pl.ds(step * BACK_HEADS + g, 1), here]
        inner = inner_ref[pl.ds(step * BACK_HEADS + g, 1), here]
        probs = jnp.exp(masked(scores, bias_ref, first, base, 0) - total)
        return (probs * (prob_grad - inner)).astype(BF16), probs.astype(BF16)

    def finish(item, done):
        first, g = item
        score_grad, probs = done
        here, lanes = slice(first, first + TILE), head_lanes(g)
        query_grad, row = None, 0
        for keys in window_keys(halo_ref, own_ref, first, lanes):
            term = rows_dot(score_grad[row : row + keys.shape[0]], keys)
            row += keys.shape[0]
            query_grad = term if query_grad is None else query_grad + term
        sums_ref[start + first : start + first + REACH, lanes] += dot(score_grad, query_of(first, g)) + dot(
            probs, grad_ref[here, lanes]
        )
        partial = partial_ref[here, lanes].astype(F32)
        ask_grad_ref[here, lanes] = (partial + jnp.where(left, query_grad * SCALE, 0.0)).astype(BF16)

    pipelined([(first, g) for g in range(BACK_HEADS) for first in range(0, rows, TILE)], products, score_grads, finish)
    memory_grad_ref[...] = sums_ref[...].astype(BF16)


def local_attention_back(base, ask, halo, own, grad, total, inner, partial, far_grad, steps, earlier=(), after=()):
    rows = ask.shape[0]
    length = far_grad.shape[0]
    first = steps[0]
    head = lambda n: pl.BlockSpec((n, BACK_HEADS * LANES), lambda h: (0, h + first))
    flat = pl.BlockSpec((H, rows), lambda h: (0, 0))
    held = [pl.BlockSpec(memory_space=pl.ANY)] * (len(earlier) + len(after))
    return pl.pallas_call(
        lambda *refs: local_back_kernel(first, *refs[:9], *refs[9 + len(held) :]),
        grid=(len(steps),),
        in_specs=[
            pl.BlockSpec(memory_space=pltpu.SMEM),
            head(rows),
            pl.BlockSpec((SPAN, BACK_HEADS * LANES), lambda h: (0, h + first)),
            head(rows),
            head(rows),
            flat,
            flat,
            head(rows),
            head(length),
        ]
        + held,
        out_specs=[head(rows), head(length)],
        out_shape=[
            pltpu.HBM((rows, WIDE), BF16),
            pltpu.HBM((length, WIDE), BF16),
        ],
        scratch_shapes=[pltpu.VMEM((length, BACK_HEADS * LANES), F32), pltpu.VMEM((REACH, TILE), F32)],
        input_output_aliases={9 + k: k for k in range(len(earlier))},
        compiler_params=pltpu.CompilerParams(vmem_limit_bytes=20 * MIB),
        cost_estimate=cost_of(0.3),
        name="local_attention_back",
    )(base, *in_hbm(ask, halo, own, grad, total, inner, partial, far_grad, *earlier), *after)


def token_tile(ref, token):
    return ref[pl.ds(pl.multiple_of(token * H, H), H), :]


def put_heads(ref, h, values):
    ref[pl.ds(h, values.shape[0], stride=H), :] = values


def take_heads(ref, h, count):
    return ref[pl.ds(h, count, stride=H), :]


def left_lanes(count):
    return lax.broadcasted_iota(jnp.int32, (count, LANES), 1) < HD


def build_table(table, *refs):
    block, base = 128, 0
    for ref in refs:

        def rows(k, carry, ref=ref, base=base):
            here = pl.ds(pl.multiple_of(k * block, block), block)
            for h in range(H):
                there = pl.ds(pl.multiple_of((base + k * block) * H, block * H) + h, block, stride=H)
                table[there, :] = ref[here, head_lanes(h)].astype(F32)
            return carry

        lax.fori_loop(0, ref.shape[0] // block, rows, 0)
        base += ref.shape[0]


def row_sums(values):
    return jnp.sum(values, axis=1, keepdims=True)


def softmax_over(match):
    top = functools.reduce(jnp.maximum, match)
    expo = [jnp.exp(m - top) for m in match]
    scale = 1.0 / functools.reduce(jnp.add, expo)
    return [e * scale for e in expo]


TOKENS = 128
GROUP = 4


def lane_sums(values):
    return dot(values.astype(BF16), jnp.ones((LANES, LANES), BF16))


def gather_group(index_ref, table, near_rows, first, group):
    for k in range(GROUP):
        t = group * GROUP + k
        for j in range(NEAR):
            near_rows[j, t * H : (t + 1) * H, :] = token_tile(table, index_ref[(first + t) * NEAR + j])


def scatter_group(index_ref, sums, terms, first, group):
    for k in range(GROUP):
        t = group * GROUP + k
        for j in range(NEAR):
            there = pl.ds(pl.multiple_of(index_ref[(first + t) * NEAR + j] * H, H), H)
            held = sums[j % len(sums)]
            held[there, :] = held[there, :] + terms[j, t * H : (t + 1) * H, :]


def retrieve_kernel(
    index_ref, far_ref, halo_ref, own_ref, ask_ref, local_ref, near_ref, weight_ref, blended_ref,
    table, ask_rows, out_rows, near_rows,
):
    step = pl.program_id(0)
    count = ask_ref.shape[0]
    first = step * count

    @pl.when(step == 0)
    def build():
        build_table(table, far_ref, halo_ref, own_ref)

    for h in range(H):
        put_heads(ask_rows, h, ask_ref[:, head_lanes(h)].astype(F32))
    left = left_lanes(GROUP * H)
    groups = count // GROUP
    rows_of = lambda group: slice(group * GROUP * H, (group + 1) * GROUP * H)

    def match(group):
        if group + 1 < groups:
            gather_group(index_ref, table, near_rows, first, group + 1)
        here = rows_of(group)
        query = jnp.where(left, ask_rows[here, :], 0.0)
        return [(lane_sums if j > 1 else row_sums)(near_rows[j, here, :] * query) for j in range(NEAR)]

    def weights(item, done):
        return softmax_over(done)

    def recall(item, weight):
        here = rows_of(item[0])
        out_rows[here, :] = functools.reduce(jnp.add, [weight[j] * near_rows[j, here, :] for j in range(NEAR)])
        for j in range(NEAR):
            weight_ref[j, here, :] = weight[j].astype(BF16)
            near_ref[j, here, :] = near_rows[j, here, :].astype(BF16)

    gather_group(index_ref, table, near_rows, first, 0)
    pipelined([(group,) for group in range(groups)], match, weights, recall)
    left = left_lanes(count)
    for h in range(H):
        lanes = head_lanes(h)
        local = local_ref[:, lanes].astype(F32)
        mix = 1.0 - jax.nn.sigmoid(ask_ref[:, lanes].astype(F32))
        blended = local + mix * (take_heads(out_rows, h, count) - local)
        blended_ref[:, lanes] = jnp.where(left, 0.0, blended).astype(BF16)


def retrieve(index, far, halo, own, ask, local):
    rows = ask.shape[0]
    length = far.shape[0] + halo.shape[0] + rows
    count = min(TOKENS, rows)
    wide = pl.BlockSpec((count, WIDE), lambda c: (c, 0))
    tall = pl.BlockSpec((NEAR, count * H, LANES), lambda c: (0, c, 0))
    return pl.pallas_call(
        retrieve_kernel,
        grid=(rows // count,),
        in_specs=[
            pl.BlockSpec(memory_space=pltpu.SMEM),
            pl.BlockSpec(far.shape, lambda c: (0, 0)),
            pl.BlockSpec(halo.shape, lambda c: (0, 0)),
            pl.BlockSpec(own.shape, lambda c: (0, 0)),
            wide,
            wide,
        ],
        out_specs=[tall, tall, wide],
        out_shape=[
            pltpu.HBM((NEAR, rows * H, LANES), BF16),
            pltpu.HBM((NEAR, rows * H, LANES), BF16),
            jax.ShapeDtypeStruct((rows, WIDE), BF16),
        ],
        scratch_shapes=[
            pltpu.VMEM((length * H, LANES), F32),
            pltpu.VMEM((count * H, LANES), F32),
            pltpu.VMEM((count * H, LANES), F32),
            pltpu.VMEM((NEAR, count * H, LANES), F32),
        ],
        compiler_params=pltpu.CompilerParams(vmem_limit_bytes=28 * MIB),
        cost_estimate=cost_of(12),
        name="retrieve",
    )(index, *in_hbm(far, halo, own, ask, local))


def retrieve_back_kernel(
    index_ref, grad_ref, ask_ref, local_ref, near_ref, weight_ref,
    local_grad_ref, inner_ref, partial_ref, far_ref,
    sums_even, sums_odd, ask_rows, grad_rows, out_rows, mixed, terms,
):
    step = pl.program_id(0)
    count = ask_ref.shape[0]
    first = step * count
    length = far_ref.shape[0]

    @pl.when(step == 0)
    def clear():
        block = 1024

        def rows(k, carry):
            here = pl.ds(pl.multiple_of(k * block, block), block)
            sums_even[here, :] = jnp.zeros((block, LANES), F32)
            sums_odd[here, :] = jnp.zeros((block, LANES), F32)
            return carry

        lax.fori_loop(0, length * H // block, rows, 0)

    left = left_lanes(count)
    lane = lax.broadcasted_iota(jnp.int32, (count, LANES), 1)
    inner_all = jnp.zeros((count, LANES), F32)
    for h in range(H):
        lanes = head_lanes(h)
        grad = grad_ref[:, lanes].astype(F32)
        ask = ask_ref[:, lanes].astype(F32)
        mix = 1.0 - jax.nn.sigmoid(ask)
        inner = row_sums(grad * local_ref[:, lanes].astype(F32))
        inner_all = jnp.where(lane == HD + h, inner - mix * inner, inner_all)
        mixed[:, lanes] = mix * inner
        local_grad_ref[:, lanes] = (grad - mix * grad).astype(BF16)
        put_heads(ask_rows, h, jnp.where(left, ask, mix))
        put_heads(grad_rows, h, grad)
    inner_ref[...] = inner_all.T[HD : HD + H, :]
    groups = count // GROUP
    left_tile = left_lanes(GROUP * H)
    sums = (sums_even, sums_odd)
    rows_of = lambda group: slice(group * GROUP * H, (group + 1) * GROUP * H)

    def weight_grads(group):
        here = rows_of(group)
        grad = ask_rows[here, :] * grad_rows[here, :]
        return [(lane_sums if j > 1 else row_sums)(near_ref[j, here, :].astype(F32) * grad) for j in range(NEAR)]

    def match_grads(item, weight_grad):
        here = rows_of(item[0])
        weight = [weight_ref[j, here, :].astype(F32) for j in range(NEAR)]
        inner = functools.reduce(jnp.add, [w * g for w, g in zip(weight, weight_grad)])
        match_grad = [w * (g - inner) for w, g in zip(weight, weight_grad)]
        query_grad = functools.reduce(
            jnp.add, [g * near_ref[j, here, :].astype(F32) for j, g in enumerate(match_grad)]
        )
        out_rows[here, :] = jnp.where(left_tile, query_grad * SCALE, inner)
        ask = ask_rows[here, :]
        source = jnp.where(left_tile, ask, ask * grad_rows[here, :])
        for j in range(NEAR):
            terms[j, here, :] = jnp.where(left_tile, match_grad[j], weight[j]) * source

    def add_terms(item, done):
        scatter_group(index_ref, sums, terms, first, item[0])

    pipelined([(group,) for group in range(groups)], weight_grads, match_grads, add_terms)
    for h in range(H):
        lanes = head_lanes(h)
        tile = take_heads(out_rows, h, count)
        gate = jax.nn.sigmoid(ask_ref[:, lanes].astype(F32))
        partial_ref[:, lanes] = jnp.where(left, tile, (gate / HD) * (mixed[:, lanes] - tile)).astype(BF16)

    @pl.when(step == pl.num_programs(0) - 1)
    def finish():
        block = 128

        def rows(k, carry):
            here = pl.ds(pl.multiple_of(k * block, block), block)
            for h in range(H):
                there = pl.ds(pl.multiple_of(k * (block * H), block * H) + h, block, stride=H)
                far_ref[here, head_lanes(h)] = (sums_even[there, :] + sums_odd[there, :]).astype(BF16)
            return carry

        lax.fori_loop(0, length // block, rows, 0)


def retrieve_back(index, grad, ask, local, near, weight, length, after=()):
    rows = ask.shape[0]
    count = min(TOKENS, rows)
    wide = pl.BlockSpec((count, WIDE), lambda c: (c, 0))
    tall = pl.BlockSpec((NEAR, count * H, LANES), lambda c: (0, c, 0))
    return pl.pallas_call(
        lambda *refs: retrieve_back_kernel(*refs[:6], *refs[6 + len(after) :]),
        grid=(rows // count,),
        in_specs=[
            pl.BlockSpec(memory_space=pltpu.SMEM),
            wide,
            wide,
            wide,
            tall,
            tall,
        ]
        + [pl.BlockSpec(memory_space=pl.ANY)] * len(after),
        out_specs=[
            wide,
            pl.BlockSpec((H, count), lambda c: (0, c)),
            wide,
            pl.BlockSpec((length, WIDE), lambda c: (0, 0)),
        ],
        out_shape=[
            pltpu.HBM((rows, WIDE), BF16),
            pltpu.HBM((H, rows), F32),
            pltpu.HBM((rows, WIDE), BF16),
            pltpu.HBM((length, WIDE), BF16),
        ],
        scratch_shapes=[
            pltpu.VMEM((length * H, LANES), F32),
            pltpu.VMEM((length * H, LANES), F32),
            pltpu.VMEM((count * H, LANES), F32),
            pltpu.VMEM((count * H, LANES), F32),
            pltpu.VMEM((count * H, LANES), F32),
            pltpu.VMEM((count, WIDE), F32),
            pltpu.VMEM((NEAR, count * H, LANES), F32),
        ],
        compiler_params=pltpu.CompilerParams(vmem_limit_bytes=40 * MIB),
        cost_estimate=cost_of(24),
        name="retrieve_back",
    )(index, *in_vmem(grad), *in_hbm(ask, local, near, weight), *after)


def turned(block, shift):
    size = lax.axis_size("seq")
    return lax.ppermute(block, "seq", [((i + shift) % size, i) for i in range(size)])


def index_bits(axis):
    return [(axis, b) for b in range(lax.axis_size(axis).bit_length() - 1)]


def level_groups():
    dp, seq = index_bits("dp"), index_bits("seq")
    return [dp[:1], dp[1:3], seq[:1] + dp[3:4]], dp[4:] + seq[1:]


def own_place(group):
    place = 0
    for k, (axis, bit) in enumerate(group):
        place = place + (((lax.axis_index(axis) >> bit) & 1) << k)
    return place


def own_chunk():
    chunk = 0
    for group in level_groups()[0]:
        chunk = (chunk << len(group)) + own_place(group)
    return jnp.reshape(chunk, (1,)).astype(jnp.int32)


def swapped(block, group, distance):
    flips = {"dp": 0, "seq": 0}
    for k, (axis, bit) in enumerate(group):
        if (distance >> k) & 1:
            flips[axis] |= 1 << bit
    n_dp, n_seq = lax.axis_size("dp"), lax.axis_size("seq")
    if not flips["seq"]:
        return lax.ppermute(block, "dp", [(i, i ^ flips["dp"]) for i in range(n_dp)])
    if not flips["dp"]:
        return lax.ppermute(block, "seq", [(i, i ^ flips["seq"]) for i in range(n_seq)])
    route = [(i, (i // n_seq ^ flips["dp"]) * n_seq + (i % n_seq ^ flips["seq"])) for i in range(n_dp * n_seq)]
    return lax.ppermute(block, ("dp", "seq"), route)


def in_hbm(*arrays):
    return [pltpu.with_memory_space_constraint(v, pltpu.HBM) for v in arrays]


def in_vmem(*arrays):
    return [pltpu.with_memory_space_constraint(v, pltpu.VMEM) for v in arrays]


def whole_call(kernel, name, *operands, outs, scratch=(), after=(), cost=0.3, spare=4, resident=(), streamed=(), inside=(), after_far=()):
    count, late = len(operands), len(streamed)
    operands = [in_hbm(v)[0] if k in streamed else v for k, v in enumerate(operands)]
    operands = [in_vmem(v)[0] if k in inside else v for k, v in enumerate(operands)]

    def place(k, v):
        if v.dtype == jnp.int32:
            return pltpu.SMEM
        return pltpu.HBM if k in streamed else pltpu.VMEM

    held = [pltpu.VMEM(operands[k].shape, operands[k].dtype) for k in streamed]
    shapes = [(v.shape, v.dtype) for k, v in enumerate(operands) if k not in inside]
    shapes += [(v.shape, v.dtype) for v in scratch]
    shapes += [out for k, out in enumerate(outs) if k not in resident]
    size = sum(math.prod(shape) * jnp.dtype(dtype).itemsize for shape, dtype in shapes)

    def wrapped(*refs):
        ins, rest = list(refs[:count]), refs[count + len(after) + len(after_far) :]
        if not late:
            return kernel(*ins, *rest)
        rest, copies = rest[: -2 * late], {}
        for n, k in enumerate(streamed):
            held_ref, sem = refs[-2 * late + n], refs[-late + n]
            copies[k] = pltpu.make_async_copy(ins[k], held_ref, sem)
            copies[k].start()
            ins[k] = held_ref
        return kernel(lambda k: copies[k].wait(), *ins, *rest)

    return pl.pallas_call(
        wrapped,
        in_specs=[pl.BlockSpec(memory_space=place(k, v)) for k, v in enumerate(operands)]
        + [pl.BlockSpec(memory_space=pl.ANY)] * len(after)
        + [pl.BlockSpec(memory_space=pltpu.HBM)] * len(after_far),
        out_specs=[pl.BlockSpec(memory_space=pltpu.VMEM)] * len(outs),
        out_shape=[
            pltpu.VMEM(shape, dtype) if k in resident else jax.ShapeDtypeStruct(shape, dtype)
            for k, (shape, dtype) in enumerate(outs)
        ],
        scratch_shapes=list(scratch) + held + [pltpu.SemaphoreType.DMA(())] * late,
        compiler_params=pltpu.CompilerParams(vmem_limit_bytes=size + spare * MIB),
        cost_estimate=cost_of(cost),
        name=name,
    )(*operands, *after, *in_hbm(*after_far))


def add_pieces(own, arrived, pieces, extra=0, **order):
    rows, width = own.shape
    count = (rows - extra) // pieces

    def kernel(*refs):
        terms, outs = refs[: 1 + len(arrived)], refs[1 + len(arrived) :]

        def total(here):
            values = terms[0][here, :].astype(F32)
            for term in terms[1:]:
                values = values + term[here, :].astype(F32)
            return values.astype(BF16)

        for k, out in enumerate(outs):
            out[:count, :] = total(slice(k * count, (k + 1) * count))
        if extra:
            last = total(slice(rows - extra, rows))
            for out in outs:
                out[count:, :] = last

    outs = [((count + extra, width), BF16)] * pieces
    return whole_call(kernel, "add_pieces", own, *arrived, outs=outs, **order)


def join_pieces(pieces, **order):
    count, width = pieces[0].shape

    def kernel(*refs):
        for k, ref in enumerate(refs[:-1]):
            refs[-1][k * count : (k + 1) * count, :] = ref[...]

    return whole_call(kernel, "join_pieces", *pieces, outs=[((count * len(pieces), width), BF16)], **order)[0]


def scatter_start(own, send):
    return own, [swapped(send, level_groups()[0][0], 1)]


def scatter_level(held, level, extra=0, **order):
    own, arrived = held
    group = level_groups()[0][level]
    pieces = add_pieces(own, arrived, 2 ** len(group), extra, **order)
    return pieces[0], [swapped(piece, group, d) for d, piece in enumerate(pieces) if d]


def scatter_finish(held, **order):
    total = add_pieces(*held, 1, **order)[0]
    for bit in level_groups()[1]:
        total = add_pieces(total, [swapped(total, [bit], 1)], 1)[0]
    return total


def gather_level(total, level):
    group = level_groups()[0][level]
    return [total] + [swapped(total, group, d) for d in range(1, 2 ** len(group))]


def rms_unit(values):
    scale = lax.rsqrt(jnp.mean(values * values, axis=-1, keepdims=True) + EPS)
    return values * scale, scale


def rms_back(unit, scale, grad):
    return scale * (grad - unit * jnp.mean(grad * unit, axis=-1, keepdims=True))


def lay_weights_kernel(wait, query_ref, key_ref, value_ref, gate_ref, output_ref, ask_ref, memory_ref, blend_ref):
    width = query_ref.shape[0]
    gate = gate_ref[...].astype(F32).T
    for k in (0, 1, 2, 4):
        wait(k)
    for h in range(H):
        here = slice(h * HD, (h + 1) * HD)
        column = jnp.broadcast_to(gate[:, h : h + 1], (width, HD)).astype(BF16)
        ask_ref[:, head_lanes(h)] = jnp.concatenate([query_ref[:, here], column], axis=1)
        memory_ref[:, head_lanes(h)] = jnp.concatenate([key_ref[:, here], value_ref[:, here]], axis=1)
        blend_ref[h * LANES : h * LANES + HD, :] = jnp.zeros((HD, width), BF16)
        blend_ref[h * LANES + HD : (h + 1) * LANES, :] = output_ref[here, :]


def lay_weights(query_weight, key_weight, value_weight, gate_weight, output_weight):
    width = query_weight.shape[0]
    wide = ((width, WIDE), BF16)
    return whole_call(
        lay_weights_kernel,
        "lay_weights",
        query_weight,
        key_weight,
        value_weight,
        gate_weight.T,
        output_weight,
        outs=[wide, wide, ((WIDE, width), BF16)],
        streamed=(0, 1, 2, 4),
    )


def project_kernel(inputs_ref, gain_ref, empty_ref, ask_weight_ref, memory_weight_ref, normed_ref, ask_ref, memory_ref):
    normed = (rms_unit(inputs_ref[...].astype(F32))[0] * gain_ref[0:1, :]).astype(BF16)
    normed_ref[...] = normed
    memory_ref[...] = dot(normed, memory_weight_ref[...]).astype(BF16)
    if ask_ref is not None:
        left = (lax.broadcasted_iota(jnp.int32, (1, WIDE), 1) % LANES) < HD
        ask = dot(normed, ask_weight_ref[...])
        block = normed.shape[0]
        row = lax.broadcasted_iota(jnp.int32, (block, block), 0)
        column = lax.broadcasted_iota(jnp.int32, (block, block), 1)
        here = pl.ds(pl.multiple_of(pl.program_id(0) * block, block), block)
        empty = jnp.sum(jnp.where(row == column, empty_ref[:, here].astype(F32), 0.0), axis=1, keepdims=True)
        gate = jnp.where(empty > 0.0, SHUT, ask)
        ask_ref[...] = jnp.where(left, ask * SCALE, gate).astype(BF16)


def row_blocks_call(kernel, name, *operands, outs, cost):
    rows = operands[0].shape[0]
    block = block_rows(rows)
    rows_spec = lambda width: pl.BlockSpec((block, width), lambda k: (k, 0))
    whole = lambda v: pl.BlockSpec(v.shape, lambda k: (0, 0))
    return pl.pallas_call(
        kernel,
        grid=(rows // block,),
        in_specs=[rows_spec(operands[0].shape[1])] + [whole(v) for v in operands[1:]],
        out_specs=[rows_spec(width) for width in outs],
        out_shape=[pltpu.HBM((rows, width), BF16) for width in outs],
        compiler_params=pltpu.CompilerParams(vmem_limit_bytes=14 * MIB),
        cost_estimate=cost_of(cost),
        name=name,
    )(*operands)


def project(inputs, gain, empty, ask_weight, memory_weight):
    width = inputs.shape[1]
    return row_blocks_call(
        project_kernel, "project", inputs, gain, empty, ask_weight, memory_weight, outs=[width, WIDE, WIDE], cost=3
    )


def project_memory(inputs, gain, memory_weight):
    def kernel(inputs_ref, gain_ref, weight_ref, normed_ref, memory_ref):
        project_kernel(inputs_ref, gain_ref, None, None, weight_ref, normed_ref, None, memory_ref)

    return row_blocks_call(
        kernel, "project_memory", inputs, gain, memory_weight, outs=[inputs.shape[1], WIDE], cost=2
    )


ROOT = 0.7978845608028654
CUBE = 0.044715


def gelu_and_slope(x):
    square = x * x
    tanh = jnp.tanh(ROOT * (x * (1.0 + CUBE * square)))
    half = 0.5 * (1.0 + tanh)
    slope = half + (0.5 * ROOT) * x * (1.0 - tanh * tanh) * (1.0 + (3.0 * CUBE) * square)
    return x * half, slope


def hidden_kernel(
    wait, chunk_ref, inputs_ref, cotangent_ref, blended_ref, blend_weight_ref, gain_ref, hidden_weight_ref, return_weight_ref,
    resid_ref, active, hidden_grad, own_ref, send_ref,
    normed, return_sums, hidden_sums,
):
    rows, width = inputs_ref.shape
    hidden = hidden_weight_ref.shape[1]
    block = block_rows(rows)
    gain = gain_ref[0:1, :]
    columns = [slice(at, at + width) for at in range(0, hidden, width)]
    wait(1)

    def row_block(k, carry):
        here = pl.ds(pl.multiple_of(k * block, block), block)
        resid = inputs_ref[here, :].astype(F32) + dot(blended_ref[here, :], blend_weight_ref[...])
        resid_ref[here, :] = resid
        normed_here = (rms_unit(resid)[0] * gain).astype(BF16)
        normed[here, :] = normed_here

        @pl.when(k == 0)
        def weights():
            for n in (2, 6, 7):
                wait(n)

        cotangent = cotangent_ref[here, :]

        def products(lanes):
            return dot(normed_here, hidden_weight_ref[:, lanes]), dot_back(cotangent, return_weight_ref[lanes, :])

        def activate(item, done):
            value, slope = gelu_and_slope(done[0])
            return value.astype(BF16), (done[1] * slope).astype(BF16)

        def keep(item, done):
            active[here, item[0]] = done[0]
            hidden_grad[here, item[0]] = done[1]

        pipelined([(lanes,) for lanes in columns], products, activate, keep)
        return carry

    lax.fori_loop(0, rows // block, row_block, 0)

    def column_block(k, carry):
        lanes = pl.ds(pl.multiple_of(k * width, width), width)
        return_sums[lanes, :] = rows_dot(active[:, lanes], cotangent_ref[...]).astype(BF16)
        hidden_sums[:, lanes] = rows_dot(normed[...], hidden_grad[:, lanes]).astype(BF16)
        return carry

    lax.fori_loop(0, hidden // width, column_block, 0)
    tall, flat = hidden // CHUNKS, width // CHUNKS

    def pack(r, carry):
        for half, out in enumerate((own_ref, send_ref)):
            chunk = chunk_ref[0] ^ (r + half * (CHUNKS // 2))
            rows_at = lambda offset, count: pl.ds(pl.multiple_of(r * EARLY_ROWS + offset, flat), count)
            out[rows_at(0, tall), :] = return_sums[pl.ds(pl.multiple_of(chunk * tall, tall), tall), :]
            for c in range(hidden // width):
                out[rows_at(tall + c * flat, flat), :] = hidden_sums[
                    pl.ds(pl.multiple_of(chunk * flat, flat), flat), c * width : (c + 1) * width
                ]
        return carry

    lax.fori_loop(0, CHUNKS // 2, pack, 0)


def hidden_layer(chunk, inputs, cotangent, blended, blend_weight, gain, hidden_weight, return_weight):
    rows, width = inputs.shape
    hidden = hidden_weight.shape[1]
    half = ((CHUNKS // 2 * EARLY_ROWS, width), BF16)
    return whole_call(
        hidden_kernel,
        "hidden_layer",
        chunk,
        inputs,
        cotangent,
        blended,
        blend_weight,
        gain,
        hidden_weight,
        return_weight,
        outs=[((rows, width), F32), ((rows, hidden), BF16), ((rows, hidden), BF16), half, half],
        scratch=[
            pltpu.VMEM((rows, width), BF16),
            pltpu.VMEM((hidden, width), BF16),
            pltpu.VMEM((width, hidden), BF16),
        ],
        cost=20,
        spare=12,
        resident=(0, 1, 2),
        streamed=(1, 6, 2, 7),
    )


def resid_kernel(
    wait, resid_ref, cotangent_ref, blended_ref, active, hidden_grad, blend_weight_ref, gain_ref, hidden_weight_ref, return_weight_ref,
    outputs_ref, resid_grad_ref, blended_grad_ref, gain_grad_ref, blend_sums_ref,
    resid_grad_b,
):
    rows, width = resid_ref.shape
    block = 2 * block_rows(rows) if rows % 512 == 0 else block_rows(rows)
    gain = gain_ref[0:1, :]
    wait(7)

    def row_block(k, gain_grad):
        here = pl.ds(pl.multiple_of(k * block, block), block)
        resid = resid_ref[here, :]
        unit, scale = rms_unit(resid)
        grad = dot_back(hidden_grad[here, :], hidden_weight_ref[...])

        @pl.when(k == 0)
        def weights():
            wait(8)
            wait(1)

        outputs_ref[here, :] = (resid + dot(active[here, :], return_weight_ref[...])).astype(BF16)
        total = cotangent_ref[here, :].astype(F32) + rms_back(unit, scale, grad * gain)
        resid_grad_ref[here, :] = total
        resid_grad_b[here, :] = total.astype(BF16)
        blended_grad_ref[here, :] = dot_back(total.astype(BF16), blend_weight_ref[...]).astype(BF16)
        return gain_grad + jnp.sum(grad * unit, axis=0, keepdims=True)

    gain_grad = lax.fori_loop(0, rows // block, row_block, jnp.zeros((1, width), F32))
    gain_grad_ref[...] = jnp.broadcast_to(gain_grad, gain_grad_ref.shape)
    blend_sums_ref[...] = rows_dot(blended_ref[...], resid_grad_b[...]).astype(BF16)


def resid_layer(resid, cotangent, blended, active, hidden_grad, blend_weight, gain, hidden_weight, return_weight, after=()):
    rows, width = resid.shape
    return whole_call(
        resid_kernel,
        "resid_layer",
        resid,
        cotangent,
        blended,
        active,
        hidden_grad,
        blend_weight,
        gain,
        hidden_weight,
        return_weight,
        outs=[
            ((rows, width), BF16),
            ((rows, width), F32),
            ((rows, WIDE), BF16),
            ((8, width), F32),
            ((WIDE, width), BF16),
        ],
        scratch=[pltpu.VMEM((rows, width), BF16)],
        after=after,
        cost=8,
        spare=6,
        streamed=(7, 8, 1),
        inside=(0, 3, 4),
        resident=(2,),
    )


def unpack_early_kernel(chunk_ref, own_ref, other_ref, return_ref, hidden_ref, token_ref):
    token_ref[...] = jnp.zeros_like(token_ref)
    width = return_ref.shape[1]
    tall, flat = return_ref.shape[0] // CHUNKS, hidden_ref.shape[0] // CHUNKS
    for r in range(CHUNKS):
        chunk = chunk_ref[0] ^ r
        source = own_ref if r < CHUNKS // 2 else other_ref
        at = (r % (CHUNKS // 2)) * EARLY_ROWS
        return_ref[pl.ds(pl.multiple_of(chunk * tall, tall), tall), :] = source[at : at + tall, :].astype(F32)
        at += tall
        there = pl.ds(pl.multiple_of(chunk * flat, flat), flat)
        for c in range(hidden_ref.shape[1] // width):
            hidden_ref[there, c * width : (c + 1) * width] = source[at : at + flat, :].astype(F32)
            at += flat


def unpack_early(chunk, own, other, return_shape, hidden_shape, after=()):
    outs = [(return_shape, F32), (hidden_shape, F32), TOKEN]
    return whole_call(unpack_early_kernel, "unpack_early", chunk, own, other, outs=outs, after=after)


def late_kernel(
    chunk_ref, far_ref, halo_ref, normed_ref, ask_ref, memory_ref, first_ref, second_ref, blend_ref, own_ref, send_ref, ask_sums, memory_sums
):
    width = normed_ref.shape[1]
    flat = width // CHUNKS
    ask_sums[...] = rows_dot(normed_ref[...], ask_ref[...]).astype(BF16)
    total, at = None, 0
    for ref in (far_ref, halo_ref, normed_ref):
        term = rows_dot(ref[...], memory_ref[at : at + ref.shape[0], :])
        total, at = term if total is None else total + term, at + ref.shape[0]
    memory_sums[...] = total.astype(BF16)
    lane = lax.broadcasted_iota(jnp.int32, (width, LANES), 1)
    small = jnp.zeros((width, LANES), F32)
    for h in range(H):
        at = h * LANES + HD
        small = jnp.where(lane == h, HD * ask_sums[:, at : at + 1].astype(F32), small)
    zeros = jnp.zeros((EXTRA_ROWS - H - 2, width), F32)
    extra = jnp.concatenate([small.T[:H, :], first_ref[0:1, :], second_ref[0:1, :], zeros], axis=0).astype(BF16)
    for out in (own_ref, send_ref):
        out[CHUNKS // 2 * LATE_ROWS :, :] = extra
    for r in range(CHUNKS):
        chunk = chunk_ref[0] ^ r
        out = own_ref if r < CHUNKS // 2 else send_ref
        at = (r % (CHUNKS // 2)) * LATE_ROWS
        here = pl.ds(pl.multiple_of(chunk * flat, flat), flat)
        for pair in range(H // 2):
            lanes = slice(pair * LANES, (pair + 1) * LANES)
            even = slice(2 * pair * LANES, 2 * pair * LANES + HD)
            odd = slice((2 * pair + 1) * LANES, (2 * pair + 1) * LANES + HD)
            out[at : at + flat, lanes] = jnp.concatenate([ask_sums[here, even], ask_sums[here, odd]], axis=1)
        out[at + flat : at + 2 * flat, :] = memory_sums[here, :width]
        out[at + 2 * flat : at + 3 * flat, :] = memory_sums[here, width:]
        row = (chunk // (HD // flat)) * LANES + HD + (chunk % (HD // flat)) * flat
        out[at + 3 * flat : at + 4 * flat, :] = blend_ref[pl.ds(pl.multiple_of(row, flat), flat), :]


def unpack_late_kernel(
    chunk_ref, own_ref, other_ref, extra_ref, query_ref, key_ref, value_ref, output_ref, gate_ref, first_ref, second_ref
):
    width = query_ref.shape[1]
    flat = width // CHUNKS
    for r in range(CHUNKS):
        chunk = chunk_ref[0] ^ r
        source = own_ref if r < CHUNKS // 2 else other_ref
        at = (r % (CHUNKS // 2)) * LATE_ROWS
        there = pl.ds(pl.multiple_of(chunk * flat, flat), flat)
        query_ref[there, :] = source[at : at + flat, :].astype(F32)
        for half in range(2):
            at += flat
            for pair in range(H // 4):
                lanes = slice((half * H // 4 + pair) * LANES, (half * H // 4 + pair + 1) * LANES)
                even = source[at : at + flat, 2 * pair * LANES : (2 * pair + 1) * LANES]
                odd = source[at : at + flat, (2 * pair + 1) * LANES : (2 * pair + 2) * LANES]
                key_ref[there, lanes] = jnp.concatenate([even[:, :HD], odd[:, :HD]], axis=1).astype(F32)
                value_ref[there, lanes] = jnp.concatenate([even[:, HD:], odd[:, HD:]], axis=1).astype(F32)
        at += flat
        output_ref[there, :] = source[at : at + flat, :].astype(F32)
    extra = extra_ref[...].astype(F32)
    gate_ref[...] = extra[:H, :]
    first_ref[...] = extra[H : H + 1, :]
    second_ref[...] = extra[H + 1 : H + 2, :]


def pack_late(chunk, far, halo, normed, ask_grad, memory_grad, first_grad, second_grad, blend_grad, after=()):
    width = normed.shape[1]
    half = ((CHUNKS // 2 * LATE_ROWS + EXTRA_ROWS, width), BF16)
    return whole_call(
        late_kernel,
        "late_weight_grads",
        chunk,
        far,
        halo,
        normed,
        ask_grad,
        memory_grad,
        first_grad,
        second_grad,
        blend_grad,
        outs=[half, half],
        scratch=[pltpu.VMEM((width, WIDE), BF16), pltpu.VMEM((width, WIDE), BF16)],
        after=after,
    )


def unpack_late(chunk, own, other, extra):
    width = own.shape[1]
    square, row = ((width, width), F32), ((1, width), F32)
    return whole_call(
        unpack_late_kernel,
        "unpack_late",
        chunk,
        own,
        other,
        extra,
        outs=[square] * 4 + [((H, width), F32), row, row],
    )


def normed_back_kernel(
    wait, inputs_ref, far_ref, halo_ref, ask_ref, memory_ref, ask_weight_ref, memory_weight_ref, own_grad_ref, others_grad_ref, gain_ref
):
    rows, width = inputs_ref.shape
    length = memory_ref.shape[0]
    block = block_rows(rows)

    def unit(ref, here):
        values = ref[here, :].astype(F32)
        return values * lax.rsqrt(jnp.mean(values * values, axis=-1, keepdims=True) + EPS)

    gain = jnp.zeros((1, width), F32)
    wait(4)
    for at in range(0, length - rows, block):
        here = slice(at, at + block)
        grad = dot_back(memory_ref[here, :], memory_weight_ref[...])
        others_grad_ref[here, :] = grad.astype(BF16)
        past = far_ref.shape[0]
        values = unit(far_ref, here) if at < past else unit(halo_ref, slice(at - past, at - past + block))
        gain = gain + jnp.sum(grad * values, axis=0, keepdims=True)
    wait(3)
    for at in range(0, rows, block):
        here = slice(at, at + block)
        there = slice(length - rows + at, length - rows + at + block)
        grad = dot_back(ask_ref[here, :], ask_weight_ref[...]) + dot_back(memory_ref[there, :], memory_weight_ref[...])
        own_grad_ref[here, :] = grad
        gain = gain + jnp.sum(grad * unit(inputs_ref, here), axis=0, keepdims=True)
    gain_ref[...] = jnp.broadcast_to(gain, gain_ref.shape)


def normed_back(inputs, far, halo, ask_grad, memory_grad, ask_weight, memory_weight, after=()):
    rows, width = inputs.shape
    return whole_call(
        normed_back_kernel,
        "normed_back",
        inputs,
        far,
        halo,
        ask_grad,
        memory_grad,
        ask_weight,
        memory_weight,
        outs=[((rows, width), F32), ((far.shape[0] + halo.shape[0], width), BF16), ((8, width), F32)],
        streamed=(4, 3),
        after=after,
    )


def input_back_kernel(inputs_ref, gain_ref, resid_grad_ref, own_ref, *refs):
    arrived, out_ref, token_ref = refs[:-2], refs[-2], refs[-1]
    token_ref[...] = jnp.zeros_like(token_ref)
    values = inputs_ref[...].astype(F32)
    grad = own_ref[...]
    for ref in arrived:
        grad = grad + ref[...].astype(F32)
    grad = grad * gain_ref[0:1, :]
    scale = lax.rsqrt(jnp.mean(values * values, axis=-1, keepdims=True) + EPS)
    unit = values * scale
    part = scale * (grad - unit * jnp.mean(grad * unit, axis=-1, keepdims=True))
    out_ref[...] = (resid_grad_ref[...] + part).astype(BF16)


def body(
    inputs,
    cotangent,
    neighbours,
    empty_rows,
    first_gain,
    query_weight,
    key_weight,
    value_weight,
    gate_weight,
    output_weight,
    second_gain,
    hidden_weight,
    return_weight,
):
    rows, width = inputs.shape[1:]
    n_seq = lax.axis_size("seq")
    length = rows * n_seq
    base = lax.axis_index("seq") * rows
    base_ref = jnp.reshape(base, (1,)).astype(jnp.int32)
    inputs = inputs.reshape(rows, width)
    cotangent = cotangent.reshape(rows, width)
    if n_seq == 2 and rows > SPAN:
        halo_inputs, far_inputs = turned(inputs[rows - SPAN :], 1), turned(inputs[: rows - SPAN], 1)
    else:
        others = jnp.concatenate([turned(inputs, shift) for shift in range(1, n_seq)], axis=0)
        halo_inputs, far_inputs = others[length - rows - SPAN :], others[: length - rows - SPAN]
    gain_rows = lambda gain: jnp.broadcast_to(gain, (8, width))
    ask_weight, memory_weight, blend_weight = lay_weights(
        query_weight, key_weight, value_weight, gate_weight, output_weight
    )
    chunk = own_chunk()
    index = (neighbours.reshape(rows * NEAR) + (length - rows - base)) % length

    normed, ask, own = project(inputs, gain_rows(first_gain), empty_rows.reshape(1, rows), ask_weight, memory_weight)
    split = SPAN if rows == 2 * SPAN else rows
    attended = ()
    if split < rows:
        attended = local_attention(base_ref, ask, own, own, split, rows)
    halo_normed, halo = project_memory(halo_inputs, gain_rows(first_gain), memory_weight)
    local_out, log_total = local_attention(base_ref, ask, halo, own, 0, split, attended)
    far_normed, far_memory = project_memory(far_inputs, gain_rows(first_gain), memory_weight)
    near, weight, blended = retrieve(index, far_memory, halo, own, ask, local_out)

    resid, active, hidden_grad, early_own, early_send = hidden_layer(
        chunk, inputs, cotangent, blended, blend_weight, gain_rows(second_gain), hidden_weight, return_weight
    )
    early = scatter_start(early_own, early_send)
    outputs, resid_grad, blended_grad, second_gain_grad, blend_grad = resid_layer(
        resid, cotangent, blended, active, hidden_grad, blend_weight, gain_rows(second_gain), hidden_weight, return_weight
    )
    early = scatter_level(early, 1, after=[second_gain_grad])
    local_grad, inner, partial, far = retrieve_back(
        index, blended_grad, ask, local_out, near, weight, length, after=[early[0]]
    )
    early = scatter_level(early, 2, after_far=[inner])
    steps = list(range(H // BACK_HEADS))
    quarter = len(steps) // 4
    back = functools.partial(
        local_attention_back, base_ref, ask, halo, own, local_grad, log_total, inner, partial, far
    )
    grads = back(steps[:quarter], after=[early[0]])
    early_total = scatter_finish(early, after_far=[grads[0]])
    early = gather_level(early_total, 2)
    grads = back(steps[quarter : 2 * quarter], grads, after=[early_total])
    early_total = join_pieces(early, after_far=[grads[0]])
    early = gather_level(early_total, 1)
    ask_grad, memory_grad = back(steps[2 * quarter :], grads, after=[early_total])
    own_grad, others_grad, first_gain_grad = normed_back(
        inputs, far_inputs, halo_inputs, ask_grad, memory_grad, ask_weight, memory_weight
    )
    arrived = [turned(others_grad[(k - 1) * rows : k * rows], n_seq - k) for k in range(1, n_seq)]
    own_late, send_late = pack_late(
        chunk, far_normed, halo_normed, normed, ask_grad, memory_grad, first_gain_grad, second_gain_grad, blend_grad,
        after=[],
    )
    late = scatter_start(own_late, send_late)
    early_own = join_pieces(early, after=[own_late])
    early_other = swapped(early_own, level_groups()[0][0], 1)
    late = scatter_level(late, 1, EXTRA_ROWS, after=[early_own])
    late = scatter_level(late, 2, EXTRA_ROWS)
    input_grad, token = whole_call(
        input_back_kernel, "input_back", inputs, gain_rows(first_gain), resid_grad, own_grad, *arrived,
        outs=[((rows, width), BF16), TOKEN], after=[late[0]],
    )
    late_total = scatter_finish(late, after=[token])
    extra = late_total[LATE_ROWS:]
    late_total = late_total[:LATE_ROWS]
    late = gather_level(late_total, 2)
    return_sum, hidden_sum, token = unpack_early(
        chunk, early_own, early_other, return_weight.shape, hidden_weight.shape, after=[late_total]
    )
    late_total = join_pieces(late, after=[token])
    late = gather_level(late_total, 1)
    late_own = join_pieces(late)
    late_other = swapped(late_own, level_groups()[0][0], 1)
    query_sum, key_sum, value_sum, output_sum, gate_sum, first_sum, second_sum = unpack_late(chunk, late_own, late_other, extra)
    return (
        outputs.reshape(1, rows, width),
        input_grad.reshape(1, rows, width),
        first_sum.reshape(width),
        query_sum,
        key_sum,
        value_sum,
        gate_sum.T,
        output_sum,
        second_sum.reshape(width),
        hidden_sum,
        return_sum,
    )


def solution(mesh):
    split = P("dp", "seq", None)
    in_specs = (split, split, split, P("dp", "seq")) + (P(),) * 9
    out_specs = (split, split) + (P(),) * 9
    return jax.shard_map(body, mesh=mesh, in_specs=in_specs, out_specs=out_specs, check_vma=False)
```

```python
import functools
import math

import jax
import jax.numpy as jnp
from jax import lax
from jax.experimental import pallas as pl
from jax.experimental.pallas import tpu as pltpu
from jax.sharding import PartitionSpec as P

H = 8
HD = 64
LANES = 2 * HD
WIDE = H * LANES
SPAN = 512
NEAR = 4
SCALE = HD ** (-0.5)
NEG = -1e30
SHUT = 100.0
EPS = 1e-06
MIB = 1024 * 1024

F32 = jnp.float32
BF16 = jnp.bfloat16
TOKEN = ((8, LANES), F32)


def dot(left, right):
    return jnp.dot(left, right, preferred_element_type=F32)


def dot_back(left, right):
    return lax.dot_general(left, right, (((1,), (1,)), ((), ())), preferred_element_type=F32)


def rows_dot(left, right):
    return lax.dot_general(left, right, (((0,), (0,)), ((), ())), preferred_element_type=F32)


def cost_of(microseconds):
    return pl.CostEstimate(flops=int(microseconds * 1e9), bytes_accessed=int(microseconds * 3e6), transcendentals=0)


def block_rows(rows):
    return 256 if rows % 256 == 0 else rows


def head_lanes(h):
    return slice(h * LANES, (h + 1) * LANES)


TILE = 256
REACH = SPAN + TILE
HEADS = 2
BACK_HEADS = 1
CHUNKS = 32
EARLY_ROWS = 128
LATE_ROWS = 64
EXTRA_ROWS = 16


def window_parts(first):
    before = max(SPAN - first, 0)
    parts = [(True, SPAN - before, before)] if before else []
    return parts + [(False, max(first - SPAN, 0), REACH - before)]


def window_keys(halo_ref, own_ref, first, lanes):
    return [(halo_ref if halo else own_ref)[at : at + n, lanes] for halo, at, n in window_parts(first)]


def window_bias(query_axis):
    shape = (TILE, REACH) if query_axis == 0 else (REACH, TILE)
    query = lax.broadcasted_iota(jnp.int32, shape, query_axis)
    key = lax.broadcasted_iota(jnp.int32, shape, 1 - query_axis)
    return jnp.where((key > query) & (key <= query + SPAN), 0.0, NEG)


def masked(scores, bias, first, base, key_axis):
    cut = lambda v, i, j: v[i:j] if key_axis == 0 else v[:, i:j]
    out = []
    for at in range(0, REACH, TILE):
        part = cut(scores, at, at + TILE)
        if at == 0 or at == SPAN:
            part = part + cut(bias, at, at + TILE)
        if first + at < SPAN:
            part = part + jnp.where(base + first + at >= SPAN, 0.0, NEG)
        out.append(part)
    return jnp.concatenate(out, axis=key_axis)


def pipelined(work, before, middle, after):
    ready = before(*work[0])
    held = None
    for k, item in enumerate(work):
        following = before(*work[k + 1]) if k + 1 < len(work) else None
        done = middle(item, ready)
        if held is not None:
            after(*held)
        held, ready = (item, done), following
    after(*held)


def local_kernel(start, base_ref, ask_ref, halo_ref, own_ref, out_ref, total_ref, bias_ref, totals):
    step = pl.program_id(0)
    base = base_ref[0]

    @pl.when(step == 0)
    def fill():
        bias_ref[...] = window_bias(0)

    lane = lax.broadcasted_iota(jnp.int32, (TILE, LANES), 1)

    def scores(at, g):
        query = jnp.where(lane < HD, ask_ref[at : at + TILE, head_lanes(g)], 0.0).astype(BF16)
        return jnp.concatenate([dot_back(query, k) for k in window_keys(halo_ref, own_ref, start + at, head_lanes(g))], axis=1)

    def softmax(item, raw):
        raw = masked(raw, bias_ref, start + item[0], base, 1)
        top = jnp.max(raw, axis=1, keepdims=True)
        expo = jnp.exp(raw - top)
        return expo.astype(BF16), jnp.sum(expo, axis=1, keepdims=True), top

    def finish(item, done):
        at, g = item
        expo, total, top = done
        out, column = None, 0
        for keys in window_keys(halo_ref, own_ref, start + at, head_lanes(g)):
            term = dot(expo[:, column : column + keys.shape[0]], keys)
            column += keys.shape[0]
            out = term if out is None else out + term
        here = slice(at, at + TILE)
        out_ref[here, head_lanes(g)] = (out * (1.0 / total)).astype(BF16)
        totals[here, :] = jnp.where(lane == step * HEADS + g, top + jnp.log(total), totals[here, :])

    pipelined([(at, g) for g in range(HEADS) for at in range(0, ask_ref.shape[0], TILE)], scores, softmax, finish)

    @pl.when(step == H // HEADS - 1)
    def turn():
        for at in range(0, ask_ref.shape[0], LANES):
            total_ref[:, at : at + LANES] = totals[at : at + LANES, :].T[:H, :]


def local_attention(base, ask, halo, own, start, stop, earlier=(), after=()):
    rows = ask.shape[0]
    count = stop - start
    wide = HEADS * LANES
    part = lambda h: (start // count, h)
    held = [pl.BlockSpec(memory_space=pl.ANY)] * (len(earlier) + len(after))
    return pl.pallas_call(
        lambda *refs: local_kernel(start, *refs[:4], *refs[4 + len(held) :]),
        grid=(H // HEADS,),
        in_specs=[
            pl.BlockSpec(memory_space=pltpu.SMEM),
            pl.BlockSpec((count, wide), part),
            pl.BlockSpec((SPAN, wide), lambda h: (0, h)),
            pl.BlockSpec((rows, wide), lambda h: (0, h)),
        ]
        + held,
        out_specs=[pl.BlockSpec((count, wide), part), pl.BlockSpec((H, count), lambda h: (0, start // count))],
        out_shape=[pltpu.HBM((rows, WIDE), BF16), pltpu.HBM((H, rows), F32)],
        scratch_shapes=[pltpu.VMEM((TILE, REACH), F32), pltpu.VMEM((count, LANES), F32)],
        input_output_aliases={4 + k: k for k in range(len(earlier))},
        compiler_params=pltpu.CompilerParams(vmem_limit_bytes=12 * MIB),
        cost_estimate=cost_of(count / 80),
        name="local_attention",
    )(base, *in_hbm(ask, halo, own, *earlier), *after)


def local_back_kernel(
    first_step, base_ref, ask_ref, halo_ref, own_ref, grad_ref, total_ref, inner_ref, partial_ref, far_grad_ref,
    ask_grad_ref, memory_grad_ref, sums_ref, bias_ref,
):
    step = pl.program_id(0) + first_step
    rows = ask_ref.shape[0]
    base = base_ref[0]
    start = far_grad_ref.shape[0] - rows - SPAN

    @pl.when(step == first_step)
    def fill():
        bias_ref[...] = window_bias(1)

    left = left_lanes(TILE)
    sums_ref[...] = far_grad_ref[...].astype(F32)

    def query_of(first, g):
        return jnp.where(left, ask_ref[first : first + TILE, head_lanes(g)], 0.0).astype(BF16)

    def products(first, g):
        keys = window_keys(halo_ref, own_ref, first, head_lanes(g))
        query, grad = query_of(first, g), grad_ref[first : first + TILE, head_lanes(g)]
        join = lambda rows: jnp.concatenate([dot_back(k, rows) for k in keys], axis=0)
        return join(query), join(grad)

    def score_grads(item, done):
        first, g = item
        scores, prob_grad = done
        here = slice(first, first + TILE)
        total = total_ref[pl.ds(step * BACK_HEADS + g, 1), here]
        inner = inner_ref[pl.ds(step * BACK_HEADS + g, 1), here]
        probs = jnp.exp(masked(scores, bias_ref, first, base, 0) - total)
        return (probs * (prob_grad - inner)).astype(BF16), probs.astype(BF16)

    def finish(item, done):
        first, g = item
        score_grad, probs = done
        here, lanes = slice(first, first + TILE), head_lanes(g)
        query_grad, row = None, 0
        for keys in window_keys(halo_ref, own_ref, first, lanes):
            term = rows_dot(score_grad[row : row + keys.shape[0]], keys)
            row += keys.shape[0]
            query_grad = term if query_grad is None else query_grad + term
        sums_ref[start + first : start + first + REACH, lanes] += dot(score_grad, query_of(first, g)) + dot(
            probs, grad_ref[here, lanes]
        )
        partial = partial_ref[here, lanes].astype(F32)
        ask_grad_ref[here, lanes] = (partial + jnp.where(left, query_grad * SCALE, 0.0)).astype(BF16)

    pipelined([(first, g) for g in range(BACK_HEADS) for first in range(0, rows, TILE)], products, score_grads, finish)
    memory_grad_ref[...] = sums_ref[...].astype(BF16)


def local_attention_back(base, ask, halo, own, grad, total, inner, partial, far_grad, steps, earlier=(), after=()):
    rows = ask.shape[0]
    length = far_grad.shape[0]
    first = steps[0]
    head = lambda n: pl.BlockSpec((n, BACK_HEADS * LANES), lambda h: (0, h + first))
    flat = pl.BlockSpec((H, rows), lambda h: (0, 0))
    held = [pl.BlockSpec(memory_space=pl.ANY)] * (len(earlier) + len(after))
    return pl.pallas_call(
        lambda *refs: local_back_kernel(first, *refs[:9], *refs[9 + len(held) :]),
        grid=(len(steps),),
        in_specs=[
            pl.BlockSpec(memory_space=pltpu.SMEM),
            head(rows),
            pl.BlockSpec((SPAN, BACK_HEADS * LANES), lambda h: (0, h + first)),
            head(rows),
            head(rows),
            flat,
            flat,
            head(rows),
            head(length),
        ]
        + held,
        out_specs=[head(rows), head(length)],
        out_shape=[
            pltpu.HBM((rows, WIDE), BF16),
            pltpu.HBM((length, WIDE), BF16),
        ],
        scratch_shapes=[pltpu.VMEM((length, BACK_HEADS * LANES), F32), pltpu.VMEM((REACH, TILE), F32)],
        input_output_aliases={9 + k: k for k in range(len(earlier))},
        compiler_params=pltpu.CompilerParams(vmem_limit_bytes=20 * MIB),
        cost_estimate=cost_of(0.3),
        name="local_attention_back",
    )(base, *in_hbm(ask, halo, own, grad, total, inner, partial, far_grad, *earlier), *after)


def token_tile(ref, token):
    return ref[pl.ds(pl.multiple_of(token * H, H), H), :]


def put_heads(ref, h, values):
    ref[pl.ds(h, values.shape[0], stride=H), :] = values


def take_heads(ref, h, count):
    return ref[pl.ds(h, count, stride=H), :]


def left_lanes(count):
    return lax.broadcasted_iota(jnp.int32, (count, LANES), 1) < HD


def build_table(table, *refs):
    block, base = 128, 0
    for ref in refs:

        def rows(k, carry, ref=ref, base=base):
            here = pl.ds(pl.multiple_of(k * block, block), block)
            for h in range(H):
                there = pl.ds(pl.multiple_of((base + k * block) * H, block * H) + h, block, stride=H)
                table[there, :] = ref[here, head_lanes(h)].astype(F32)
            return carry

        lax.fori_loop(0, ref.shape[0] // block, rows, 0)
        base += ref.shape[0]


def row_sums(values):
    return jnp.sum(values, axis=1, keepdims=True)


def softmax_over(match):
    top = functools.reduce(jnp.maximum, match)
    expo = [jnp.exp(m - top) for m in match]
    scale = 1.0 / functools.reduce(jnp.add, expo)
    return [e * scale for e in expo]


TOKENS = 128
GROUP = 4


def lane_sums(values):
    return dot(values.astype(BF16), jnp.ones((LANES, LANES), BF16))


def gather_group(index_ref, table, near_rows, first, group):
    for k in range(GROUP):
        t = group * GROUP + k
        for j in range(NEAR):
            near_rows[j, t * H : (t + 1) * H, :] = token_tile(table, index_ref[(first + t) * NEAR + j])


def scatter_group(index_ref, sums, terms, first, group):
    for k in range(GROUP):
        t = group * GROUP + k
        for j in range(NEAR):
            there = pl.ds(pl.multiple_of(index_ref[(first + t) * NEAR + j] * H, H), H)
            held = sums[j % len(sums)]
            held[there, :] = held[there, :] + terms[j, t * H : (t + 1) * H, :]


def retrieve_kernel(
    index_ref, far_ref, halo_ref, own_ref, ask_ref, local_ref, near_ref, weight_ref, blended_ref,
    table, ask_rows, out_rows, near_rows,
):
    step = pl.program_id(0)
    count = ask_ref.shape[0]
    first = step * count

    @pl.when(step == 0)
    def build():
        build_table(table, far_ref, halo_ref, own_ref)

    for h in range(H):
        put_heads(ask_rows, h, ask_ref[:, head_lanes(h)].astype(F32))
    left = left_lanes(GROUP * H)
    groups = count // GROUP
    rows_of = lambda group: slice(group * GROUP * H, (group + 1) * GROUP * H)

    def match(group):
        if group + 1 < groups:
            gather_group(index_ref, table, near_rows, first, group + 1)
        here = rows_of(group)
        query = jnp.where(left, ask_rows[here, :], 0.0)
        return [(lane_sums if j > 1 else row_sums)(near_rows[j, here, :] * query) for j in range(NEAR)]

    def weights(item, done):
        return softmax_over(done)

    def recall(item, weight):
        here = rows_of(item[0])
        out_rows[here, :] = functools.reduce(jnp.add, [weight[j] * near_rows[j, here, :] for j in range(NEAR)])
        for j in range(NEAR):
            weight_ref[j, here, :] = weight[j].astype(BF16)
            near_ref[j, here, :] = near_rows[j, here, :].astype(BF16)

    gather_group(index_ref, table, near_rows, first, 0)
    pipelined([(group,) for group in range(groups)], match, weights, recall)
    left = left_lanes(count)
    for h in range(H):
        lanes = head_lanes(h)
        local = local_ref[:, lanes].astype(F32)
        mix = 1.0 - jax.nn.sigmoid(ask_ref[:, lanes].astype(F32))
        blended = local + mix * (take_heads(out_rows, h, count) - local)
        blended_ref[:, lanes] = jnp.where(left, 0.0, blended).astype(BF16)


def retrieve(index, far, halo, own, ask, local):
    rows = ask.shape[0]
    length = far.shape[0] + halo.shape[0] + rows
    count = min(TOKENS, rows)
    wide = pl.BlockSpec((count, WIDE), lambda c: (c, 0))
    tall = pl.BlockSpec((NEAR, count * H, LANES), lambda c: (0, c, 0))
    return pl.pallas_call(
        retrieve_kernel,
        grid=(rows // count,),
        in_specs=[
            pl.BlockSpec(memory_space=pltpu.SMEM),
            pl.BlockSpec(far.shape, lambda c: (0, 0)),
            pl.BlockSpec(halo.shape, lambda c: (0, 0)),
            pl.BlockSpec(own.shape, lambda c: (0, 0)),
            wide,
            wide,
        ],
        out_specs=[tall, tall, wide],
        out_shape=[
            pltpu.HBM((NEAR, rows * H, LANES), BF16),
            pltpu.HBM((NEAR, rows * H, LANES), BF16),
            jax.ShapeDtypeStruct((rows, WIDE), BF16),
        ],
        scratch_shapes=[
            pltpu.VMEM((length * H, LANES), F32),
            pltpu.VMEM((count * H, LANES), F32),
            pltpu.VMEM((count * H, LANES), F32),
            pltpu.VMEM((NEAR, count * H, LANES), F32),
        ],
        compiler_params=pltpu.CompilerParams(vmem_limit_bytes=28 * MIB),
        cost_estimate=cost_of(12),
        name="retrieve",
    )(index, *in_hbm(far, halo, own, ask, local))


def retrieve_back_kernel(
    index_ref, grad_ref, ask_ref, local_ref, near_ref, weight_ref,
    local_grad_ref, inner_ref, partial_ref, far_ref,
    sums_even, sums_odd, ask_rows, grad_rows, out_rows, mixed, terms,
):
    step = pl.program_id(0)
    count = ask_ref.shape[0]
    first = step * count
    length = far_ref.shape[0]

    @pl.when(step == 0)
    def clear():
        block = 1024

        def rows(k, carry):
            here = pl.ds(pl.multiple_of(k * block, block), block)
            sums_even[here, :] = jnp.zeros((block, LANES), F32)
            sums_odd[here, :] = jnp.zeros((block, LANES), F32)
            return carry

        lax.fori_loop(0, length * H // block, rows, 0)

    left = left_lanes(count)
    lane = lax.broadcasted_iota(jnp.int32, (count, LANES), 1)
    inner_all = jnp.zeros((count, LANES), F32)
    for h in range(H):
        lanes = head_lanes(h)
        grad = grad_ref[:, lanes].astype(F32)
        ask = ask_ref[:, lanes].astype(F32)
        mix = 1.0 - jax.nn.sigmoid(ask)
        inner = row_sums(grad * local_ref[:, lanes].astype(F32))
        inner_all = jnp.where(lane == HD + h, inner - mix * inner, inner_all)
        mixed[:, lanes] = mix * inner
        local_grad_ref[:, lanes] = (grad - mix * grad).astype(BF16)
        put_heads(ask_rows, h, jnp.where(left, ask, mix))
        put_heads(grad_rows, h, grad)
    inner_ref[...] = inner_all.T[HD : HD + H, :]
    groups = count // GROUP
    left_tile = left_lanes(GROUP * H)
    sums = (sums_even, sums_odd)
    rows_of = lambda group: slice(group * GROUP * H, (group + 1) * GROUP * H)

    def weight_grads(group):
        here = rows_of(group)
        grad = ask_rows[here, :] * grad_rows[here, :]
        return [(lane_sums if j > 1 else row_sums)(near_ref[j, here, :].astype(F32) * grad) for j in range(NEAR)]

    def match_grads(item, weight_grad):
        here = rows_of(item[0])
        weight = [weight_ref[j, here, :].astype(F32) for j in range(NEAR)]
        inner = functools.reduce(jnp.add, [w * g for w, g in zip(weight, weight_grad)])
        match_grad = [w * (g - inner) for w, g in zip(weight, weight_grad)]
        query_grad = functools.reduce(
            jnp.add, [g * near_ref[j, here, :].astype(F32) for j, g in enumerate(match_grad)]
        )
        out_rows[here, :] = jnp.where(left_tile, query_grad * SCALE, inner)
        ask = ask_rows[here, :]
        source = jnp.where(left_tile, ask, ask * grad_rows[here, :])
        for j in range(NEAR):
            terms[j, here, :] = jnp.where(left_tile, match_grad[j], weight[j]) * source

    def add_terms(item, done):
        scatter_group(index_ref, sums, terms, first, item[0])

    pipelined([(group,) for group in range(groups)], weight_grads, match_grads, add_terms)
    for h in range(H):
        lanes = head_lanes(h)
        tile = take_heads(out_rows, h, count)
        gate = jax.nn.sigmoid(ask_ref[:, lanes].astype(F32))
        partial_ref[:, lanes] = jnp.where(left, tile, (gate / HD) * (mixed[:, lanes] - tile)).astype(BF16)

    @pl.when(step == pl.num_programs(0) - 1)
    def finish():
        block = 128

        def rows(k, carry):
            here = pl.ds(pl.multiple_of(k * block, block), block)
            for h in range(H):
                there = pl.ds(pl.multiple_of(k * (block * H), block * H) + h, block, stride=H)
                far_ref[here, head_lanes(h)] = (sums_even[there, :] + sums_odd[there, :]).astype(BF16)
            return carry

        lax.fori_loop(0, length // block, rows, 0)


def retrieve_back(index, grad, ask, local, near, weight, length, after=()):
    rows = ask.shape[0]
    count = min(TOKENS, rows)
    wide = pl.BlockSpec((count, WIDE), lambda c: (c, 0))
    tall = pl.BlockSpec((NEAR, count * H, LANES), lambda c: (0, c, 0))
    return pl.pallas_call(
        lambda *refs: retrieve_back_kernel(*refs[:6], *refs[6 + len(after) :]),
        grid=(rows // count,),
        in_specs=[
            pl.BlockSpec(memory_space=pltpu.SMEM),
            wide,
            wide,
            wide,
            tall,
            tall,
        ]
        + [pl.BlockSpec(memory_space=pl.ANY)] * len(after),
        out_specs=[
            wide,
            pl.BlockSpec((H, count), lambda c: (0, c)),
            wide,
            pl.BlockSpec((length, WIDE), lambda c: (0, 0)),
        ],
        out_shape=[
            pltpu.HBM((rows, WIDE), BF16),
            pltpu.HBM((H, rows), F32),
            pltpu.HBM((rows, WIDE), BF16),
            pltpu.HBM((length, WIDE), BF16),
        ],
        scratch_shapes=[
            pltpu.VMEM((length * H, LANES), F32),
            pltpu.VMEM((length * H, LANES), F32),
            pltpu.VMEM((count * H, LANES), F32),
            pltpu.VMEM((count * H, LANES), F32),
            pltpu.VMEM((count * H, LANES), F32),
            pltpu.VMEM((count, WIDE), F32),
            pltpu.VMEM((NEAR, count * H, LANES), F32),
        ],
        compiler_params=pltpu.CompilerParams(vmem_limit_bytes=40 * MIB),
        cost_estimate=cost_of(24),
        name="retrieve_back",
    )(index, *in_vmem(grad), *in_hbm(ask, local, near, weight), *after)


def turned(block, shift):
    size = lax.axis_size("seq")
    return lax.ppermute(block, "seq", [((i + shift) % size, i) for i in range(size)])


def index_bits(axis):
    return [(axis, b) for b in range(lax.axis_size(axis).bit_length() - 1)]


def level_groups():
    dp, seq = index_bits("dp"), index_bits("seq")
    return [dp[:1], dp[1:3], seq[:1] + dp[3:4]], dp[4:] + seq[1:]


def own_place(group):
    place = 0
    for k, (axis, bit) in enumerate(group):
        place = place + (((lax.axis_index(axis) >> bit) & 1) << k)
    return place


def own_chunk():
    chunk = 0
    for group in level_groups()[0]:
        chunk = (chunk << len(group)) + own_place(group)
    return jnp.reshape(chunk, (1,)).astype(jnp.int32)


def swapped(block, group, distance):
    flips = {"dp": 0, "seq": 0}
    for k, (axis, bit) in enumerate(group):
        if (distance >> k) & 1:
            flips[axis] |= 1 << bit
    n_dp, n_seq = lax.axis_size("dp"), lax.axis_size("seq")
    if not flips["seq"]:
        return lax.ppermute(block, "dp", [(i, i ^ flips["dp"]) for i in range(n_dp)])
    if not flips["dp"]:
        return lax.ppermute(block, "seq", [(i, i ^ flips["seq"]) for i in range(n_seq)])
    route = [(i, (i // n_seq ^ flips["dp"]) * n_seq + (i % n_seq ^ flips["seq"])) for i in range(n_dp * n_seq)]
    return lax.ppermute(block, ("dp", "seq"), route)


def in_hbm(*arrays):
    return [pltpu.with_memory_space_constraint(v, pltpu.HBM) for v in arrays]


def in_vmem(*arrays):
    return [pltpu.with_memory_space_constraint(v, pltpu.VMEM) for v in arrays]


def whole_call(kernel, name, *operands, outs, scratch=(), after=(), cost=0.3, spare=4, resident=(), streamed=(), inside=(), after_far=()):
    count, late = len(operands), len(streamed)
    operands = [in_hbm(v)[0] if k in streamed else v for k, v in enumerate(operands)]
    operands = [in_vmem(v)[0] if k in inside else v for k, v in enumerate(operands)]

    def place(k, v):
        if v.dtype == jnp.int32:
            return pltpu.SMEM
        return pltpu.HBM if k in streamed else pltpu.VMEM

    held = [pltpu.VMEM(operands[k].shape, operands[k].dtype) for k in streamed]
    shapes = [(v.shape, v.dtype) for k, v in enumerate(operands) if k not in inside]
    shapes += [(v.shape, v.dtype) for v in scratch]
    shapes += [out for k, out in enumerate(outs) if k not in resident]
    size = sum(math.prod(shape) * jnp.dtype(dtype).itemsize for shape, dtype in shapes)

    def wrapped(*refs):
        ins, rest = list(refs[:count]), refs[count + len(after) + len(after_far) :]
        if not late:
            return kernel(*ins, *rest)
        rest, copies = rest[: -2 * late], {}
        for n, k in enumerate(streamed):
            held_ref, sem = refs[-2 * late + n], refs[-late + n]
            copies[k] = pltpu.make_async_copy(ins[k], held_ref, sem)
            copies[k].start()
            ins[k] = held_ref
        return kernel(lambda k: copies[k].wait(), *ins, *rest)

    return pl.pallas_call(
        wrapped,
        in_specs=[pl.BlockSpec(memory_space=place(k, v)) for k, v in enumerate(operands)]
        + [pl.BlockSpec(memory_space=pl.ANY)] * len(after)
        + [pl.BlockSpec(memory_space=pltpu.HBM)] * len(after_far),
        out_specs=[pl.BlockSpec(memory_space=pltpu.VMEM)] * len(outs),
        out_shape=[
            pltpu.VMEM(shape, dtype) if k in resident else jax.ShapeDtypeStruct(shape, dtype)
            for k, (shape, dtype) in enumerate(outs)
        ],
        scratch_shapes=list(scratch) + held + [pltpu.SemaphoreType.DMA(())] * late,
        compiler_params=pltpu.CompilerParams(vmem_limit_bytes=size + spare * MIB),
        cost_estimate=cost_of(cost),
        name=name,
    )(*operands, *after, *in_hbm(*after_far))


def add_pieces(own, arrived, pieces, extra=0, **order):
    rows, width = own.shape
    count = (rows - extra) // pieces

    def kernel(*refs):
        terms, outs = refs[: 1 + len(arrived)], refs[1 + len(arrived) :]

        def total(here):
            values = terms[0][here, :].astype(F32)
            for term in terms[1:]:
                values = values + term[here, :].astype(F32)
            return values.astype(BF16)

        for k, out in enumerate(outs):
            out[:count, :] = total(slice(k * count, (k + 1) * count))
        if extra:
            last = total(slice(rows - extra, rows))
            for out in outs:
                out[count:, :] = last

    outs = [((count + extra, width), BF16)] * pieces
    return whole_call(kernel, "add_pieces", own, *arrived, outs=outs, **order)


def join_pieces(pieces, **order):
    count, width = pieces[0].shape

    def kernel(*refs):
        for k, ref in enumerate(refs[:-1]):
            refs[-1][k * count : (k + 1) * count, :] = ref[...]

    return whole_call(kernel, "join_pieces", *pieces, outs=[((count * len(pieces), width), BF16)], **order)[0]


def scatter_start(own, send):
    return own, [swapped(send, level_groups()[0][0], 1)]


def scatter_level(held, level, extra=0, **order):
    own, arrived = held
    group = level_groups()[0][level]
    pieces = add_pieces(own, arrived, 2 ** len(group), extra, **order)
    return pieces[0], [swapped(piece, group, d) for d, piece in enumerate(pieces) if d]


def scatter_finish(held, **order):
    total = add_pieces(*held, 1, **order)[0]
    for bit in level_groups()[1]:
        total = add_pieces(total, [swapped(total, [bit], 1)], 1)[0]
    return total


def gather_level(total, level):
    group = level_groups()[0][level]
    return [total] + [swapped(total, group, d) for d in range(1, 2 ** len(group))]


def rms_unit(values):
    scale = lax.rsqrt(jnp.mean(values * values, axis=-1, keepdims=True) + EPS)
    return values * scale, scale


def rms_back(unit, scale, grad):
    return scale * (grad - unit * jnp.mean(grad * unit, axis=-1, keepdims=True))


def lay_weights_kernel(wait, query_ref, key_ref, value_ref, gate_ref, output_ref, ask_ref, memory_ref, blend_ref):
    width = query_ref.shape[0]
    gate = gate_ref[...].astype(F32).T
    for k in (0, 1, 2, 4):
        wait(k)
    for h in range(H):
        here = slice(h * HD, (h + 1) * HD)
        column = jnp.broadcast_to(gate[:, h : h + 1], (width, HD)).astype(BF16)
        ask_ref[:, head_lanes(h)] = jnp.concatenate([query_ref[:, here], column], axis=1)
        memory_ref[:, head_lanes(h)] = jnp.concatenate([key_ref[:, here], value_ref[:, here]], axis=1)
        blend_ref[h * LANES : h * LANES + HD, :] = jnp.zeros((HD, width), BF16)
        blend_ref[h * LANES + HD : (h + 1) * LANES, :] = output_ref[here, :]


def lay_weights(query_weight, key_weight, value_weight, gate_weight, output_weight):
    width = query_weight.shape[0]
    wide = ((width, WIDE), BF16)
    return whole_call(
        lay_weights_kernel,
        "lay_weights",
        query_weight,
        key_weight,
        value_weight,
        gate_weight.T,
        output_weight,
        outs=[wide, wide, ((WIDE, width), BF16)],
        streamed=(0, 1, 2, 4),
    )


def project_kernel(inputs_ref, gain_ref, empty_ref, ask_weight_ref, memory_weight_ref, normed_ref, ask_ref, memory_ref):
    normed = (rms_unit(inputs_ref[...].astype(F32))[0] * gain_ref[0:1, :]).astype(BF16)
    normed_ref[...] = normed
    memory_ref[...] = dot(normed, memory_weight_ref[...]).astype(BF16)
    if ask_ref is not None:
        left = (lax.broadcasted_iota(jnp.int32, (1, WIDE), 1) % LANES) < HD
        ask = dot(normed, ask_weight_ref[...])
        block = normed.shape[0]
        row = lax.broadcasted_iota(jnp.int32, (block, block), 0)
        column = lax.broadcasted_iota(jnp.int32, (block, block), 1)
        here = pl.ds(pl.multiple_of(pl.program_id(0) * block, block), block)
        empty = jnp.sum(jnp.where(row == column, empty_ref[:, here].astype(F32), 0.0), axis=1, keepdims=True)
        gate = jnp.where(empty > 0.0, SHUT, ask)
        ask_ref[...] = jnp.where(left, ask * SCALE, gate).astype(BF16)


def row_blocks_call(kernel, name, *operands, outs, cost):
    rows = operands[0].shape[0]
    block = block_rows(rows)
    rows_spec = lambda width: pl.BlockSpec((block, width), lambda k: (k, 0))
    whole = lambda v: pl.BlockSpec(v.shape, lambda k: (0, 0))
    return pl.pallas_call(
        kernel,
        grid=(rows // block,),
        in_specs=[rows_spec(operands[0].shape[1])] + [whole(v) for v in operands[1:]],
        out_specs=[rows_spec(width) for width in outs],
        out_shape=[pltpu.HBM((rows, width), BF16) for width in outs],
        compiler_params=pltpu.CompilerParams(vmem_limit_bytes=14 * MIB),
        cost_estimate=cost_of(cost),
        name=name,
    )(*operands)


def project(inputs, gain, empty, ask_weight, memory_weight):
    width = inputs.shape[1]
    return row_blocks_call(
        project_kernel, "project", inputs, gain, empty, ask_weight, memory_weight, outs=[width, WIDE, WIDE], cost=3
    )


def project_memory(inputs, gain, memory_weight):
    def kernel(inputs_ref, gain_ref, weight_ref, normed_ref, memory_ref):
        project_kernel(inputs_ref, gain_ref, None, None, weight_ref, normed_ref, None, memory_ref)

    return row_blocks_call(
        kernel, "project_memory", inputs, gain, memory_weight, outs=[inputs.shape[1], WIDE], cost=2
    )


ROOT = 0.7978845608028654
CUBE = 0.044715


def gelu_and_slope(x):
    square = x * x
    half = 0.5 + 0.5 * jnp.tanh(x * (ROOT + (ROOT * CUBE) * square))
    value = x * half
    slope = half + (value * (1.0 - half)) * (2.0 * ROOT + (6.0 * ROOT * CUBE) * square)
    return value, slope


def hidden_kernel(
    wait, chunk_ref, inputs_ref, cotangent_ref, blended_ref, blend_weight_ref, gain_ref, hidden_weight_ref, return_weight_ref,
    resid_ref, active, hidden_grad, own_ref, send_ref,
    normed, return_sums, hidden_sums,
):
    rows, width = inputs_ref.shape
    hidden = hidden_weight_ref.shape[1]
    block = block_rows(rows)
    gain = gain_ref[0:1, :]
    columns = [slice(at, at + width) for at in range(0, hidden, width)]
    wait(1)

    def row_block(k, carry):
        here = pl.ds(pl.multiple_of(k * block, block), block)
        resid = inputs_ref[here, :].astype(F32) + dot(blended_ref[here, :], blend_weight_ref[...])
        resid_ref[here, :] = resid
        normed_here = (rms_unit(resid)[0] * gain).astype(BF16)
        normed[here, :] = normed_here

        @pl.when(k == 0)
        def weights():
            for n in (2, 6, 7):
                wait(n)

        cotangent = cotangent_ref[here, :]

        def products(lanes):
            return dot(normed_here, hidden_weight_ref[:, lanes]), dot_back(cotangent, return_weight_ref[lanes, :])

        def activate(item, done):
            value, slope = gelu_and_slope(done[0])
            return value.astype(BF16), (done[1] * slope).astype(BF16)

        def keep(item, done):
            active[here, item[0]] = done[0]
            hidden_grad[here, item[0]] = done[1]

        pipelined([(lanes,) for lanes in columns], products, activate, keep)
        return carry

    lax.fori_loop(0, rows // block, row_block, 0)

    def column_block(k, carry):
        lanes = pl.ds(pl.multiple_of(k * width, width), width)
        return_sums[lanes, :] = rows_dot(active[:, lanes], cotangent_ref[...]).astype(BF16)
        hidden_sums[:, lanes] = rows_dot(normed[...], hidden_grad[:, lanes]).astype(BF16)
        return carry

    lax.fori_loop(0, hidden // width, column_block, 0)
    tall, flat = hidden // CHUNKS, width // CHUNKS

    def pack(r, carry):
        for half, out in enumerate((own_ref, send_ref)):
            chunk = chunk_ref[0] ^ (r + half * (CHUNKS // 2))
            rows_at = lambda offset, count: pl.ds(pl.multiple_of(r * EARLY_ROWS + offset, flat), count)
            out[rows_at(0, tall), :] = return_sums[pl.ds(pl.multiple_of(chunk * tall, tall), tall), :]
            for c in range(hidden // width):
                out[rows_at(tall + c * flat, flat), :] = hidden_sums[
                    pl.ds(pl.multiple_of(chunk * flat, flat), flat), c * width : (c + 1) * width
                ]
        return carry

    lax.fori_loop(0, CHUNKS // 2, pack, 0)


def hidden_layer(chunk, inputs, cotangent, blended, blend_weight, gain, hidden_weight, return_weight):
    rows, width = inputs.shape
    hidden = hidden_weight.shape[1]
    half = ((CHUNKS // 2 * EARLY_ROWS, width), BF16)
    return whole_call(
        hidden_kernel,
        "hidden_layer",
        chunk,
        inputs,
        cotangent,
        blended,
        blend_weight,
        gain,
        hidden_weight,
        return_weight,
        outs=[((rows, width), F32), ((rows, hidden), BF16), ((rows, hidden), BF16), half, half],
        scratch=[
            pltpu.VMEM((rows, width), BF16),
            pltpu.VMEM((hidden, width), BF16),
            pltpu.VMEM((width, hidden), BF16),
        ],
        cost=20,
        spare=12,
        resident=(0, 1, 2),
        streamed=(1, 6, 2, 7),
    )


def resid_kernel(
    wait, resid_ref, cotangent_ref, blended_ref, active, hidden_grad, blend_weight_ref, gain_ref, hidden_weight_ref, return_weight_ref,
    outputs_ref, resid_grad_ref, blended_grad_ref, gain_grad_ref, blend_sums_ref,
    resid_grad_b,
):
    rows, width = resid_ref.shape
    block = 2 * block_rows(rows) if rows % 512 == 0 else block_rows(rows)
    gain = gain_ref[0:1, :]
    wait(7)

    def row_block(k, gain_grad):
        here = pl.ds(pl.multiple_of(k * block, block), block)
        resid = resid_ref[here, :]
        unit, scale = rms_unit(resid)
        grad = dot_back(hidden_grad[here, :], hidden_weight_ref[...])

        @pl.when(k == 0)
        def weights():
            wait(8)
            wait(1)

        outputs_ref[here, :] = (resid + dot(active[here, :], return_weight_ref[...])).astype(BF16)
        total = cotangent_ref[here, :].astype(F32) + rms_back(unit, scale, grad * gain)
        resid_grad_ref[here, :] = total
        resid_grad_b[here, :] = total.astype(BF16)
        blended_grad_ref[here, :] = dot_back(total.astype(BF16), blend_weight_ref[...]).astype(BF16)
        return gain_grad + jnp.sum(grad * unit, axis=0, keepdims=True)

    gain_grad = lax.fori_loop(0, rows // block, row_block, jnp.zeros((1, width), F32))
    gain_grad_ref[...] = jnp.broadcast_to(gain_grad, gain_grad_ref.shape)
    blend_sums_ref[...] = rows_dot(blended_ref[...], resid_grad_b[...]).astype(BF16)


def resid_layer(resid, cotangent, blended, active, hidden_grad, blend_weight, gain, hidden_weight, return_weight, after=()):
    rows, width = resid.shape
    return whole_call(
        resid_kernel,
        "resid_layer",
        resid,
        cotangent,
        blended,
        active,
        hidden_grad,
        blend_weight,
        gain,
        hidden_weight,
        return_weight,
        outs=[
            ((rows, width), BF16),
            ((rows, width), F32),
            ((rows, WIDE), BF16),
            ((8, width), F32),
            ((WIDE, width), BF16),
        ],
        scratch=[pltpu.VMEM((rows, width), BF16)],
        after=after,
        cost=8,
        spare=6,
        streamed=(7, 8, 1),
        inside=(0, 3, 4),
        resident=(2,),
    )


def unpack_early_kernel(chunk_ref, own_ref, other_ref, return_ref, hidden_ref, token_ref):
    token_ref[...] = jnp.zeros_like(token_ref)
    width = return_ref.shape[1]
    tall, flat = return_ref.shape[0] // CHUNKS, hidden_ref.shape[0] // CHUNKS
    for r in range(CHUNKS):
        chunk = chunk_ref[0] ^ r
        source = own_ref if r < CHUNKS // 2 else other_ref
        at = (r % (CHUNKS // 2)) * EARLY_ROWS
        return_ref[pl.ds(pl.multiple_of(chunk * tall, tall), tall), :] = source[at : at + tall, :].astype(F32)
        at += tall
        there = pl.ds(pl.multiple_of(chunk * flat, flat), flat)
        for c in range(hidden_ref.shape[1] // width):
            hidden_ref[there, c * width : (c + 1) * width] = source[at : at + flat, :].astype(F32)
            at += flat


def unpack_early(chunk, own, other, return_shape, hidden_shape, after=()):
    outs = [(return_shape, F32), (hidden_shape, F32), TOKEN]
    return whole_call(unpack_early_kernel, "unpack_early", chunk, own, other, outs=outs, after=after)


def late_kernel(
    chunk_ref, far_ref, halo_ref, normed_ref, ask_ref, memory_ref, first_ref, second_ref, blend_ref, own_ref, send_ref, ask_sums, memory_sums
):
    width = normed_ref.shape[1]
    flat = width // CHUNKS
    ask_sums[...] = rows_dot(normed_ref[...], ask_ref[...]).astype(BF16)
    total, at = None, 0
    for ref in (far_ref, halo_ref, normed_ref):
        term = rows_dot(ref[...], memory_ref[at : at + ref.shape[0], :])
        total, at = term if total is None else total + term, at + ref.shape[0]
    memory_sums[...] = total.astype(BF16)
    lane = lax.broadcasted_iota(jnp.int32, (width, LANES), 1)
    small = jnp.zeros((width, LANES), F32)
    for h in range(H):
        at = h * LANES + HD
        small = jnp.where(lane == h, HD * ask_sums[:, at : at + 1].astype(F32), small)
    zeros = jnp.zeros((EXTRA_ROWS - H - 2, width), F32)
    extra = jnp.concatenate([small.T[:H, :], first_ref[0:1, :], second_ref[0:1, :], zeros], axis=0).astype(BF16)
    for out in (own_ref, send_ref):
        out[CHUNKS // 2 * LATE_ROWS :, :] = extra
    for r in range(CHUNKS):
        chunk = chunk_ref[0] ^ r
        out = own_ref if r < CHUNKS // 2 else send_ref
        at = (r % (CHUNKS // 2)) * LATE_ROWS
        here = pl.ds(pl.multiple_of(chunk * flat, flat), flat)
        for pair in range(H // 2):
            lanes = slice(pair * LANES, (pair + 1) * LANES)
            even = slice(2 * pair * LANES, 2 * pair * LANES + HD)
            odd = slice((2 * pair + 1) * LANES, (2 * pair + 1) * LANES + HD)
            out[at : at + flat, lanes] = jnp.concatenate([ask_sums[here, even], ask_sums[here, odd]], axis=1)
        out[at + flat : at + 2 * flat, :] = memory_sums[here, :width]
        out[at + 2 * flat : at + 3 * flat, :] = memory_sums[here, width:]
        row = (chunk // (HD // flat)) * LANES + HD + (chunk % (HD // flat)) * flat
        out[at + 3 * flat : at + 4 * flat, :] = blend_ref[pl.ds(pl.multiple_of(row, flat), flat), :]


def unpack_late_kernel(
    chunk_ref, own_ref, other_ref, extra_ref, query_ref, key_ref, value_ref, output_ref, gate_ref, first_ref, second_ref
):
    width = query_ref.shape[1]
    flat = width // CHUNKS
    for r in range(CHUNKS):
        chunk = chunk_ref[0] ^ r
        source = own_ref if r < CHUNKS // 2 else other_ref
        at = (r % (CHUNKS // 2)) * LATE_ROWS
        there = pl.ds(pl.multiple_of(chunk * flat, flat), flat)
        query_ref[there, :] = source[at : at + flat, :].astype(F32)
        for half in range(2):
            at += flat
            for pair in range(H // 4):
                lanes = slice((half * H // 4 + pair) * LANES, (half * H // 4 + pair + 1) * LANES)
                even = source[at : at + flat, 2 * pair * LANES : (2 * pair + 1) * LANES]
                odd = source[at : at + flat, (2 * pair + 1) * LANES : (2 * pair + 2) * LANES]
                key_ref[there, lanes] = jnp.concatenate([even[:, :HD], odd[:, :HD]], axis=1).astype(F32)
                value_ref[there, lanes] = jnp.concatenate([even[:, HD:], odd[:, HD:]], axis=1).astype(F32)
        at += flat
        output_ref[there, :] = source[at : at + flat, :].astype(F32)
    extra = extra_ref[...].astype(F32)
    gate_ref[...] = extra[:H, :]
    first_ref[...] = extra[H : H + 1, :]
    second_ref[...] = extra[H + 1 : H + 2, :]


def pack_late(chunk, far, halo, normed, ask_grad, memory_grad, first_grad, second_grad, blend_grad, after=()):
    width = normed.shape[1]
    half = ((CHUNKS // 2 * LATE_ROWS + EXTRA_ROWS, width), BF16)
    return whole_call(
        late_kernel,
        "late_weight_grads",
        chunk,
        far,
        halo,
        normed,
        ask_grad,
        memory_grad,
        first_grad,
        second_grad,
        blend_grad,
        outs=[half, half],
        scratch=[pltpu.VMEM((width, WIDE), BF16), pltpu.VMEM((width, WIDE), BF16)],
        after=after,
    )


def unpack_late(chunk, own, other, extra):
    width = own.shape[1]
    square, row = ((width, width), F32), ((1, width), F32)
    return whole_call(
        unpack_late_kernel,
        "unpack_late",
        chunk,
        own,
        other,
        extra,
        outs=[square] * 4 + [((H, width), F32), row, row],
    )


def normed_back_kernel(
    wait, inputs_ref, far_ref, halo_ref, ask_ref, memory_ref, ask_weight_ref, memory_weight_ref, own_grad_ref, others_grad_ref, gain_ref
):
    rows, width = inputs_ref.shape
    length = memory_ref.shape[0]
    block = block_rows(rows)

    def unit(ref, here):
        values = ref[here, :].astype(F32)
        return values * lax.rsqrt(jnp.mean(values * values, axis=-1, keepdims=True) + EPS)

    gain = jnp.zeros((1, width), F32)
    wait(4)
    for at in range(0, length - rows, block):
        here = slice(at, at + block)
        grad = dot_back(memory_ref[here, :], memory_weight_ref[...])
        others_grad_ref[here, :] = grad.astype(BF16)
        past = far_ref.shape[0]
        values = unit(far_ref, here) if at < past else unit(halo_ref, slice(at - past, at - past + block))
        gain = gain + jnp.sum(grad * values, axis=0, keepdims=True)
    wait(3)
    for at in range(0, rows, block):
        here = slice(at, at + block)
        there = slice(length - rows + at, length - rows + at + block)
        grad = dot_back(ask_ref[here, :], ask_weight_ref[...]) + dot_back(memory_ref[there, :], memory_weight_ref[...])
        own_grad_ref[here, :] = grad
        gain = gain + jnp.sum(grad * unit(inputs_ref, here), axis=0, keepdims=True)
    gain_ref[...] = jnp.broadcast_to(gain, gain_ref.shape)


def normed_back(inputs, far, halo, ask_grad, memory_grad, ask_weight, memory_weight, after=()):
    rows, width = inputs.shape
    return whole_call(
        normed_back_kernel,
        "normed_back",
        inputs,
        far,
        halo,
        ask_grad,
        memory_grad,
        ask_weight,
        memory_weight,
        outs=[((rows, width), F32), ((far.shape[0] + halo.shape[0], width), BF16), ((8, width), F32)],
        streamed=(4, 3),
        after=after,
    )


def input_back_kernel(inputs_ref, gain_ref, resid_grad_ref, own_ref, *refs):
    arrived, out_ref, token_ref = refs[:-2], refs[-2], refs[-1]
    token_ref[...] = jnp.zeros_like(token_ref)
    values = inputs_ref[...].astype(F32)
    grad = own_ref[...]
    for ref in arrived:
        grad = grad + ref[...].astype(F32)
    grad = grad * gain_ref[0:1, :]
    scale = lax.rsqrt(jnp.mean(values * values, axis=-1, keepdims=True) + EPS)
    unit = values * scale
    part = scale * (grad - unit * jnp.mean(grad * unit, axis=-1, keepdims=True))
    out_ref[...] = (resid_grad_ref[...] + part).astype(BF16)


def body(
    inputs,
    cotangent,
    neighbours,
    empty_rows,
    first_gain,
    query_weight,
    key_weight,
    value_weight,
    gate_weight,
    output_weight,
    second_gain,
    hidden_weight,
    return_weight,
):
    rows, width = inputs.shape[1:]
    n_seq = lax.axis_size("seq")
    length = rows * n_seq
    base = lax.axis_index("seq") * rows
    base_ref = jnp.reshape(base, (1,)).astype(jnp.int32)
    inputs = inputs.reshape(rows, width)
    cotangent = cotangent.reshape(rows, width)
    if n_seq == 2 and rows > SPAN:
        halo_inputs, far_inputs = turned(inputs[rows - SPAN :], 1), turned(inputs[: rows - SPAN], 1)
    else:
        others = jnp.concatenate([turned(inputs, shift) for shift in range(1, n_seq)], axis=0)
        halo_inputs, far_inputs = others[length - rows - SPAN :], others[: length - rows - SPAN]
    gain_rows = lambda gain: jnp.broadcast_to(gain, (8, width))
    ask_weight, memory_weight, blend_weight = lay_weights(
        query_weight, key_weight, value_weight, gate_weight, output_weight
    )
    chunk = own_chunk()
    index = (neighbours.reshape(rows * NEAR) + (length - rows - base)) % length

    normed, ask, own = project(inputs, gain_rows(first_gain), empty_rows.reshape(1, rows), ask_weight, memory_weight)
    split = SPAN if rows == 2 * SPAN else rows
    attended = ()
    if split < rows:
        attended = local_attention(base_ref, ask, own, own, split, rows)
    halo_normed, halo = project_memory(halo_inputs, gain_rows(first_gain), memory_weight)
    local_out, log_total = local_attention(base_ref, ask, halo, own, 0, split, attended)
    far_normed, far_memory = project_memory(far_inputs, gain_rows(first_gain), memory_weight)
    near, weight, blended = retrieve(index, far_memory, halo, own, ask, local_out)

    resid, active, hidden_grad, early_own, early_send = hidden_layer(
        chunk, inputs, cotangent, blended, blend_weight, gain_rows(second_gain), hidden_weight, return_weight
    )
    early = scatter_start(early_own, early_send)
    outputs, resid_grad, blended_grad, second_gain_grad, blend_grad = resid_layer(
        resid, cotangent, blended, active, hidden_grad, blend_weight, gain_rows(second_gain), hidden_weight, return_weight
    )
    early = scatter_level(early, 1, after=[second_gain_grad])
    local_grad, inner, partial, far = retrieve_back(
        index, blended_grad, ask, local_out, near, weight, length, after=[early[0]]
    )
    early = scatter_level(early, 2, after_far=[inner])
    steps = list(range(H // BACK_HEADS))
    first, second = len(steps) * 3 // 8, len(steps) * 5 // 8
    back = functools.partial(
        local_attention_back, base_ref, ask, halo, own, local_grad, log_total, inner, partial, far
    )
    grads = back(steps[:first], after=[early[0]])
    early_total = scatter_finish(early, after_far=[grads[0]])
    early = gather_level(early_total, 2)
    grads = back(steps[first:second], grads, after=[early_total])
    early_total = join_pieces(early, after_far=[grads[0]])
    early = gather_level(early_total, 1)
    ask_grad, memory_grad = back(steps[second:], grads, after=[early_total])
    own_grad, others_grad, first_gain_grad = normed_back(
        inputs, far_inputs, halo_inputs, ask_grad, memory_grad, ask_weight, memory_weight
    )
    arrived = [turned(others_grad[(k - 1) * rows : k * rows], n_seq - k) for k in range(1, n_seq)]
    own_late, send_late = pack_late(
        chunk, far_normed, halo_normed, normed, ask_grad, memory_grad, first_gain_grad, second_gain_grad, blend_grad,
        after=[],
    )
    late = scatter_start(own_late, send_late)
    early_own = join_pieces(early, after=[own_late])
    early_other = swapped(early_own, level_groups()[0][0], 1)
    late = scatter_level(late, 1, EXTRA_ROWS, after=[early_own])
    return_sum, hidden_sum, token = unpack_early(
        chunk, early_own, early_other, return_weight.shape, hidden_weight.shape, after=[late[0]]
    )
    late = scatter_level(late, 2, EXTRA_ROWS, after=[token])
    input_grad, token = whole_call(
        input_back_kernel, "input_back", inputs, gain_rows(first_gain), resid_grad, own_grad, *arrived,
        outs=[((rows, width), BF16), TOKEN], after=[late[0]],
    )
    late_total = scatter_finish(late, after=[token])
    extra = late_total[LATE_ROWS:]
    late_total = late_total[:LATE_ROWS]
    late = gather_level(late_total, 2)
    late_total = join_pieces(late)
    late = gather_level(late_total, 1)
    late_own = join_pieces(late)
    late_other = swapped(late_own, level_groups()[0][0], 1)
    query_sum, key_sum, value_sum, output_sum, gate_sum, first_sum, second_sum = unpack_late(chunk, late_own, late_other, extra)
    return (
        outputs.reshape(1, rows, width),
        input_grad.reshape(1, rows, width),
        first_sum.reshape(width),
        query_sum,
        key_sum,
        value_sum,
        gate_sum.T,
        output_sum,
        second_sum.reshape(width),
        hidden_sum,
        return_sum,
    )


def solution(mesh):
    split = P("dp", "seq", None)
    in_specs = (split, split, split, P("dp", "seq")) + (P(),) * 9
    out_specs = (split, split) + (P(),) * 9
    return jax.shard_map(body, mesh=mesh, in_specs=in_specs, out_specs=out_specs, check_vma=False)
```
